128 devices in a mesh: dp: 128 (over z, y, x, core).
Axes of the slice: x: 4, y: 4, z: 4, core: 2. Of those that a mesh axis runs over, the one named last changes fastest.
Arguments:
- embeddings: bfloat16 [131072, 1024], P('dp')
- partners: int32 [128, 13], P('dp'), may hold values from 0 to 127, as said below
- pair_count: int32 [128], P('dp'), may hold values from 1 to 13, as said below
Outputs:
- soft_cosine: float32 [131072], P('dp')
The draws below stay inside these ranges and needn't reach their ends.
Inputs may be any that keep to these rules, and one draw needn't show every extreme that they name: Entry 0 of partners[h] is h; the live entries of partners[h] are distinct blocks from h to min(h + 16, 127), so each unordered pair of blocks stands once; entries past pair_count[h] are arbitrary blocks in that range and are not pairs. `pair_count`: at most 13 live pairs for one block; some block has exactly 13.
All inputs are finite; a program needn't handle non-finite values.
Results may differ from the reference program's by a relative error of at most 0.00043.
Values may be sent and summed in bfloat16 or wider, within the bound.
No kernel may reach another device: no remote copies, remote signals or barrier semaphores. Data moves between devices by JAX's collectives and lax.ppermute only.
A program may use at most 128 MiB of HBM per device.

```python
import math
import jax
import jax.numpy as jnp
from jax import lax

D = 1024
B = 1024
WIN = 16
MOSTP = 12
SLOTS = 13
N_DP = 128


def plan(key):
    key_a, key_b, key_c, key_d, key_e = jax.random.split(key, 5)
    block = jnp.arange(N_DP, dtype=jnp.int32)
    many = jax.random.randint(key_a, (N_DP,), 0, 4) * jax.random.randint(key_b, (N_DP,), 0, 5)
    star = jax.random.randint(key_c, (), 0, N_DP - WIN)
    many = jnp.where(block == star, MOSTP, many).astype(jnp.int32)
    ranks = jax.random.randint(key_d, (N_DP, WIN), 0, 4096) * WIN + jnp.arange(WIN, dtype=jnp.int32)[None, :]
    offsets = jnp.argsort(ranks, axis=1)[:, :MOSTP].astype(jnp.int32) + 1
    target = block[:, None] + offsets
    keep = (jnp.arange(MOSTP, dtype=jnp.int32)[None, :] < many[:, None]) & (target < N_DP)
    order = jnp.argsort(1 - keep.astype(jnp.int32), axis=1, stable=True)
    packed = jnp.take_along_axis(target, order, 1)
    kept = jnp.take_along_axis(keep, order, 1)
    count = (1 + jnp.sum(keep.astype(jnp.int32), 1)).astype(jnp.int32)
    filler = jnp.minimum(block[:, None] + jax.random.randint(key_e, (N_DP, MOSTP), 0, WIN + 1), N_DP - 1)
    tail = jnp.where(kept, packed, filler).astype(jnp.int32)
    return (jnp.concatenate([block[:, None], tail], 1), count)


def draw_partners(key, part):
    return plan(key)[0]


def draw_pair_count(key, part):
    return plan(key)[1]


def draw_embeddings(key, part):
    partner_list, count = plan(key)
    block = jnp.arange(N_DP, dtype=jnp.int32)
    mate = jnp.where(count > 1, partner_list[:, 1], block)
    key = jax.random.fold_in(key, 7)
    key_a = jax.random.fold_in(key, 0)
    key_c = jax.random.fold_in(key, 2)
    key_d = jax.random.fold_in(key, 3)
    key_e = jax.random.fold_in(key, 4)
    key_f = jax.random.fold_in(key, 5)
    group = B // 8
    base = jax.random.normal(key_a, (N_DP, B, D), jnp.float32)
    spread = math.log(10.0)
    source = base[:, :group]
    mates = jnp.take(source, mate, axis=0)
    near = mates + 0.07 * jax.random.normal(key_c, mates.shape, jnp.float32)
    farther = mates + 0.12 * jax.random.normal(key_d, mates.shape, jnp.float32)
    whole = jnp.concatenate([source, near, farther, base[:, 3 * group:]], 1)
    shuffle = jax.vmap(lambda one: jax.random.permutation(one, B))(jax.random.split(key_e, N_DP))
    whole = jnp.take_along_axis(whole, shuffle[:, :, None], 1)
    scale = jnp.exp(jax.random.uniform(key_f, (N_DP, B, 1), jnp.float32, 0.0, spread))
    return (whole * scale).reshape(N_DP * B, D).astype(jnp.bfloat16)


def setup_inputs(seed: int = 0) -> dict:
    splits = jax.random.split(jax.random.key(seed), 4)
    return {
        "embeddings": draw_embeddings(jax.random.fold_in(splits[3], 71), 0),
        "partners": draw_partners(jax.random.fold_in(splits[3], 71), 0),
        "pair_count": draw_pair_count(jax.random.fold_in(splits[3], 71), 0),
    }


SCALE = 256.0
FLOOR = -1e+30

def normalize(embeddings):
    values = embeddings.astype(jnp.float32)
    return (values * lax.rsqrt(lax.optimization_barrier(jnp.sum(values * values, -1, keepdims=True)) + 1e-06)).astype(jnp.bfloat16)

def merge(first_m, first_s, second_m, second_s):
    top = jnp.maximum(first_m, second_m)
    return (top, first_s * jnp.exp(first_m - top) + second_s * jnp.exp(second_m - top))

def reference(embeddings, partners, pair_count):
    unit = normalize(embeddings).reshape(N_DP, B, D)
    owner = jnp.repeat(jnp.arange(N_DP, dtype=jnp.int32), SLOTS)
    target = partners.reshape(-1).astype(jnp.int32)
    live = jnp.arange(N_DP * SLOTS, dtype=jnp.int32) % SLOTS < pair_count[owner]
    eye = jnp.arange(B)[:, None] == jnp.arange(B)[None, :]
    start = (jnp.full((N_DP, B), FLOOR, jnp.float32), jnp.zeros((N_DP, B), jnp.float32))

    def visit(carry, item):
        row_block, col_block, present = item

        def work(state):
            best, total = state
            left = lax.dynamic_index_in_dim(unit, row_block, 0, keepdims=False)
            right = lax.dynamic_index_in_dim(unit, col_block, 0, keepdims=False)
            scores = lax.dot_general(left, right, (((1,), (1,)), ((), ())), preferred_element_type=jnp.float32) * SCALE
            same = row_block == col_block
            scores = jnp.where(eye & same, FLOOR, scores)
            row_m = lax.optimization_barrier(jnp.max(scores, 1))
            row_s = lax.optimization_barrier(jnp.sum(jnp.exp(scores - row_m[:, None]), 1))
            col_m = lax.optimization_barrier(jnp.max(scores, 0))
            col_s = lax.optimization_barrier(jnp.sum(jnp.exp(scores - col_m[None, :]), 0))
            col_m = jnp.where(same, FLOOR, col_m)
            col_s = jnp.where(same, 0.0, col_s)
            new_m, new_s = merge(best[row_block], total[row_block], row_m, row_s)
            best = best.at[row_block].set(new_m)
            total = total.at[row_block].set(new_s)
            new_m, new_s = merge(best[col_block], total[col_block], col_m, col_s)
            best = best.at[col_block].set(new_m)
            total = total.at[col_block].set(new_s)
            return (best, total)
        return (lax.cond(present, work, lambda state: state, carry), None)
    (best, total), _ = lax.scan(visit, start, (owner, target, live))
    return ((best + jnp.log(total)) / SCALE).reshape(N_DP * B)
```

```python
import functools

import jax
import jax.numpy as jnp
from jax import lax
from jax.experimental import pallas as pl
from jax.experimental.pallas import tpu as pltpu
from jax.sharding import PartitionSpec as P

SCALE = 256.0
LOG2E = 1.4426950408889634
LN2 = 0.6931471805599453
GAIN = SCALE * LOG2E
PLAIN = 78.0 / SCALE
FLOOR = -1e30
MASKED = -1e27
B = 1024
D = 1024
CH = 256
G = 32
COUNT = 128
RING = 8


def around(dx):
    moves = []
    for d in range(COUNT):
        core, x, rest = d % 2, (d // 2) % 4, d // RING
        moves.append((d, rest * RING + ((x + dx) % 4) * 2 + core))
    return moves


def along(steps, flip=0):
    return [(d, (d + steps) ^ flip) for d in range(COUNT) if 0 <= d + steps < COUNT]


def send(value, moves):
    return lax.ppermute(value, "dp", moves)


def unit_kernel(x_ref, o_ref):
    for g in range(x_ref.shape[0] // G):
        v = x_ref[g * G : (g + 1) * G, :].astype(jnp.float32)
        size = jnp.sum(v * v, -1, keepdims=True)
        o_ref[g * G : (g + 1) * G, :] = (v * lax.rsqrt(size + 1e-06)).astype(jnp.bfloat16)


def normalize(embeddings):
    return pl.pallas_call(
        unit_kernel,
        grid=(B // CH,),
        in_specs=[pl.BlockSpec((CH, D), lambda i: (i, 0))],
        out_specs=pl.BlockSpec((CH, D), lambda i: (i, 0)),
        out_shape=jax.ShapeDtypeStruct((B, D), jnp.bfloat16),
        name="unit_rows",
    )(embeddings)


def lanes(value, op):
    return functools.reduce(op, [value[:, q * 128 : (q + 1) * 128] for q in range(value.shape[1] // 128)])


def rows8(value, op):
    return functools.reduce(op, [value[q * 8 : (q + 1) * 8, :] for q in range(value.shape[0] // 8)])


def fold(m, s, f, axis):
    top = jnp.max(m, axis, keepdims=True)
    plain = jnp.sum(f, axis, keepdims=True)
    top = jnp.maximum(top, jnp.where(plain > 0.0, 0.0, FLOOR))
    total = jnp.sum(s * jnp.exp2(m - top), axis, keepdims=True)
    total = total + plain * jnp.exp2(jnp.minimum(-top, 0.0))
    return jnp.maximum(top + jnp.log2(total), FLOOR)


def log2_add(a, b):
    top = jnp.maximum(a, b)
    return top + jnp.log2(jnp.exp2(a - top) + jnp.exp2(b - top))


def stage_kernel(plan, live, prev, *refs):
    nl, nr, lefts, rights, own_first = plan
    blocks, refs = refs[: len(lefts) + len(rights)], refs[len(lefts) + len(rights) :]
    row_out, col_out = refs[:2]
    (lbuf, rbuf, sc, row_t, col_t, chk, row_f, row_m, row_s, col_f, col_m, col_s, waited, lsem, rsem) = refs[2:]

    def copies(side, slot):
        pieces = lefts if side == 0 else rights
        base = 0 if side == 0 else len(lefts)
        buf, sem = (lbuf, lsem) if side == 0 else (rbuf, rsem)
        made = []
        for i, (s, row, count) in enumerate(pieces):
            if s == slot:
                made.append(
                    pltpu.make_async_copy(blocks[base + i], buf.at[slot, row : row + count, :], sem.at[slot])
                )
        return made

    def used(flags):
        return functools.reduce(jnp.logical_or, [f > 0 for f in flags])

    need_l = [used([live[q * nr + r] for r in range(nr)]) for q in range(nl)]
    need_r = [used([live[q * nr + r] for q in range(nl)]) for r in range(nr)]
    for q in range(nl):

        @pl.when(need_l[q])
        def _(q=q):
            for c in copies(0, q):
                c.start()

    for r in range(nr):
        waited[r] = 0

        @pl.when(need_r[r])
        def _(r=r):
            for c in copies(1, r):
                c.start()

    col_f[...] = jnp.zeros_like(col_f)
    col_s[...] = jnp.zeros_like(col_s)
    col_m[...] = jnp.full_like(col_m, FLOOR)

    def pair(q, r, diag):
        def dot(i):
            sc[i * CH : (i + 1) * CH, :] = lax.dot_general(
                lbuf[q, i * CH : (i + 1) * CH, :],
                rbuf[r],
                (((1,), (1,)), ((), ())),
                preferred_element_type=jnp.float32,
            )

        def sums(i):
            cols = jnp.zeros((8, B), jnp.float32)
            size = jnp.zeros((8, 128), jnp.float32)
            for g in range(CH // G):
                at = i * CH + g * G
                v = sc[at : at + G, :]
                if diag:
                    r_at = lax.broadcasted_iota(jnp.int32, (G, B), 0) + at
                    c_at = lax.broadcasted_iota(jnp.int32, (G, B), 1)
                    eye = r_at == c_at
                    absv = jnp.where(eye, 0.0, jnp.abs(v))
                    v = jnp.where(eye, MASKED, v)
                    sc[at : at + G, :] = v
                else:
                    absv = jnp.abs(v)
                e = jnp.exp2(v * GAIN)
                row_t[at : at + G, :] = lanes(e, jnp.add)
                if not diag:
                    cols = cols + rows8(e, jnp.add)
                size = jnp.maximum(size, rows8(lanes(absv, jnp.maximum), jnp.maximum))
            if not diag:
                col_t[...] = cols if i == 0 else col_t[...] + cols
            chk[...] = size if i == 0 else jnp.maximum(chk[...], size)

        n = B // CH
        dot(0)
        for i in range(n):
            if i + 1 < n:
                dot(i + 1)
            sums(i)
        plain = jnp.max(chk[...]) <= PLAIN

        @pl.when(plain)
        def _():
            row_f[...] += row_t[...]
            if not diag:
                col_f[r] += col_t[...]

        @pl.when(jnp.logical_not(plain))
        def _():
            def group(g, _):
                at = pl.multiple_of(g * G, G)
                w = sc[pl.ds(at, G), :] * GAIN
                old = row_m[pl.ds(at, G), :]
                top = jnp.maximum(old, lanes(w, jnp.maximum))
                total = row_s[pl.ds(at, G), :] * jnp.exp2(old - top)
                for k in range(B // 128):
                    total = total + jnp.exp2(w[:, k * 128 : (k + 1) * 128] - top)
                row_m[pl.ds(at, G), :] = top
                row_s[pl.ds(at, G), :] = total
                if not diag:
                    old = col_m[r]
                    top = jnp.maximum(old, rows8(w, jnp.maximum))
                    total = col_s[r] * jnp.exp2(old - top)
                    for k in range(G // 8):
                        total = total + jnp.exp2(w[k * 8 : (k + 1) * 8, :] - top)
                    col_m[r] = top
                    col_s[r] = total
                return 0

            lax.fori_loop(0, B // G, group, 0)

    def arrive(r):
        @pl.when(waited[r] == 0)
        def _():
            for s in range(nr):

                @pl.when(r == s)
                def _(s=s):
                    for c in copies(1, s):
                        c.wait()

            waited[r] = 1

    for q in range(nl):
        row_f[...] = jnp.zeros_like(row_f)
        row_s[...] = jnp.zeros_like(row_s)
        row_m[...] = jnp.full_like(row_m, FLOOR)

        @pl.when(need_l[q])
        def _(q=q):
            for c in copies(0, q):
                c.wait()

        first = 0
        if own_first and q == 0:
            arrive(0)
            pair(0, 0, True)
            first = 1

        def step(r, _, q=q):
            @pl.when(live[q * nr + r] > 0)
            def _():
                arrive(r)
                pair(q, r, False)

            return 0

        lax.fori_loop(first, nr, step, 0)
        row_out[q : q + 1, :] = fold(row_m[...].T, row_s[...].T, row_f[...].T, 0)
    for r in range(nr):
        col_out[r : r + 1, :] = log2_add(fold(col_m[r], col_s[r], col_f[r], 0), prev[r : r + 1, :])


def stage(name, live, prev, lefts, rights, own_first=False):
    nl, nr = len(lefts), len(rights)
    flat, tables = [], []
    for side in (lefts, rights):
        table = []
        for slot, pieces in enumerate(side):
            for array, row in pieces:
                flat.append(array)
                table.append((slot, row, array.shape[0]))
        tables.append(tuple(table))
    plan = (nl, nr, tables[0], tables[1], own_first)
    f32 = jnp.float32
    return pl.pallas_call(
        functools.partial(stage_kernel, plan),
        out_shape=[jax.ShapeDtypeStruct((nl, B), f32), jax.ShapeDtypeStruct((nr, B), f32)],
        in_specs=[pl.BlockSpec(memory_space=pltpu.SMEM), pl.BlockSpec(memory_space=pltpu.VMEM)]
        + [pl.BlockSpec(memory_space=pl.ANY)] * len(flat),
        out_specs=[pl.BlockSpec(memory_space=pltpu.VMEM)] * 2,
        scratch_shapes=[
            pltpu.VMEM((nl, B, D), jnp.bfloat16),
            pltpu.VMEM((nr, B, D), jnp.bfloat16),
            pltpu.VMEM((B, B), f32),
            pltpu.VMEM((B, 128), f32),
            pltpu.VMEM((8, B), f32),
            pltpu.VMEM((8, 128), f32),
            pltpu.VMEM((B, 128), f32),
            pltpu.VMEM((B, 128), f32),
            pltpu.VMEM((B, 128), f32),
            pltpu.VMEM((nr, 8, B), f32),
            pltpu.VMEM((nr, 8, B), f32),
            pltpu.VMEM((nr, 8, B), f32),
            pltpu.SMEM((nr,), jnp.int32),
            pltpu.SemaphoreType.DMA((nl,)),
            pltpu.SemaphoreType.DMA((nr,)),
        ],
        compiler_params=pltpu.CompilerParams(vmem_limit_bytes=40 * 2**20),
        cost_estimate=pl.CostEstimate(
            flops=2 * B * B * D * max(1, nl * nr // 4), bytes_accessed=2 * B * D * (nl + nr), transcendentals=0
        ),
        name=name,
    )(live, prev, *flat)


def body(embeddings, partners, pair_count):
    unit = normalize(embeddings)
    me = lax.axis_index("dp")
    column = me % RING
    ring = me - column
    chip, core = column // 2, column % 2

    slots = partners[0]
    meta = jnp.where(jnp.arange(slots.shape[0]) < pair_count[0], slots, -1)[None, :]
    half = B // 2
    top, low = unit[:half], unit[half:]

    meta_a, meta_b = send(meta, around(1)), send(meta, around(-1))
    meta_c = send(meta, around(2))
    a_top = send(top, around(1))
    b_low = send(low, around(-1))
    sib = send(unit, along(0, 1))
    c_own = send(unit, along(-RING))
    a_low = send(low, around(1))
    b_top = send(top, around(-1))
    d_top = send(top, along(-2 * RING))
    over = []
    for d in range(COUNT):
        y = (d // RING) % 4
        over.append((d, d - y * RING + ((y + 1) % 4) * RING))
    relay = dict(over)
    d_mid = send(low, over)
    d_low = send(d_mid, [(relay[d], d - 2 * RING) for d in range(2 * RING, COUNT)])
    f_top = send(a_top, around(1))
    f_low = send(b_low, around(-1))
    c_sib = send(c_own, along(0, 1))
    d_own = jnp.concatenate([d_top, d_low], 0)
    d_sib = send(d_own, along(0, 1))

    other = 1 - core
    targets = [
        ring + chip * 2 + core,
        ring + chip * 2 + other,
        ring + RING + chip * 2 + core,
        ring + RING + chip * 2 + other,
        ring + 2 * RING + chip * 2 + core,
        ring + 2 * RING + chip * 2 + other,
    ]
    targets = jnp.stack(targets).astype(jnp.int32)
    lists = jnp.concatenate([meta, meta_a, meta_b, meta_c], 0)
    live = jnp.any(lists[:, None, :] == targets[None, :, None], -1).astype(jnp.int32)

    blocks = [[(unit, 0)], [(sib, 0)], [(c_own, 0)], [(c_sib, 0)], [(d_own, 0)], [(d_sib, 0)]]
    none = jnp.full((6, B), FLOOR, jnp.float32)
    row_0, col_0 = stage("own_ring", live[0, :2], none[:2], [blocks[0]], blocks[:2], own_first=True)
    left_a = [(a_top, 0), (a_low, half)]
    left_b = [(b_top, 0), (b_low, half)]
    left_c = [(f_top, 0), (f_low, half)]
    prev = jnp.concatenate([col_0, none[:4]], 0)
    live_1 = jnp.concatenate([live[:1].at[:, :2].set(0), live[1:3]], 0).reshape(-1)
    row_1, col_1 = stage("near", live_1, prev, [blocks[0], left_a, left_b], blocks)
    row_2, col_2 = stage("far", live[3], col_1, [left_c], blocks)

    got = [row_0[0], row_1[0], col_2[0]]
    got.append(send(row_1[1], around(-1)))
    got.append(send(row_1[2], around(1)))
    got.append(send(row_2[0], around(2)))
    got.append(send(col_2[1], along(0, 1)))
    for k in range(2):
        for flip in range(2):
            moves = along((k + 1) * RING, flip)
            back = send(col_2[2 + 2 * k + flip], moves)
            got.append(jnp.where(me >= (k + 1) * RING, back, FLOOR))
    got = jnp.stack(got)
    best = jnp.max(got, 0)
    return (best + jnp.log2(jnp.sum(jnp.exp2(got - best), 0))) * (LN2 / SCALE)


def solution(mesh):
    placed = (P("dp", None), P("dp", None), P("dp"))
    return jax.shard_map(body, mesh=mesh, in_specs=placed, out_specs=P("dp"), check_vma=False)
```

```python
import functools

import jax
import jax.numpy as jnp
from jax import lax
from jax.experimental import pallas as pl
from jax.experimental.pallas import tpu as pltpu
from jax.sharding import PartitionSpec as P

SCALE = 256.0
LOG2E = 1.4426950408889634
LN2 = 0.6931471805599453
GAIN = SCALE * LOG2E
PLAIN = 78.0 / SCALE
FLOOR = -1e30
MASKED = -1e27
B = 1024
D = 1024
CH = 256
G = 32
COUNT = 128
RING = 8
HALVES = B // 2 // CH


def around(dx):
    moves = []
    for d in range(COUNT):
        core, x, rest = d % 2, (d // 2) % 4, d // RING
        moves.append((d, rest * RING + ((x + dx) % 4) * 2 + core))
    return moves


def along(steps, flip=0):
    return [(d, (d + steps) ^ flip) for d in range(COUNT) if 0 <= d + steps < COUNT]


def send(value, moves):
    return lax.ppermute(value, "dp", moves)


def unit_kernel(x_ref, o_ref, top_ref, low_ref):
    i = pl.program_id(0)
    for g in range(CH // G):
        at = slice(g * G, (g + 1) * G)
        v = x_ref[at, :].astype(jnp.float32)
        size = jnp.sum(v * v, -1, keepdims=True)
        o_ref[at, :] = (v * lax.rsqrt(size + 1e-06)).astype(jnp.bfloat16)

    @pl.when(i < HALVES)
    def _():
        top_ref[...] = o_ref[...]

    @pl.when(i >= HALVES)
    def _():
        low_ref[...] = o_ref[...]


def normalize(embeddings):
    bf16 = jnp.bfloat16
    return pl.pallas_call(
        unit_kernel,
        grid=(B // CH,),
        in_specs=[pl.BlockSpec((CH, D), lambda i: (i, 0))],
        out_specs=[
            pl.BlockSpec((CH, D), lambda i: (i, 0)),
            pl.BlockSpec((CH, D), lambda i: (jnp.minimum(i, HALVES - 1), 0)),
            pl.BlockSpec((CH, D), lambda i: (jnp.maximum(i - HALVES, 0), 0)),
        ],
        out_shape=[
            jax.ShapeDtypeStruct((B, D), bf16),
            jax.ShapeDtypeStruct((B // 2, D), bf16),
            jax.ShapeDtypeStruct((B // 2, D), bf16),
        ],
        name="unit_rows",
    )(embeddings)


def lanes(value, op):
    return functools.reduce(op, [value[:, q * 128 : (q + 1) * 128] for q in range(value.shape[1] // 128)])


def rows8(value, op):
    return functools.reduce(op, [value[q * 8 : (q + 1) * 8, :] for q in range(value.shape[0] // 8)])


def fold(m, s, f, axis):
    top = jnp.max(m, axis, keepdims=True)
    plain = jnp.sum(f, axis, keepdims=True)
    top = jnp.maximum(top, jnp.where(plain > 0.0, 0.0, FLOOR))
    total = jnp.sum(s * jnp.exp2(m - top), axis, keepdims=True)
    total = total + plain * jnp.exp2(jnp.minimum(-top, 0.0))
    return jnp.maximum(top + jnp.log2(total), FLOOR)


def log2_add(a, b):
    top = jnp.maximum(a, b)
    return top + jnp.log2(jnp.exp2(a - top) + jnp.exp2(b - top))


def stage_kernel(plan, live, row_prev, col_prev, *refs):
    nl, nr, lefts, rights, own_first = plan
    blocks, refs = refs[: len(lefts) + len(rights)], refs[len(lefts) + len(rights) :]
    row_out, col_out = refs[:2]
    (lbuf, rbuf, sc, row_t, col_t, chk, row_f, row_m, row_s, col_f, col_m, col_s, waited, lsem, rsem) = refs[2:]

    def copies(side, slot):
        pieces = lefts if side == 0 else rights
        base = 0 if side == 0 else len(lefts)
        buf, sem = (lbuf, lsem) if side == 0 else (rbuf, rsem)
        made = []
        for i, (s, row, count) in enumerate(pieces):
            if s == slot:
                made.append(
                    pltpu.make_async_copy(blocks[base + i], buf.at[slot, row : row + count, :], sem.at[slot])
                )
        return made

    def used(flags):
        return functools.reduce(jnp.logical_or, [f > 0 for f in flags])

    need_l = [used([live[q * nr + r] for r in range(nr)]) for q in range(nl)]
    need_r = [used([live[q * nr + r] for q in range(nl)]) for r in range(nr)]
    for q in range(nl):

        @pl.when(need_l[q])
        def _(q=q):
            for c in copies(0, q):
                c.start()

    for r in range(nr):
        waited[r] = 0

        @pl.when(need_r[r])
        def _(r=r):
            for c in copies(1, r):
                c.start()

    col_f[...] = jnp.zeros_like(col_f)
    col_s[...] = jnp.zeros_like(col_s)
    col_m[...] = jnp.full_like(col_m, FLOOR)

    def pair(q, r, diag):
        def dot(i):
            sc[i * CH : (i + 1) * CH, :] = lax.dot_general(
                lbuf[q, i * CH : (i + 1) * CH, :],
                rbuf[r],
                (((1,), (1,)), ((), ())),
                preferred_element_type=jnp.float32,
            )

        def sums(i):
            cols = jnp.zeros((8, B), jnp.float32)
            size = jnp.zeros((8, 128), jnp.float32)
            for g in range(CH // G):
                at = i * CH + g * G
                v = sc[at : at + G, :]
                if diag:
                    r_at = lax.broadcasted_iota(jnp.int32, (G, B), 0) + at
                    c_at = lax.broadcasted_iota(jnp.int32, (G, B), 1)
                    eye = r_at == c_at
                    absv = jnp.where(eye, 0.0, jnp.abs(v))
                    v = jnp.where(eye, MASKED, v)
                    sc[at : at + G, :] = v
                else:
                    absv = jnp.abs(v)
                e = jnp.exp2(v * GAIN)
                row_t[at : at + G, :] = lanes(e, jnp.add)
                if not diag:
                    cols = cols + rows8(e, jnp.add)
                size = jnp.maximum(size, rows8(lanes(absv, jnp.maximum), jnp.maximum))
            if not diag:
                col_t[...] = cols if i == 0 else col_t[...] + cols
            chk[...] = size if i == 0 else jnp.maximum(chk[...], size)

        n = B // CH
        dot(0)
        for i in range(n):
            if i + 1 < n:
                dot(i + 1)
            sums(i)
        plain = jnp.max(chk[...]) <= PLAIN

        @pl.when(plain)
        def _():
            row_f[...] += row_t[...]
            if not diag:
                col_f[r] += col_t[...]

        @pl.when(jnp.logical_not(plain))
        def _():
            def group(g, _):
                at = pl.multiple_of(g * G, G)
                w = sc[pl.ds(at, G), :] * GAIN
                old = row_m[pl.ds(at, G), :]
                top = jnp.maximum(old, lanes(w, jnp.maximum))
                total = row_s[pl.ds(at, G), :] * jnp.exp2(old - top)
                for k in range(B // 128):
                    total = total + jnp.exp2(w[:, k * 128 : (k + 1) * 128] - top)
                row_m[pl.ds(at, G), :] = top
                row_s[pl.ds(at, G), :] = total
                if not diag:
                    old = col_m[r]
                    top = jnp.maximum(old, rows8(w, jnp.maximum))
                    total = col_s[r] * jnp.exp2(old - top)
                    for k in range(G // 8):
                        total = total + jnp.exp2(w[k * 8 : (k + 1) * 8, :] - top)
                    col_m[r] = top
                    col_s[r] = total
                return 0

            lax.fori_loop(0, B // G, group, 0)

    def arrive(r):
        @pl.when(waited[r] == 0)
        def _():
            for s in range(nr):

                @pl.when(r == s)
                def _(s=s):
                    for c in copies(1, s):
                        c.wait()

            waited[r] = 1

    for q in range(nl):
        row_f[...] = jnp.zeros_like(row_f)
        row_s[...] = jnp.zeros_like(row_s)
        row_m[...] = jnp.full_like(row_m, FLOOR)

        @pl.when(need_l[q])
        def _(q=q):
            for c in copies(0, q):
                c.wait()

        first = 0
        if own_first and q == 0:
            arrive(0)
            pair(0, 0, True)
            first = 1

        def step(r, _, q=q):
            @pl.when(live[q * nr + r] > 0)
            def _():
                arrive(r)
                pair(q, r, False)

            return 0

        lax.fori_loop(first, nr, step, 0)
        row_out[q : q + 1, :] = row_prev[q : q + 1, :]

        @pl.when(need_l[q])
        def _(q=q):
            found = fold(row_m[...].T, row_s[...].T, row_f[...].T, 0)
            row_out[q : q + 1, :] = log2_add(found, row_prev[q : q + 1, :])

    for r in range(nr):
        col_out[r : r + 1, :] = col_prev[r : r + 1, :]

        @pl.when(need_r[r])
        def _(r=r):
            col_out[r : r + 1, :] = log2_add(fold(col_m[r], col_s[r], col_f[r], 0), col_prev[r : r + 1, :])


def stage(name, live, row_prev, col_prev, lefts, rights, own_first=False):
    nl, nr = len(lefts), len(rights)
    flat, tables = [], []
    for side in (lefts, rights):
        table = []
        for slot, pieces in enumerate(side):
            for array, row in pieces:
                flat.append(array)
                table.append((slot, row, array.shape[0]))
        tables.append(tuple(table))
    plan = (nl, nr, tables[0], tables[1], own_first)
    f32 = jnp.float32
    return pl.pallas_call(
        functools.partial(stage_kernel, plan),
        out_shape=[jax.ShapeDtypeStruct((nl, B), f32), jax.ShapeDtypeStruct((nr, B), f32)],
        in_specs=[pl.BlockSpec(memory_space=pltpu.SMEM)]
        + [pl.BlockSpec(memory_space=pltpu.VMEM)] * 2
        + [pl.BlockSpec(memory_space=pl.ANY)] * len(flat),
        out_specs=[pl.BlockSpec(memory_space=pltpu.VMEM)] * 2,
        scratch_shapes=[
            pltpu.VMEM((nl, B, D), jnp.bfloat16),
            pltpu.VMEM((nr, B, D), jnp.bfloat16),
            pltpu.VMEM((B, B), f32),
            pltpu.VMEM((B, 128), f32),
            pltpu.VMEM((8, B), f32),
            pltpu.VMEM((8, 128), f32),
            pltpu.VMEM((B, 128), f32),
            pltpu.VMEM((B, 128), f32),
            pltpu.VMEM((B, 128), f32),
            pltpu.VMEM((nr, 8, B), f32),
            pltpu.VMEM((nr, 8, B), f32),
            pltpu.VMEM((nr, 8, B), f32),
            pltpu.SMEM((nr,), jnp.int32),
            pltpu.SemaphoreType.DMA((nl,)),
            pltpu.SemaphoreType.DMA((nr,)),
        ],
        compiler_params=pltpu.CompilerParams(vmem_limit_bytes=40 * 2**20),
        cost_estimate=pl.CostEstimate(
            flops=2 * B * B * D * max(1, nl * nr // 4), bytes_accessed=2 * B * D * (nl + nr), transcendentals=0
        ),
        name=name,
    )(live, row_prev, col_prev, *flat)


def last_kernel(own_ref, ring_ref, back_ref, o_ref):
    got = jnp.concatenate([own_ref[...], ring_ref[...], back_ref[...]], 0)
    best = jnp.max(got, 0, keepdims=True)
    total = jnp.sum(jnp.exp2(got - best), 0, keepdims=True)
    o_ref[...] = (best + jnp.log2(total)) * (LN2 / SCALE)


def body(embeddings, partners, pair_count):
    unit, top, low = normalize(embeddings)
    me = lax.axis_index("dp")
    column = me % RING
    ring = me - column
    chip, core = column // 2, column % 2
    half = B // 2
    none = jnp.full((1, B), FLOOR, jnp.float32)

    sib = send(unit, along(0, 1))
    a = send(unit, around(1))
    b = send(unit, around(-1))
    c_own = send(unit, along(-RING))
    over = [(d, d - d % 32 + (d + RING) % 32) for d in range(COUNT)]
    relay = dict(over)
    mid = send(low, over)
    mine = [(unit, 0)]
    self_row, _ = stage("own", jnp.ones((1,), jnp.int32), none, none, [mine], [mine], own_first=True)
    mid, a, b, c_own, sib, _ = lax.optimization_barrier((mid, a, b, c_own, sib, self_row))
    d_low = send(mid, [(relay[d], d - 2 * RING) for d in range(2 * RING, COUNT)])
    blocks = [mine, [(sib, 0)], [(c_own, 0)]]

    slots = partners[0]
    meta = jnp.where(jnp.arange(slots.shape[0]) < pair_count[0], slots, -1)[None, :]
    meta, _ = lax.optimization_barrier((meta, self_row))
    groups = [[r * RING + x * 2 + k for x in range(4)] for r in range(COUNT // RING) for k in range(2)]
    lists = lax.all_gather(meta, "dp", axis_index_groups=groups, tiled=True)
    lists = jnp.stack([lists[(chip + k) % 4] for k in (0, -1, 1, 2)])

    f_top = send(a[:half], around(1))
    f_low = send(b[half:], around(-1))
    c_sib = send(c_own, along(0, 1))
    late, _ = lax.optimization_barrier((top, c_own))
    d_top = send(late, along(-2 * RING))
    d_low_sib = send(d_low, along(0, 1))

    column_of = [chip * 2 + core, chip * 2 + 1 - core]
    targets = jnp.stack([ring + k * RING + c for k in range(3) for c in column_of]).astype(jnp.int32)
    live = jnp.any(lists[:, None, :] == targets[None, :, None], -1).astype(jnp.int32)
    live = live.at[0, 0].set(0)

    blocks.append([(c_sib, 0)])
    left = [mine, [(a, 0)], [(b, 0)]]
    row_prev = jnp.concatenate([self_row, none, none], 0)
    col_prev = jnp.concatenate([none] * 4, 0)
    row, col = stage("near", live[:3, :4].reshape(-1), row_prev, col_prev, left, blocks)
    d_top, f_top, f_low, row = lax.optimization_barrier((d_top, f_top, f_low, row))
    d_top_sib = send(d_top, along(0, 1))
    blocks.append([(d_top, 0), (d_low, half)])
    blocks.append([(d_top_sib, 0), (d_low_sib, half)])
    left.append([(f_top, 0), (f_low, half)])
    row_prev = jnp.concatenate([row, none], 0)
    col_prev = jnp.concatenate([col, none, none], 0)
    live_far = live.at[:3, :4].set(0)
    row, col = stage("far", live_far.reshape(-1), row_prev, col_prev, left, blocks)

    back = []
    for k in range(2):
        for flip in range(2):
            moved = send(col[2 + 2 * k + flip], along((k + 1) * RING, flip))
            back.append(jnp.where(me >= (k + 1) * RING, moved, FLOOR))
    ring_part = jnp.full((RING, B), FLOOR, jnp.float32)
    for q, dx in ((1, -1), (2, 1), (3, 2)):
        ring_part = lax.dynamic_update_slice(ring_part, row[q : q + 1], (((chip + dx) % 4) * 2 + core, 0))
    ring_part = lax.dynamic_update_slice(ring_part, col[1:2], (chip * 2 + 1 - core, 0))
    groups = [[r * RING + k for k in range(RING)] for r in range(COUNT // RING)]
    ring_got = lax.all_to_all(ring_part, "dp", 0, 0, axis_index_groups=groups, tiled=True)
    own = jnp.concatenate([row[:1], col[:1]], 0)
    out = pl.pallas_call(
        last_kernel,
        out_shape=jax.ShapeDtypeStruct((1, B), jnp.float32),
        name="last_sum",
    )(own, ring_got, jnp.stack(back))
    return out.reshape(B)


def solution(mesh):
    placed = (P("dp", None), P("dp", None), P("dp"))
    return jax.shard_map(body, mesh=mesh, in_specs=placed, out_specs=P("dp"), check_vma=False)
```

```python
import functools

import jax
import jax.numpy as jnp
from jax import lax
from jax.experimental import pallas as pl
from jax.experimental.pallas import tpu as pltpu
from jax.sharding import PartitionSpec as P

SCALE = 256.0
LOG2E = 1.4426950408889634
LN2 = 0.6931471805599453
GAIN = SCALE * LOG2E
PLAIN = 78.0 / SCALE
FLOOR = -1e30
MASKED = -1e27
SCRATCH = 17
B = 1024
D = 1024
CH = 256
G = 32
COUNT = 128
RING = 8
HALVES = B // 2 // CH


def around(dx):
    moves = []
    for d in range(COUNT):
        core, x, rest = d % 2, (d // 2) % 4, d // RING
        moves.append((d, rest * RING + ((x + dx) % 4) * 2 + core))
    return moves


def along(steps, flip=0):
    return [(d, (d + steps) ^ flip) for d in range(COUNT) if 0 <= d + steps < COUNT]


def send(value, moves):
    return lax.ppermute(value, "dp", moves)


def unit_kernel(x_ref, o_ref, top_ref, low_ref):
    i = pl.program_id(0)
    for g in range(CH // G):
        at = slice(g * G, (g + 1) * G)
        v = x_ref[at, :].astype(jnp.float32)
        size = jnp.sum(v * v, -1, keepdims=True)
        o_ref[at, :] = (v * lax.rsqrt(size + 1e-06)).astype(jnp.bfloat16)

    @pl.when(i < HALVES)
    def _():
        top_ref[...] = o_ref[...]

    @pl.when(i >= HALVES)
    def _():
        low_ref[...] = o_ref[...]


def normalize(embeddings):
    bf16 = jnp.bfloat16
    return pl.pallas_call(
        unit_kernel,
        grid=(B // CH,),
        in_specs=[pl.BlockSpec((CH, D), lambda i: (i, 0))],
        out_specs=[
            pl.BlockSpec((CH, D), lambda i: (i, 0)),
            pl.BlockSpec((CH, D), lambda i: (jnp.minimum(i, HALVES - 1), 0)),
            pl.BlockSpec((CH, D), lambda i: (jnp.maximum(i - HALVES, 0), 0)),
        ],
        out_shape=[
            jax.ShapeDtypeStruct((B, D), bf16),
            jax.ShapeDtypeStruct((B // 2, D), bf16),
            jax.ShapeDtypeStruct((B // 2, D), bf16),
        ],
        name="unit_rows",
    )(embeddings)


def lanes(value, op):
    return functools.reduce(op, [value[:, q * 128 : (q + 1) * 128] for q in range(value.shape[1] // 128)])


def rows8(value, op):
    return functools.reduce(op, [value[q * 8 : (q + 1) * 8, :] for q in range(value.shape[0] // 8)])


def fold(m, s, f, axis):
    top = jnp.max(m, axis, keepdims=True)
    plain = jnp.sum(f, axis, keepdims=True)
    top = jnp.maximum(top, jnp.where(plain > 0.0, 0.0, FLOOR))
    total = jnp.sum(s * jnp.exp2(m - top), axis, keepdims=True)
    total = total + plain * jnp.exp2(jnp.minimum(-top, 0.0))
    return jnp.maximum(top + jnp.log2(total), FLOOR)


def log2_add(a, b):
    top = jnp.maximum(a, b)
    return top + jnp.log2(jnp.exp2(a - top) + jnp.exp2(b - top))


def stage_kernel(plan, live, row_prev, col_prev, *refs):
    nl, nr, lefts, rights, own_first, last = plan
    blocks, refs = refs[: len(lefts) + len(rights)], refs[len(lefts) + len(rights) :]
    outs, refs = refs[: -SCRATCH], refs[-SCRATCH:]
    row_out, col_out = refs[-2:] if last else outs
    (lbuf, rbuf, sc, row_t, col_t, chk, row_f, row_m, row_s, col_f, col_m, col_s, waited, lsem, rsem) = refs[:-2]

    def copies(side, slot):
        pieces = lefts if side == 0 else rights
        base = 0 if side == 0 else len(lefts)
        buf, sem = (lbuf, lsem) if side == 0 else (rbuf, rsem)
        made = []
        for i, (s, row, count) in enumerate(pieces):
            if s == slot:
                made.append(
                    pltpu.make_async_copy(blocks[base + i], buf.at[slot, row : row + count, :], sem.at[slot])
                )
        return made

    def used(flags):
        return functools.reduce(jnp.logical_or, [f > 0 for f in flags])

    need_l = [used([live[q * nr + r] for r in range(nr)]) for q in range(nl)]
    need_r = [used([live[q * nr + r] for q in range(nl)]) for r in range(nr)]
    for q in range(nl):

        @pl.when(need_l[q])
        def _(q=q):
            for c in copies(0, q):
                c.start()

    for r in range(nr):
        waited[r] = 0

        @pl.when(need_r[r])
        def _(r=r):
            for c in copies(1, r):
                c.start()

    col_f[...] = jnp.zeros_like(col_f)
    col_s[...] = jnp.zeros_like(col_s)
    col_m[...] = jnp.full_like(col_m, FLOOR)

    def pair(q, r, diag):
        def dot(i):
            sc[i * CH : (i + 1) * CH, :] = lax.dot_general(
                lbuf[q, i * CH : (i + 1) * CH, :],
                rbuf[r],
                (((1,), (1,)), ((), ())),
                preferred_element_type=jnp.float32,
            )

        def sums(i):
            cols = jnp.zeros((8, B), jnp.float32)
            size = jnp.zeros((8, 128), jnp.float32)
            for g in range(CH // G):
                at = i * CH + g * G
                v = sc[at : at + G, :]
                if diag:
                    r_at = lax.broadcasted_iota(jnp.int32, (G, B), 0) + at
                    c_at = lax.broadcasted_iota(jnp.int32, (G, B), 1)
                    eye = r_at == c_at
                    absv = jnp.where(eye, 0.0, jnp.abs(v))
                    v = jnp.where(eye, MASKED, v)
                    sc[at : at + G, :] = v
                else:
                    absv = jnp.abs(v)
                e = jnp.exp2(v * GAIN)
                row_t[at : at + G, :] = lanes(e, jnp.add)
                if not diag:
                    cols = cols + rows8(e, jnp.add)
                size = jnp.maximum(size, rows8(lanes(absv, jnp.maximum), jnp.maximum))
            if not diag:
                col_t[...] = cols if i == 0 else col_t[...] + cols
            chk[...] = size if i == 0 else jnp.maximum(chk[...], size)

        n = B // CH
        dot(0)
        for i in range(n):
            if i + 1 < n:
                dot(i + 1)
            sums(i)
        plain = jnp.max(chk[...]) <= PLAIN

        @pl.when(plain)
        def _():
            row_f[...] += row_t[...]
            if not diag:
                col_f[r] += col_t[...]

        @pl.when(jnp.logical_not(plain))
        def _():
            def group(g, _):
                at = pl.multiple_of(g * G, G)
                w = sc[pl.ds(at, G), :] * GAIN
                old = row_m[pl.ds(at, G), :]
                top = jnp.maximum(old, lanes(w, jnp.maximum))
                total = row_s[pl.ds(at, G), :] * jnp.exp2(old - top)
                for k in range(B // 128):
                    total = total + jnp.exp2(w[:, k * 128 : (k + 1) * 128] - top)
                row_m[pl.ds(at, G), :] = top
                row_s[pl.ds(at, G), :] = total
                if not diag:
                    old = col_m[r]
                    top = jnp.maximum(old, rows8(w, jnp.maximum))
                    total = col_s[r] * jnp.exp2(old - top)
                    for k in range(G // 8):
                        total = total + jnp.exp2(w[k * 8 : (k + 1) * 8, :] - top)
                    col_m[r] = top
                    col_s[r] = total
                return 0

            lax.fori_loop(0, B // G, group, 0)

    def arrive(r):
        @pl.when(waited[r] == 0)
        def _():
            for s in range(nr):

                @pl.when(r == s)
                def _(s=s):
                    for c in copies(1, s):
                        c.wait()

            waited[r] = 1

    for q in range(nl):
        row_f[...] = jnp.zeros_like(row_f)
        row_s[...] = jnp.zeros_like(row_s)
        row_m[...] = jnp.full_like(row_m, FLOOR)

        @pl.when(need_l[q])
        def _(q=q):
            for c in copies(0, q):
                c.wait()

        first = 0
        if own_first and q == 0:
            arrive(0)
            pair(0, 0, True)
            first = 1

        def step(r, _, q=q):
            @pl.when(live[q * nr + r] > 0)
            def _():
                arrive(r)
                pair(q, r, False)

            return 0

        lax.fori_loop(first, nr, step, 0)
        row_out[q : q + 1, :] = row_prev[q : q + 1, :]

        @pl.when(need_l[q])
        def _(q=q):
            found = fold(row_m[...].T, row_s[...].T, row_f[...].T, 0)
            row_out[q : q + 1, :] = log2_add(found, row_prev[q : q + 1, :])

    for r in range(nr):
        col_out[r : r + 1, :] = col_prev[r : r + 1, :]

        @pl.when(need_r[r])
        def _(r=r):
            col_out[r : r + 1, :] = log2_add(fold(col_m[r], col_s[r], col_f[r], 0), col_prev[r : r + 1, :])

    if last:
        ring_out = outs[0]
        ring_out[...] = jnp.full_like(ring_out, FLOOR)
        chip, core = live[nl * nr], live[nl * nr + 1]
        mine = chip * 2 + core
        ring_out[pl.ds(mine, 1), :] = log2_add(row_out[0:1, :], col_out[0:1, :])
        ring_out[pl.ds(mine + 1 - 2 * core, 1), :] = col_out[1:2, :]
        for q, dx in ((1, 3), (2, 1), (3, 2)):
            ring_out[pl.ds((chip + dx) % 4 * 2 + core, 1), :] = row_out[q : q + 1, :]
        for r in range(2, nr):
            outs[r - 1][...] = col_out[r : r + 1, :]


def stage(name, live, row_prev, col_prev, lefts, rights, own_first=False, last=False):
    nl, nr = len(lefts), len(rights)
    flat, tables = [], []
    for side in (lefts, rights):
        table = []
        for slot, pieces in enumerate(side):
            for array, row in pieces:
                flat.append(array)
                table.append((slot, row, array.shape[0]))
        tables.append(tuple(table))
    plan = (nl, nr, tables[0], tables[1], own_first, last)
    f32 = jnp.float32
    shapes = [(RING, B)] + [(1, B)] * (nr - 2) if last else [(nl, B), (nr, B)]
    shapes = [jax.ShapeDtypeStruct(shape, f32) for shape in shapes]
    return pl.pallas_call(
        functools.partial(stage_kernel, plan),
        out_shape=shapes,
        in_specs=[pl.BlockSpec(memory_space=pltpu.SMEM)]
        + [pl.BlockSpec(memory_space=pltpu.VMEM)] * 2
        + [pl.BlockSpec(memory_space=pl.ANY)] * len(flat),
        out_specs=[pl.BlockSpec(memory_space=pltpu.VMEM)] * len(shapes),
        scratch_shapes=[
            pltpu.VMEM((nl, B, D), jnp.bfloat16),
            pltpu.VMEM((nr, B, D), jnp.bfloat16),
            pltpu.VMEM((B, B), f32),
            pltpu.VMEM((B, 128), f32),
            pltpu.VMEM((8, B), f32),
            pltpu.VMEM((8, 128), f32),
            pltpu.VMEM((B, 128), f32),
            pltpu.VMEM((B, 128), f32),
            pltpu.VMEM((B, 128), f32),
            pltpu.VMEM((nr, 8, B), f32),
            pltpu.VMEM((nr, 8, B), f32),
            pltpu.VMEM((nr, 8, B), f32),
            pltpu.SMEM((nr,), jnp.int32),
            pltpu.SemaphoreType.DMA((nl,)),
            pltpu.SemaphoreType.DMA((nr,)),
            pltpu.VMEM((nl, B), f32),
            pltpu.VMEM((nr, B), f32),
        ],
        compiler_params=pltpu.CompilerParams(vmem_limit_bytes=62 * 2**20),
        cost_estimate=pl.CostEstimate(
            flops=2 * B * B * D * max(1, nl * nr // 4), bytes_accessed=2 * B * D * (nl + nr), transcendentals=0
        ),
        name=name,
    )(live, row_prev, col_prev, *flat)


def last_kernel(row_ref, ring_ref, *refs):
    parts, o_ref = refs[:-1], refs[-1]
    row = row_ref[0]
    got = [ring_ref[...]]
    for k, part in enumerate(parts):
        got.append(jnp.where(row > k // 2, part[...], FLOOR))
    got = jnp.concatenate(got, 0)
    best = jnp.max(got, 0, keepdims=True)
    total = jnp.sum(jnp.exp2(got - best), 0, keepdims=True)
    o_ref[...] = (best + jnp.log2(total)) * (LN2 / SCALE)


def body(embeddings, partners, pair_count):
    unit, top, low = normalize(embeddings)
    me = lax.axis_index("dp")
    column = me % RING
    ring = me - column
    chip, core = column // 2, column % 2
    half = B // 2
    none = jnp.full((1, B), FLOOR, jnp.float32)

    sib = send(unit, along(0, 1))
    a = send(unit, around(1))
    b = send(unit, around(-1))
    c_own = send(unit, along(-RING))
    over = [(d, d - d % 32 + (d + RING) % 32) for d in range(COUNT)]
    relay = dict(over)
    mid = send(low, over)
    mine = [(unit, 0)]
    self_row, _ = stage("own", jnp.ones((1,), jnp.int32), none, none, [mine], [mine], own_first=True)
    slots = partners[0]
    meta = jnp.where(jnp.arange(slots.shape[0]) < pair_count[0], slots, -1)[None, :]
    meta, _ = lax.optimization_barrier((meta, self_row))
    groups = [[r * RING + x * 2 + k for x in range(4)] for r in range(COUNT // RING) for k in range(2)]
    meta = jnp.broadcast_to(meta, (4, meta.shape[1]))
    lists = lax.all_to_all(meta, "dp", 0, 0, axis_index_groups=groups, tiled=True)
    mid, lists = lax.optimization_barrier((mid, lists))
    d_low = send(mid, [(relay[d], d - 2 * RING) for d in range(2 * RING, COUNT)])
    a, b, c_own, d_low = lax.optimization_barrier((a, b, c_own, d_low))
    blocks = [mine, [(sib, 0)], [(c_own, 0)]]
    lists = jnp.stack([lists[(chip + k) % 4] for k in (0, -1, 1, 2)])

    f_top = send(a[:half], around(1))
    f_low = send(b[half:], around(-1))
    c_sib = send(c_own, along(0, 1))
    late, _ = lax.optimization_barrier((top, c_own))
    d_top = send(late, along(-2 * RING))
    d_low_sib = send(d_low, along(0, 1))

    column_of = [chip * 2 + core, chip * 2 + 1 - core]
    targets = jnp.stack([ring + k * RING + c for k in range(3) for c in column_of]).astype(jnp.int32)
    live = jnp.any(lists[:, None, :] == targets[None, :, None], -1).astype(jnp.int32)
    live = live.at[0, 0].set(0)

    blocks.append([(c_sib, 0)])
    left = [mine, [(a, 0)], [(b, 0)]]
    row_prev = jnp.concatenate([self_row, none, none], 0)
    col_prev = jnp.concatenate([none] * 4, 0)
    row, col = stage("near", live[:3, :4].reshape(-1), row_prev, col_prev, left, blocks)
    d_top, f_top, f_low, row = lax.optimization_barrier((d_top, f_top, f_low, row))
    d_top_sib = send(d_top, along(0, 1))
    blocks.append([(d_top, 0), (d_low, half)])
    blocks.append([(d_top_sib, 0), (d_low_sib, half)])
    left.append([(f_top, 0), (f_low, half)])
    row_prev = jnp.concatenate([row, none], 0)
    col_prev = jnp.concatenate([col, none, none], 0)
    live_far = live.at[:3, :4].set(0)
    place = jnp.stack([chip, core]).astype(jnp.int32)
    live_far = jnp.concatenate([live_far.reshape(-1), place])
    ring_part, *cols = stage("far", live_far, row_prev, col_prev, left, blocks, last=True)

    back = [send(col, along((k // 2 + 1) * RING, k % 2)) for k, col in enumerate(cols)]
    groups = [[r * RING + k for k in range(RING)] for r in range(COUNT // RING)]
    ring_got = lax.all_to_all(ring_part, "dp", 0, 0, axis_index_groups=groups, tiled=True)
    out = pl.pallas_call(
        last_kernel,
        in_specs=[pl.BlockSpec(memory_space=pltpu.SMEM)] + [pl.BlockSpec(memory_space=pltpu.VMEM)] * 5,
        out_shape=jax.ShapeDtypeStruct((1, B), jnp.float32),
        name="last_sum",
    )((me // RING)[None].astype(jnp.int32), ring_got, *back)
    return out.reshape(B)


def solution(mesh):
    placed = (P("dp", None), P("dp", None), P("dp"))
    return jax.shard_map(body, mesh=mesh, in_specs=placed, out_specs=P("dp"), check_vma=False)
```

```python
import functools

import jax
import jax.numpy as jnp
from jax import lax
from jax.experimental import pallas as pl
from jax.experimental.pallas import tpu as pltpu
from jax.sharding import PartitionSpec as P

SCALE = 256.0
LOG2E = 1.4426950408889634
LN2 = 0.6931471805599453
GAIN = SCALE * LOG2E
PLAIN = 78.0 / SCALE
FLOOR = -1e30
MASKED = -1e27
SCRATCH = 17
PLACES = [(0, 0), (0, 1), (3, 0), (1, 0), (3, 1), (1, 1), (2, 0), (2, 1)]
B = 1024
D = 1024
CH = 256
G = 32
COUNT = 128
RING = 8
HALVES = B // 2 // CH
LIST = 16
GRANT = 62 * 2**20


def around(dx):
    moves = []
    for d in range(COUNT):
        core, x, rest = d % 2, (d // 2) % 4, d // RING
        moves.append((d, rest * RING + ((x + dx) % 4) * 2 + core))
    return moves


def along(steps, flip=0):
    return [(d, (d + steps) ^ flip) for d in range(COUNT) if 0 <= d + steps < COUNT]


def send(value, moves):
    return lax.ppermute(value, "dp", moves)


def unit_kernel(list_ref, count_ref, x_ref, o_ref, top_ref, low_ref, x, o, in_sem, out_sem):
    def rows(i):
        return pl.ds(i * CH, CH)

    loads = [pltpu.make_async_copy(x_ref.at[rows(i), :], x.at[rows(i), :], in_sem.at[i]) for i in range(B // CH)]
    for load in loads:
        load.start()
    lane = lax.broadcasted_iota(jnp.int32, (LIST, D), 1)
    pairs = jnp.full((LIST, D), -1.0, jnp.float32)
    for k in range(list_ref.shape[1]):
        entry = jnp.where(k < count_ref[0], list_ref[0, k], -1).astype(jnp.float32)
        pairs = jnp.where(lane == k, entry, pairs)
    o[B : B + LIST, :] = pairs.astype(jnp.bfloat16)
    stores = [pltpu.make_async_copy(o.at[pl.ds(B, LIST), :], o_ref.at[pl.ds(B, LIST), :], out_sem.at[0])]
    stores[0].start()
    for i in range(B // CH):
        loads[i].wait()
        for g in range(CH // G):
            at = slice(i * CH + g * G, i * CH + (g + 1) * G)
            v = x[at, :].astype(jnp.float32)
            size = jnp.sum(v * v, -1, keepdims=True)
            o[at, :] = (v * lax.rsqrt(size + 1e-06)).astype(jnp.bfloat16)
        stores.append(pltpu.make_async_copy(o.at[rows(i), :], o_ref.at[rows(i), :], out_sem.at[2 * i + 1]))
        half = top_ref.at[rows(i), :] if i < HALVES else low_ref.at[rows(i - HALVES), :]
        stores.append(pltpu.make_async_copy(o.at[rows(i), :], half, out_sem.at[2 * i + 2]))
        stores[-2].start()
        stores[-1].start()
    for store in stores:
        store.wait()


def normalize(embeddings, partners, pair_count):
    bf16 = jnp.bfloat16
    smem, anywhere = pl.BlockSpec(memory_space=pltpu.SMEM), pl.BlockSpec(memory_space=pl.ANY)
    return pl.pallas_call(
        unit_kernel,
        in_specs=[smem, smem, anywhere],
        out_specs=[anywhere] * 3,
        out_shape=[
            jax.ShapeDtypeStruct((B + LIST, D), bf16),
            jax.ShapeDtypeStruct((B // 2, D), bf16),
            jax.ShapeDtypeStruct((B // 2, D), bf16),
        ],
        scratch_shapes=[
            pltpu.VMEM((B, D), bf16),
            pltpu.VMEM((B + LIST, D), bf16),
            pltpu.SemaphoreType.DMA((B // CH,)),
            pltpu.SemaphoreType.DMA((2 * (B // CH) + 1,)),
        ],
        compiler_params=pltpu.CompilerParams(vmem_limit_bytes=GRANT),
        name="unit_rows",
    )(partners, pair_count, embeddings)


def halves_kernel(a_ref, b_ref, top_ref, low_ref, sem):
    copies = [
        pltpu.make_async_copy(a_ref.at[pl.ds(0, B // 2), :], top_ref, sem.at[0]),
        pltpu.make_async_copy(b_ref.at[pl.ds(B // 2, B // 2 + LIST), :], low_ref, sem.at[1]),
    ]
    for copy in copies:
        copy.start()
    for copy in copies:
        copy.wait()


def halves(a, b):
    bf16, anywhere = jnp.bfloat16, pl.BlockSpec(memory_space=pl.ANY)
    return pl.pallas_call(
        halves_kernel,
        in_specs=[anywhere] * 2,
        out_specs=[anywhere] * 2,
        out_shape=[jax.ShapeDtypeStruct((B // 2, D), bf16), jax.ShapeDtypeStruct((B // 2 + LIST, D), bf16)],
        scratch_shapes=[pltpu.SemaphoreType.DMA((2,))],
        compiler_params=pltpu.CompilerParams(vmem_limit_bytes=GRANT),
        name="halves",
    )(a, b)


def lanes(value, op):
    return functools.reduce(op, [value[:, q * 128 : (q + 1) * 128] for q in range(value.shape[1] // 128)])


def rows8(value, op):
    return functools.reduce(op, [value[q * 8 : (q + 1) * 8, :] for q in range(value.shape[0] // 8)])


def fold(m, s, f, axis):
    top = jnp.max(m, axis, keepdims=True)
    plain = jnp.sum(f, axis, keepdims=True)
    top = jnp.maximum(top, jnp.where(plain > 0.0, 0.0, FLOOR))
    total = jnp.sum(s * jnp.exp2(m - top), axis, keepdims=True)
    total = total + plain * jnp.exp2(jnp.minimum(-top, 0.0))
    return jnp.maximum(top + jnp.log2(total), FLOOR)


def log2_add(a, b):
    top = jnp.maximum(a, b)
    return top + jnp.log2(jnp.exp2(a - top) + jnp.exp2(b - top))


def stage_kernel(plan, live, *refs):
    nl, nr, lefts, rights, widths, nrow, ncol, own_first, last = plan
    prevs, refs = refs[:2], refs[2:]
    blocks, refs = refs[: len(lefts) + len(rights)], refs[len(lefts) + len(rights) :]
    outs, refs = refs[:-SCRATCH], refs[-SCRATCH:]
    row_out, col_out = refs[-2:] if last else outs
    (lbuf, rbuf, sc, row_t, col_t, chk, row_f, row_m, row_s, col_f, col_m, col_s, waited, lsem, rsem) = refs[:-2]

    def copies(side, slot):
        pieces = lefts if side == 0 else rights
        base = 0 if side == 0 else len(lefts)
        buf, sem = (lbuf, lsem) if side == 0 else (rbuf, rsem)
        made = []
        for i, (s, row, count) in enumerate(pieces):
            if s == slot:
                made.append(
                    pltpu.make_async_copy(
                        blocks[base + i].at[pl.ds(0, count), :], buf.at[slot, pl.ds(row, count), :], sem.at[slot]
                    )
                )
        return made

    def used(flags):
        return functools.reduce(jnp.logical_or, [f > 0 for f in flags])

    need_l = [used([live[q * nr + r] for r in range(nr)]) for q in range(nl)]
    need_r = [used([live[q * nr + r] for q in range(nl)]) for r in range(nr)]
    for r in range(nr):
        waited[r] = 0

        @pl.when(need_r[r])
        def _(r=r):
            for c in copies(1, r):
                c.start()

    for q in range(nl):

        @pl.when(need_l[q])
        def _(q=q):
            for c in copies(0, q):
                c.start()

    col_f[...] = jnp.zeros_like(col_f)
    col_s[...] = jnp.zeros_like(col_s)
    col_m[...] = jnp.full_like(col_m, FLOOR)

    def pair(q, r, width, diag):
        def dot(i):
            sc[i * CH : (i + 1) * CH, :width] = lax.dot_general(
                lbuf[q, i * CH : (i + 1) * CH, :],
                rbuf[r, :width, :],
                (((1,), (1,)), ((), ())),
                preferred_element_type=jnp.float32,
            )

        def sums(i):
            cols = jnp.zeros((8, width), jnp.float32)
            size = jnp.zeros((8, 128), jnp.float32)
            for g in range(CH // G):
                at = i * CH + g * G
                v = sc[at : at + G, :width]
                if diag:
                    r_at = lax.broadcasted_iota(jnp.int32, (G, width), 0) + at
                    c_at = lax.broadcasted_iota(jnp.int32, (G, width), 1)
                    eye = r_at == c_at
                    absv = jnp.where(eye, 0.0, jnp.abs(v))
                    v = jnp.where(eye, MASKED, v)
                    sc[at : at + G, :width] = v
                else:
                    absv = jnp.abs(v)
                e = jnp.exp2(v * GAIN)
                row_t[at : at + G, :] = lanes(e, jnp.add)
                if not diag:
                    cols = cols + rows8(e, jnp.add)
                size = jnp.maximum(size, rows8(lanes(absv, jnp.maximum), jnp.maximum))
            if not diag:
                col_t[:, :width] = cols if i == 0 else col_t[:, :width] + cols
            chk[...] = size if i == 0 else jnp.maximum(chk[...], size)

        n = B // CH
        dot(0)
        for i in range(n):
            if i + 1 < n:
                dot(i + 1)
            sums(i)
        plain = jnp.max(chk[...]) <= PLAIN

        @pl.when(plain)
        def _():
            row_f[...] += row_t[...]
            if not diag:
                col_f[r, :, :width] += col_t[:, :width]

        @pl.when(jnp.logical_not(plain))
        def _():
            def group(g, _):
                at = pl.multiple_of(g * G, G)
                w = sc[pl.ds(at, G), :width] * GAIN
                old = row_m[pl.ds(at, G), :]
                top = jnp.maximum(old, lanes(w, jnp.maximum))
                total = row_s[pl.ds(at, G), :] * jnp.exp2(old - top)
                for k in range(width // 128):
                    total = total + jnp.exp2(w[:, k * 128 : (k + 1) * 128] - top)
                row_m[pl.ds(at, G), :] = top
                row_s[pl.ds(at, G), :] = total
                if not diag:
                    old = col_m[r, :, :width]
                    top = jnp.maximum(old, rows8(w, jnp.maximum))
                    total = col_s[r, :, :width] * jnp.exp2(old - top)
                    for k in range(G // 8):
                        total = total + jnp.exp2(w[k * 8 : (k + 1) * 8, :] - top)
                    col_m[r, :, :width] = top
                    col_s[r, :, :width] = total
                return 0

            lax.fori_loop(0, B // G, group, 0)

    def arrive(r):
        @pl.when(waited[r] == 0)
        def _():
            for s in range(nr):

                @pl.when(r == s)
                def _(s=s):
                    for c in copies(1, s):
                        c.wait()

            waited[r] = 1

    def runs():
        start = 0
        for r in range(1, nr + 1):
            if r == nr or widths[r] != widths[start]:
                yield start, r, widths[start]
                start = r

    def left(q, _):
        needed = functools.reduce(jnp.logical_or, [live[q * nr + r] > 0 for r in range(nr)])
        row_out[pl.ds(q, 1), :] = jnp.full((1, B), FLOOR, jnp.float32)

        @pl.when(needed)
        def _():
            row_f[...] = jnp.zeros_like(row_f)
            row_s[...] = jnp.zeros_like(row_s)
            row_m[...] = jnp.full_like(row_m, FLOOR)
            for s in range(nl):

                @pl.when(q == s)
                def _(s=s):
                    for c in copies(0, s):
                        c.wait()

            if own_first:

                @pl.when(q == 0)
                def _():
                    arrive(0)
                    pair(0, 0, B, True)

            for start, stop, width in runs():

                def step(r, _, width=width):
                    go = live[q * nr + r] > 0
                    if own_first:
                        go = jnp.logical_and(go, q + r > 0)

                    @pl.when(go)
                    def _():
                        arrive(r)
                        pair(q, r, width, False)

                    return 0

                lax.fori_loop(start, stop, step, 0)
            row_out[pl.ds(q, 1), :] = fold(row_m[...].T, row_s[...].T, row_f[...].T, 0)

        return 0

    lax.fori_loop(0, nl, left, 0)
    for q in range(nrow):
        row_out[q : q + 1, :] = log2_add(row_out[q : q + 1, :], prevs[0][q : q + 1, :])
    for r in range(nr):
        col_out[r : r + 1, :] = jnp.full((1, B), FLOOR, jnp.float32)

        @pl.when(need_r[r])
        def _(r=r):
            col_out[r : r + 1, :] = fold(col_m[r], col_s[r], col_f[r], 0)

        if r < ncol:
            col_out[r : r + 1, :] = log2_add(col_out[r : r + 1, :], prevs[1][r : r + 1, :])

    if last:
        ring_out, next_out, after_out = outs
        chip, core = live[nl * nr], live[nl * nr + 1]
        for q in range(nl):
            at = (chip + PLACES[q][0]) % 4 * 2 + (core + PLACES[q][1]) % 2
            row = row_out[q : q + 1, :]
            ring_out[at] = row if q else log2_add(row, col_out[0:1, :])
        next_out[...] = col_out[1:2, :]
        after_out[:, : B // 2] = col_out[3:4, : B // 2]
        after_out[:, B // 2 :] = col_out[2:3, : B // 2]


def stage(name, live, lefts, rights, row_prev=None, col_prev=None, own_first=False, last=False):
    nl, nr = len(lefts), len(rights)
    flat, tables = [], []
    for side in (lefts, rights):
        table = []
        for slot, pieces in enumerate(side):
            for array, row, count in pieces:
                flat.append(array)
                table.append((slot, row, count))
        tables.append(tuple(table))
    widths = tuple(sum(piece[2] for piece in pieces) for pieces in rights)
    prevs = [jnp.zeros((1, B), jnp.float32) if p is None else p for p in (row_prev, col_prev)]
    nrow, ncol = (0 if p is None else p.shape[0] for p in (row_prev, col_prev))
    plan = (nl, nr, tables[0], tables[1], widths, nrow, ncol, own_first, last)
    f32 = jnp.float32
    shapes = [(RING, 1, B), (1, B), (1, B)] if last else [(nl, B), (nr, B)]
    shapes = [jax.ShapeDtypeStruct(shape, f32) for shape in shapes]
    return pl.pallas_call(
        functools.partial(stage_kernel, plan),
        out_shape=shapes,
        in_specs=[pl.BlockSpec(memory_space=pltpu.SMEM)]
        + [pl.BlockSpec(memory_space=pltpu.VMEM)] * 2
        + [pl.BlockSpec(memory_space=pl.ANY)] * len(flat),
        out_specs=[pl.BlockSpec(memory_space=pltpu.VMEM)] * len(shapes),
        scratch_shapes=[
            pltpu.VMEM((nl, B, D), jnp.bfloat16),
            pltpu.VMEM((nr, B, D), jnp.bfloat16),
            pltpu.VMEM((B, B), f32),
            pltpu.VMEM((B, 128), f32),
            pltpu.VMEM((8, B), f32),
            pltpu.VMEM((8, 128), f32),
            pltpu.VMEM((B, 128), f32),
            pltpu.VMEM((B, 128), f32),
            pltpu.VMEM((B, 128), f32),
            pltpu.VMEM((nr, 8, B), f32),
            pltpu.VMEM((nr, 8, B), f32),
            pltpu.VMEM((nr, 8, B), f32),
            pltpu.SMEM((nr,), jnp.int32),
            pltpu.SemaphoreType.DMA((nl,)),
            pltpu.SemaphoreType.DMA((nr,)),
            pltpu.VMEM((nl, B), f32),
            pltpu.VMEM((nr, B), f32),
        ],
        compiler_params=pltpu.CompilerParams(vmem_limit_bytes=GRANT),
        cost_estimate=pl.CostEstimate(
            flops=2 * B * B * D * max(1, nl * nr // 4), bytes_accessed=2 * B * D * (nl + nr), transcendentals=0
        ),
        name=name,
    )(live, *prevs, *flat)


def last_kernel(row_ref, ring_ref, *refs):
    parts, o_ref = refs[:-1], refs[-1]
    row = row_ref[0]
    got = [ring_ref[k] for k in range(RING)]
    for k, part in enumerate(parts):
        got.append(jnp.where(row > k, part[...], FLOOR))
    got = jnp.concatenate(got, 0)
    best = jnp.max(got, 0, keepdims=True)
    total = jnp.sum(jnp.exp2(got - best), 0, keepdims=True)
    o_ref[...] = (best + jnp.log2(total)) * (LN2 / SCALE)


def body(embeddings, partners, pair_count):
    unit, top, low = normalize(embeddings, partners, pair_count)
    me = lax.axis_index("dp")
    column = me % RING
    half = B // 2
    swap = along(0, 1)

    sib = send(unit, swap)
    a = send(unit, around(1))
    b = send(unit, around(-1))
    c = send(unit, along(-RING))
    over = [(d, d - d % 32 + (d + RING) % 32) for d in range(COUNT)]
    relay = dict(over)
    mid = send(low, over)

    targets = me + RING * jnp.array([0, 1, 2, 2], jnp.int32)

    def pairs_of(*arrays):
        lists = jnp.concatenate([x[-LIST : 1 - LIST, :16] for x in arrays], 0).astype(jnp.int32)
        return jnp.any(lists[:, None, :] == targets[None, :, None], -1).astype(jnp.int32)

    def whole(array):
        return [(array, 0, B)]

    near_pairs = pairs_of(unit, sib)
    rights = [whole(unit)]
    row_0, col_0 = stage("own", near_pairs[:, 0], [whole(unit), whole(sib)], rights, own_first=True)

    mid, row_0 = lax.optimization_barrier((mid, row_0))
    d_low = send(mid, [(relay[d], d - 2 * RING) for d in range(2 * RING, COUNT)])
    a, b, c, d_low = lax.optimization_barrier((a, b, c, d_low))

    a_top, b_low = halves(a, b)
    f_top = send(a_top, around(1))
    f_low = send(b_low, around(-1))
    late, _ = lax.optimization_barrier((top, a_top))
    d_top = send(late, along(-2 * RING))
    a_sib = send(a, swap)
    b_sib = send(b, swap)

    rights = [whole(unit), whole(c), [(d_low, 0, half)]]
    live = jnp.concatenate([near_pairs.at[:, 0].set(0), pairs_of(a, b)], 0)[:, :3]
    lefts = [whole(unit), whole(sib), whole(a), whole(b)]
    row_1, col_1 = stage("near", live.reshape(-1), lefts, rights, row_0, col_0)
    a_sib, b_sib, row_1 = lax.optimization_barrier((a_sib, b_sib, row_1))
    more = pairs_of(a_sib, b_sib)
    row_2, col_2 = stage("mid", more[:, :3].reshape(-1), [whole(a_sib), whole(b_sib)], rights, None, col_1)
    f_top, f_low, d_top, row_2 = lax.optimization_barrier((f_top, f_low, d_top, row_2))
    f_top_sib = send(f_top, swap)
    f_low_sib = send(f_low, swap)

    rights.append([(d_top, 0, half)])
    lefts += [whole(a_sib), whole(b_sib)]
    lefts += [[(f_top, 0, half), (f_low, half, half)], [(f_top_sib, 0, half), (f_low_sib, half, half)]]
    early = jnp.concatenate([near_pairs, pairs_of(a, b), more], 0).at[:, :3].set(0)
    live = jnp.concatenate([early, pairs_of(f_low, f_low_sib)], 0)
    place = jnp.stack([column // 2, column % 2]).astype(jnp.int32)
    live = jnp.concatenate([live.reshape(-1), place])
    row_prev = jnp.concatenate([row_1, row_2], 0)
    ring_part, next_part, after_part = stage("far", live, lefts, rights, row_prev, col_2, last=True)

    next_got = send(next_part, along(RING))
    after_got = send(after_part, along(2 * RING))
    groups = [[r * RING + k for k in range(RING)] for r in range(COUNT // RING)]
    ring_got = lax.all_to_all(ring_part, "dp", 0, 0, axis_index_groups=groups, tiled=True)
    out = pl.pallas_call(
        last_kernel,
        in_specs=[pl.BlockSpec(memory_space=pltpu.SMEM)] + [pl.BlockSpec(memory_space=pltpu.VMEM)] * 3,
        out_shape=jax.ShapeDtypeStruct((1, B), jnp.float32),
        name="last_sum",
    )((me // RING)[None].astype(jnp.int32), ring_got, next_got, after_got)
    return out.reshape(B)


def solution(mesh):
    placed = (P("dp", None), P("dp", None), P("dp"))
    return jax.shard_map(body, mesh=mesh, in_specs=placed, out_specs=P("dp"), check_vma=False)
```

```python
import functools

import jax
import jax.numpy as jnp
from jax import lax
from jax.experimental import pallas as pl
from jax.experimental.pallas import tpu as pltpu
from jax.sharding import PartitionSpec as P

SCALE = 256.0
LOG2E = 1.4426950408889634
LN2 = 0.6931471805599453
GAIN = SCALE * LOG2E
PLAIN = 78.0 / SCALE
FLOOR = -1e30
MASKED = -1e27
SCRATCH = 17
PLACES = [(0, 0), (0, 1), (3, 0), (1, 0), (3, 1), (1, 1), (2, 0), (2, 1)]
B = 1024
D = 1024
CH = 256
G = 32
COUNT = 128
RING = 8
HALVES = B // 2 // CH
LIST = 16
GRANT = 62 * 2**20


def around(dx):
    moves = []
    for d in range(COUNT):
        core, x, rest = d % 2, (d // 2) % 4, d // RING
        moves.append((d, rest * RING + ((x + dx) % 4) * 2 + core))
    return moves


def along(steps, flip=0):
    return [(d, (d + steps) ^ flip) for d in range(COUNT) if 0 <= d + steps < COUNT]


def send(value, moves):
    return lax.ppermute(value, "dp", moves)


def unit_kernel(list_ref, count_ref, x_ref, o_ref, top_ref, low_ref, x, o, in_sem, out_sem):
    def rows(i):
        return pl.ds(i * CH, CH)

    loads = [pltpu.make_async_copy(x_ref.at[rows(i), :], x.at[rows(i), :], in_sem.at[i]) for i in range(B // CH)]
    for load in loads:
        load.start()
    lane = lax.broadcasted_iota(jnp.int32, (LIST, D), 1)
    pairs = jnp.full((LIST, D), -1.0, jnp.float32)
    for k in range(list_ref.shape[1]):
        entry = jnp.where(k < count_ref[0], list_ref[0, k], -1).astype(jnp.float32)
        pairs = jnp.where(lane == k, entry, pairs)
    o[B : B + LIST, :] = pairs.astype(jnp.bfloat16)
    stores = [pltpu.make_async_copy(o.at[pl.ds(B, LIST), :], o_ref.at[pl.ds(B, LIST), :], out_sem.at[0])]
    stores[0].start()
    for i in range(B // CH):
        loads[i].wait()
        for g in range(CH // G):
            at = slice(i * CH + g * G, i * CH + (g + 1) * G)
            v = x[at, :].astype(jnp.float32)
            size = jnp.sum(v * v, -1, keepdims=True)
            o[at, :] = (v * lax.rsqrt(size + 1e-06)).astype(jnp.bfloat16)
        stores.append(pltpu.make_async_copy(o.at[rows(i), :], o_ref.at[rows(i), :], out_sem.at[2 * i + 1]))
        half = top_ref.at[rows(i), :] if i < HALVES else low_ref.at[rows(i - HALVES), :]
        stores.append(pltpu.make_async_copy(o.at[rows(i), :], half, out_sem.at[2 * i + 2]))
        stores[-2].start()
        stores[-1].start()
    for store in stores:
        store.wait()


def normalize(embeddings, partners, pair_count):
    bf16 = jnp.bfloat16
    smem, anywhere = pl.BlockSpec(memory_space=pltpu.SMEM), pl.BlockSpec(memory_space=pl.ANY)
    return pl.pallas_call(
        unit_kernel,
        in_specs=[smem, smem, anywhere],
        out_specs=[anywhere] * 3,
        out_shape=[
            jax.ShapeDtypeStruct((B + LIST, D), bf16),
            jax.ShapeDtypeStruct((B // 2, D), bf16),
            jax.ShapeDtypeStruct((B // 2, D), bf16),
        ],
        scratch_shapes=[
            pltpu.VMEM((B, D), bf16),
            pltpu.VMEM((B + LIST, D), bf16),
            pltpu.SemaphoreType.DMA((B // CH,)),
            pltpu.SemaphoreType.DMA((2 * (B // CH) + 1,)),
        ],
        compiler_params=pltpu.CompilerParams(vmem_limit_bytes=GRANT),
        name="unit_rows",
    )(partners, pair_count, embeddings)


def halves_kernel(a_ref, b_ref, top_ref, low_ref, buf, sem):
    n = B // 2 // CH
    moves = []
    for i in range(2 * n):
        count = CH + LIST if i == 2 * n - 1 else CH
        src = a_ref.at[pl.ds(i * CH, count), :] if i < n else b_ref.at[pl.ds(i * CH, count), :]
        dst = top_ref.at[pl.ds(i * CH, count), :] if i < n else low_ref.at[pl.ds((i - n) * CH, count), :]
        held = buf.at[pl.ds(i * CH, count), :]
        moves.append((pltpu.make_async_copy(src, held, sem.at[2 * i]), pltpu.make_async_copy(held, dst, sem.at[2 * i + 1])))
    for load, _ in moves:
        load.start()
    for load, store in moves:
        load.wait()
        store.start()
    for _, store in moves:
        store.wait()


def halves(a, b):
    bf16, anywhere = jnp.bfloat16, pl.BlockSpec(memory_space=pl.ANY)
    return pl.pallas_call(
        halves_kernel,
        in_specs=[anywhere] * 2,
        out_specs=[anywhere] * 2,
        out_shape=[jax.ShapeDtypeStruct((B // 2, D), bf16), jax.ShapeDtypeStruct((B // 2 + LIST, D), bf16)],
        scratch_shapes=[pltpu.VMEM((B + LIST, D), bf16), pltpu.SemaphoreType.DMA((2 * B // CH,))],
        compiler_params=pltpu.CompilerParams(vmem_limit_bytes=GRANT),
        name="halves",
    )(a, b)


def lanes(value, op):
    return functools.reduce(op, [value[:, q * 128 : (q + 1) * 128] for q in range(value.shape[1] // 128)])


def rows8(value, op):
    return functools.reduce(op, [value[q * 8 : (q + 1) * 8, :] for q in range(value.shape[0] // 8)])


def fold(m, s, f, axis):
    top = jnp.max(m, axis, keepdims=True)
    plain = jnp.sum(f, axis, keepdims=True)
    top = jnp.maximum(top, jnp.where(plain > 0.0, 0.0, FLOOR))
    total = jnp.sum(s * jnp.exp2(m - top), axis, keepdims=True)
    total = total + plain * jnp.exp2(jnp.minimum(-top, 0.0))
    return jnp.maximum(top + jnp.log2(total), FLOOR)


def log2_add(a, b):
    top = jnp.maximum(a, b)
    return top + jnp.log2(jnp.exp2(a - top) + jnp.exp2(b - top))


def stage_kernel(plan, live, *refs):
    nl, nr, lefts, rights, widths, nrow, ncol, own_first, last = plan
    prevs, refs = refs[:2], refs[2:]
    blocks, refs = refs[: len(lefts) + len(rights)], refs[len(lefts) + len(rights) :]
    outs, refs = refs[:-SCRATCH], refs[-SCRATCH:]
    row_out, col_out = refs[-2:] if last else outs
    (lbuf, rbuf, sc, row_t, col_t, chk, row_f, row_m, row_s, col_f, col_m, col_s, waited, lsem, rsem) = refs[:-2]

    def copies(side, slot):
        pieces = lefts if side == 0 else rights
        base = 0 if side == 0 else len(lefts)
        buf, sem = (lbuf, lsem) if side == 0 else (rbuf, rsem)
        made = []
        for i, (s, row, count) in enumerate(pieces):
            if s == slot:
                made.append(
                    pltpu.make_async_copy(
                        blocks[base + i].at[pl.ds(0, count), :], buf.at[slot, pl.ds(row, count), :], sem.at[slot]
                    )
                )
        return made

    def used(flags):
        return functools.reduce(jnp.logical_or, [f > 0 for f in flags])

    need_l = [used([live[q * nr + r] for r in range(nr)]) for q in range(nl)]
    need_r = [used([live[q * nr + r] for q in range(nl)]) for r in range(nr)]
    for r in range(nr):
        waited[r] = 0

        @pl.when(need_r[r])
        def _(r=r):
            for c in copies(1, r):
                c.start()

    for q in range(nl):

        @pl.when(need_l[q])
        def _(q=q):
            for c in copies(0, q):
                c.start()

    col_f[...] = jnp.zeros_like(col_f)
    col_s[...] = jnp.zeros_like(col_s)
    col_m[...] = jnp.full_like(col_m, FLOOR)

    def pair(q, r, width, diag):
        def dot(i):
            sc[i * CH : (i + 1) * CH, :width] = lax.dot_general(
                lbuf[q, i * CH : (i + 1) * CH, :],
                rbuf[r, :width, :],
                (((1,), (1,)), ((), ())),
                preferred_element_type=jnp.float32,
            )

        def sums(i):
            cols = jnp.zeros((8, width), jnp.float32)
            size = jnp.zeros((8, 128), jnp.float32)
            for g in range(CH // G):
                at = i * CH + g * G
                v = sc[at : at + G, :width]
                if diag:
                    r_at = lax.broadcasted_iota(jnp.int32, (G, width), 0) + at
                    c_at = lax.broadcasted_iota(jnp.int32, (G, width), 1)
                    eye = r_at == c_at
                    absv = jnp.where(eye, 0.0, jnp.abs(v))
                    v = jnp.where(eye, MASKED, v)
                    sc[at : at + G, :width] = v
                else:
                    absv = jnp.abs(v)
                e = jnp.exp2(v * GAIN)
                row_t[at : at + G, :] = lanes(e, jnp.add)
                if not diag:
                    cols = cols + rows8(e, jnp.add)
                size = jnp.maximum(size, rows8(lanes(absv, jnp.maximum), jnp.maximum))
            if not diag:
                col_t[:, :width] = cols if i == 0 else col_t[:, :width] + cols
            chk[...] = size if i == 0 else jnp.maximum(chk[...], size)

        n = B // CH
        dot(0)
        for i in range(n):
            if i + 1 < n:
                dot(i + 1)
            sums(i)
        plain = jnp.max(chk[...]) <= PLAIN

        @pl.when(plain)
        def _():
            row_f[...] += row_t[...]
            if not diag:
                col_f[r, :, :width] += col_t[:, :width]

        @pl.when(jnp.logical_not(plain))
        def _():
            def group(g, _):
                at = pl.multiple_of(g * G, G)
                w = sc[pl.ds(at, G), :width] * GAIN
                old = row_m[pl.ds(at, G), :]
                top = jnp.maximum(old, lanes(w, jnp.maximum))
                total = row_s[pl.ds(at, G), :] * jnp.exp2(old - top)
                for k in range(width // 128):
                    total = total + jnp.exp2(w[:, k * 128 : (k + 1) * 128] - top)
                row_m[pl.ds(at, G), :] = top
                row_s[pl.ds(at, G), :] = total
                if not diag:
                    old = col_m[r, :, :width]
                    top = jnp.maximum(old, rows8(w, jnp.maximum))
                    total = col_s[r, :, :width] * jnp.exp2(old - top)
                    for k in range(G // 8):
                        total = total + jnp.exp2(w[k * 8 : (k + 1) * 8, :] - top)
                    col_m[r, :, :width] = top
                    col_s[r, :, :width] = total
                return 0

            lax.fori_loop(0, B // G, group, 0)

    def arrive(r):
        @pl.when(waited[r] == 0)
        def _():
            for s in range(nr):

                @pl.when(r == s)
                def _(s=s):
                    for c in copies(1, s):
                        c.wait()

            waited[r] = 1

    def runs():
        start = 0
        for r in range(1, nr + 1):
            if r == nr or widths[r] != widths[start]:
                yield start, r, widths[start]
                start = r

    def left(q, _):
        needed = functools.reduce(jnp.logical_or, [live[q * nr + r] > 0 for r in range(nr)])
        row_out[pl.ds(q, 1), :] = jnp.full((1, B), FLOOR, jnp.float32)

        @pl.when(needed)
        def _():
            row_f[...] = jnp.zeros_like(row_f)
            row_s[...] = jnp.zeros_like(row_s)
            row_m[...] = jnp.full_like(row_m, FLOOR)
            for s in range(nl):

                @pl.when(q == s)
                def _(s=s):
                    for c in copies(0, s):
                        c.wait()

            if own_first:

                @pl.when(q == 0)
                def _():
                    arrive(0)
                    pair(0, 0, B, True)

            for start, stop, width in runs():

                def step(r, _, width=width):
                    go = live[q * nr + r] > 0
                    if own_first:
                        go = jnp.logical_and(go, q + r > 0)

                    @pl.when(go)
                    def _():
                        arrive(r)
                        pair(q, r, width, False)

                    return 0

                lax.fori_loop(start, stop, step, 0)
            row_out[pl.ds(q, 1), :] = fold(row_m[...].T, row_s[...].T, row_f[...].T, 0)

        return 0

    lax.fori_loop(0, nl, left, 0)
    for q in range(nrow):
        row_out[q : q + 1, :] = log2_add(row_out[q : q + 1, :], prevs[0][q : q + 1, :])
    for r in range(nr):
        col_out[r : r + 1, :] = jnp.full((1, B), FLOOR, jnp.float32)

        @pl.when(need_r[r])
        def _(r=r):
            col_out[r : r + 1, :] = fold(col_m[r], col_s[r], col_f[r], 0)

        if r < ncol:
            col_out[r : r + 1, :] = log2_add(col_out[r : r + 1, :], prevs[1][r : r + 1, :])

    if last:
        ring_out, next_out, after_out = outs
        chip, core = live[nl * nr], live[nl * nr + 1]
        for q in range(nl):
            at = (chip + PLACES[q][0]) % 4 * 2 + (core + PLACES[q][1]) % 2
            row = row_out[q : q + 1, :]
            ring_out[at] = row if q else log2_add(row, col_out[0:1, :])
        next_out[...] = col_out[1:2, :]
        after_out[:, : B // 2] = col_out[3:4, : B // 2]
        after_out[:, B // 2 :] = col_out[2:3, : B // 2]


def stage(name, live, lefts, rights, row_prev=None, col_prev=None, own_first=False, last=False):
    nl, nr = len(lefts), len(rights)
    flat, tables = [], []
    for side in (lefts, rights):
        table = []
        for slot, pieces in enumerate(side):
            for array, row, count in pieces:
                flat.append(array)
                table.append((slot, row, count))
        tables.append(tuple(table))
    widths = tuple(sum(piece[2] for piece in pieces) for pieces in rights)
    prevs = [jnp.zeros((1, B), jnp.float32) if p is None else p for p in (row_prev, col_prev)]
    nrow, ncol = (0 if p is None else p.shape[0] for p in (row_prev, col_prev))
    plan = (nl, nr, tables[0], tables[1], widths, nrow, ncol, own_first, last)
    f32 = jnp.float32
    shapes = [(RING, 1, B), (1, B), (1, B)] if last else [(nl, B), (nr, B)]
    shapes = [jax.ShapeDtypeStruct(shape, f32) for shape in shapes]
    return pl.pallas_call(
        functools.partial(stage_kernel, plan),
        out_shape=shapes,
        in_specs=[pl.BlockSpec(memory_space=pltpu.SMEM)]
        + [pl.BlockSpec(memory_space=pltpu.VMEM)] * 2
        + [pl.BlockSpec(memory_space=pl.ANY)] * len(flat),
        out_specs=[pl.BlockSpec(memory_space=pltpu.VMEM)] * len(shapes),
        scratch_shapes=[
            pltpu.VMEM((nl, B, D), jnp.bfloat16),
            pltpu.VMEM((nr, B, D), jnp.bfloat16),
            pltpu.VMEM((B, B), f32),
            pltpu.VMEM((B, 128), f32),
            pltpu.VMEM((8, B), f32),
            pltpu.VMEM((8, 128), f32),
            pltpu.VMEM((B, 128), f32),
            pltpu.VMEM((B, 128), f32),
            pltpu.VMEM((B, 128), f32),
            pltpu.VMEM((nr, 8, B), f32),
            pltpu.VMEM((nr, 8, B), f32),
            pltpu.VMEM((nr, 8, B), f32),
            pltpu.SMEM((nr,), jnp.int32),
            pltpu.SemaphoreType.DMA((nl,)),
            pltpu.SemaphoreType.DMA((nr,)),
            pltpu.VMEM((nl, B), f32),
            pltpu.VMEM((nr, B), f32),
        ],
        compiler_params=pltpu.CompilerParams(vmem_limit_bytes=GRANT),
        cost_estimate=pl.CostEstimate(
            flops=2 * B * B * D * max(1, nl * nr // 4), bytes_accessed=2 * B * D * (nl + nr), transcendentals=0
        ),
        name=name,
    )(live, *prevs, *flat)


def last_kernel(row_ref, ring_ref, *refs):
    parts, o_ref = refs[:-1], refs[-1]
    row = row_ref[0]
    got = [ring_ref[k] for k in range(RING)]
    for k, part in enumerate(parts):
        got.append(jnp.where(row > k, part[...], FLOOR))
    got = jnp.concatenate(got, 0)
    best = jnp.max(got, 0, keepdims=True)
    total = jnp.sum(jnp.exp2(got - best), 0, keepdims=True)
    o_ref[...] = (best + jnp.log2(total)) * (LN2 / SCALE)


def body(embeddings, partners, pair_count):
    unit, top, low = normalize(embeddings, partners, pair_count)
    me = lax.axis_index("dp")
    column = me % RING
    half = B // 2
    swap = along(0, 1)

    sib = send(unit, swap)
    a = send(unit, around(1))
    b = send(unit, around(-1))
    c = send(unit, along(-RING))
    over = [(d, d - d % 32 + (d + RING) % 32) for d in range(COUNT)]
    relay = dict(over)
    mid = send(low, over)

    targets = me + RING * jnp.array([0, 1, 2, 2], jnp.int32)

    def pairs_of(*arrays):
        lists = jnp.concatenate([x[-LIST : 1 - LIST, :16] for x in arrays], 0).astype(jnp.int32)
        return jnp.any(lists[:, None, :] == targets[None, :, None], -1).astype(jnp.int32)

    def whole(array):
        return [(array, 0, B)]

    near_pairs = pairs_of(unit, sib)
    rights = [whole(unit)]
    row_0, col_0 = stage("own", near_pairs[:, 0], [whole(unit), whole(sib)], rights, own_first=True)

    mid, row_0 = lax.optimization_barrier((mid, row_0))
    d_low = send(mid, [(relay[d], d - 2 * RING) for d in range(2 * RING, COUNT)])
    a, b, c, d_low = lax.optimization_barrier((a, b, c, d_low))

    a_top, b_low = halves(a, b)
    f_top = send(a_top, around(1))
    f_low = send(b_low, around(-1))
    late, _ = lax.optimization_barrier((top, a_top))
    d_top = send(late, along(-2 * RING))
    a_sib = send(a, swap)
    b_sib = send(b, swap)

    rights = [whole(unit), whole(c), [(d_low, 0, half)]]
    live = jnp.concatenate([near_pairs.at[:, 0].set(0), pairs_of(a, b)], 0)[:, :3]
    lefts = [whole(unit), whole(sib), whole(a), whole(b)]
    row_1, col_1 = stage("near", live.reshape(-1), lefts, rights, row_0, col_0)
    a_sib, b_sib, row_1 = lax.optimization_barrier((a_sib, b_sib, row_1))
    more = pairs_of(a_sib, b_sib)
    row_2, col_2 = stage("mid", more[:, :3].reshape(-1), [whole(a_sib), whole(b_sib)], rights, None, col_1)
    f_top, f_low, d_top, row_2 = lax.optimization_barrier((f_top, f_low, d_top, row_2))
    f_top_sib = send(f_top, swap)
    f_low_sib = send(f_low, swap)

    rights.append([(d_top, 0, half)])
    lefts += [whole(a_sib), whole(b_sib)]
    lefts += [[(f_top, 0, half), (f_low, half, half)], [(f_top_sib, 0, half), (f_low_sib, half, half)]]
    early = jnp.concatenate([near_pairs, pairs_of(a, b), more], 0).at[:, :3].set(0)
    live = jnp.concatenate([early, pairs_of(f_low, f_low_sib)], 0)
    place = jnp.stack([column // 2, column % 2]).astype(jnp.int32)
    live = jnp.concatenate([live.reshape(-1), place])
    row_prev = jnp.concatenate([row_1, row_2], 0)
    ring_part, next_part, after_part = stage("far", live, lefts, rights, row_prev, col_2, last=True)

    next_got = send(next_part, along(RING))
    after_got = send(after_part, along(2 * RING))
    groups = [[r * RING + k for k in range(RING)] for r in range(COUNT // RING)]
    ring_got = lax.all_to_all(ring_part, "dp", 0, 0, axis_index_groups=groups, tiled=True)
    out = pl.pallas_call(
        last_kernel,
        in_specs=[pl.BlockSpec(memory_space=pltpu.SMEM)] + [pl.BlockSpec(memory_space=pltpu.VMEM)] * 3,
        out_shape=jax.ShapeDtypeStruct((1, B), jnp.float32),
        name="last_sum",
    )((me // RING)[None].astype(jnp.int32), ring_got, next_got, after_got)
    return out.reshape(B)


def solution(mesh):
    placed = (P("dp", None), P("dp", None), P("dp"))
    return jax.shard_map(body, mesh=mesh, in_specs=placed, out_specs=P("dp"), check_vma=False)
```

```python
import functools

import jax
import jax.numpy as jnp
from jax import lax
from jax.experimental import pallas as pl
from jax.experimental.pallas import tpu as pltpu
from jax.sharding import PartitionSpec as P

SCALE = 256.0
LOG2E = 1.4426950408889634
LN2 = 0.6931471805599453
GAIN = SCALE * LOG2E
PLAIN = 78.0 / SCALE
FLOOR = -1e30
MASKED = -1e27
SCRATCH = 17
PLACES = [(0, 0), (0, 1), (3, 0), (1, 0), (3, 1), (1, 1), (2, 0), (2, 1)]
B = 1024
D = 1024
H = B // 2
CH = 256
G = 32
COUNT = 128
RING = 8
HALVES = B // 2 // CH
LIST = 16
GRANT = 62 * 2**20


def around(dx):
    moves = []
    for d in range(COUNT):
        core, x, rest = d % 2, (d // 2) % 4, d // RING
        moves.append((d, rest * RING + ((x + dx) % 4) * 2 + core))
    return moves


def along(steps, flip=0):
    return [(d, (d + steps) ^ flip) for d in range(COUNT) if 0 <= d + steps < COUNT]


def send(value, moves):
    return lax.ppermute(value, "dp", moves)


def unit_kernel(list_ref, count_ref, x_ref, o_ref, top_ref, low_ref, x, o, in_sem, out_sem):
    def rows(i):
        return pl.ds(i * CH, CH)

    loads = [pltpu.make_async_copy(x_ref.at[rows(i), :], x.at[rows(i), :], in_sem.at[i]) for i in range(B // CH)]
    for load in loads:
        load.start()
    lane = lax.broadcasted_iota(jnp.int32, (LIST, D), 1)
    pairs = jnp.full((LIST, D), -1.0, jnp.float32)
    for k in range(list_ref.shape[1]):
        entry = jnp.where(k < count_ref[0], list_ref[0, k], -1).astype(jnp.float32)
        pairs = jnp.where(lane == k, entry, pairs)
    o[B : B + LIST, :] = pairs.astype(jnp.bfloat16)
    stores = [pltpu.make_async_copy(o.at[pl.ds(B, LIST), :], o_ref.at[pl.ds(B, LIST), :], out_sem.at[0])]
    stores[0].start()
    for i in range(B // CH):
        loads[i].wait()
        for g in range(CH // G):
            at = slice(i * CH + g * G, i * CH + (g + 1) * G)
            v = x[at, :].astype(jnp.float32)
            size = jnp.sum(v * v, -1, keepdims=True)
            o[at, :] = (v * lax.rsqrt(size + 1e-06)).astype(jnp.bfloat16)
        stores.append(pltpu.make_async_copy(o.at[rows(i), :], o_ref.at[rows(i), :], out_sem.at[2 * i + 1]))
        half = top_ref.at[rows(i), :] if i < HALVES else low_ref.at[rows(i - HALVES), :]
        stores.append(pltpu.make_async_copy(o.at[rows(i), :], half, out_sem.at[2 * i + 2]))
        stores[-2].start()
        stores[-1].start()
    for store in stores:
        store.wait()


def normalize(embeddings, partners, pair_count):
    bf16 = jnp.bfloat16
    smem, anywhere = pl.BlockSpec(memory_space=pltpu.SMEM), pl.BlockSpec(memory_space=pl.ANY)
    return pl.pallas_call(
        unit_kernel,
        in_specs=[smem, smem, anywhere],
        out_specs=[anywhere] * 3,
        out_shape=[
            jax.ShapeDtypeStruct((B + LIST, D), bf16),
            jax.ShapeDtypeStruct((B // 2, D), bf16),
            jax.ShapeDtypeStruct((B // 2, D), bf16),
        ],
        scratch_shapes=[
            pltpu.VMEM((B, D), bf16),
            pltpu.VMEM((B + LIST, D), bf16),
            pltpu.SemaphoreType.DMA((B // CH,)),
            pltpu.SemaphoreType.DMA((2 * (B // CH) + 1,)),
        ],
        compiler_params=pltpu.CompilerParams(vmem_limit_bytes=GRANT),
        name="unit_rows",
    )(partners, pair_count, embeddings)


def halves_kernel(a_ref, b_ref, top_ref, low_ref, buf, sem):
    n = B // 2 // CH
    moves = []
    for i in range(2 * n):
        count = CH + LIST if i == 2 * n - 1 else CH
        src = a_ref.at[pl.ds(i * CH, count), :] if i < n else b_ref.at[pl.ds(i * CH, count), :]
        dst = top_ref.at[pl.ds(i * CH, count), :] if i < n else low_ref.at[pl.ds((i - n) * CH, count), :]
        held = buf.at[pl.ds(i * CH, count), :]
        moves.append((pltpu.make_async_copy(src, held, sem.at[2 * i]), pltpu.make_async_copy(held, dst, sem.at[2 * i + 1])))
    for load, _ in moves:
        load.start()
    for load, store in moves:
        load.wait()
        store.start()
    for _, store in moves:
        store.wait()


def halves(a, b):
    bf16, anywhere = jnp.bfloat16, pl.BlockSpec(memory_space=pl.ANY)
    return pl.pallas_call(
        halves_kernel,
        in_specs=[anywhere] * 2,
        out_specs=[anywhere] * 2,
        out_shape=[jax.ShapeDtypeStruct((B // 2, D), bf16), jax.ShapeDtypeStruct((B // 2 + LIST, D), bf16)],
        scratch_shapes=[pltpu.VMEM((B + LIST, D), bf16), pltpu.SemaphoreType.DMA((2 * B // CH,))],
        compiler_params=pltpu.CompilerParams(vmem_limit_bytes=GRANT),
        name="halves",
    )(a, b)


def lanes(value, op):
    return functools.reduce(op, [value[:, q * 128 : (q + 1) * 128] for q in range(value.shape[1] // 128)])


def rows8(value, op):
    return functools.reduce(op, [value[q * 8 : (q + 1) * 8, :] for q in range(value.shape[0] // 8)])


def fold(m, s, f, axis):
    top = jnp.max(m, axis, keepdims=True)
    plain = jnp.sum(f, axis, keepdims=True)
    top = jnp.maximum(top, jnp.where(plain > 0.0, 0.0, FLOOR))
    total = jnp.sum(s * jnp.exp2(m - top), axis, keepdims=True)
    total = total + plain * jnp.exp2(jnp.minimum(-top, 0.0))
    return jnp.maximum(top + jnp.log2(total), FLOOR)


def log2_add(a, b):
    top = jnp.maximum(a, b)
    return top + jnp.log2(jnp.exp2(a - top) + jnp.exp2(b - top))


def stage_kernel(plan, live, *refs):
    nl, nr, lefts, rights, widths, nrow, ncol, own_first, last = plan
    row_prev, col_prev, refs = refs[: len(nrow)], refs[len(nrow) : len(nrow) + len(ncol)], refs[len(nrow) + len(ncol) :]
    blocks, refs = refs[: len(lefts) + len(rights)], refs[len(lefts) + len(rights) :]
    outs, refs = refs[:-SCRATCH], refs[-SCRATCH:]
    row_out, col_out = refs[-2:] if last else outs
    (lbuf, rbuf, sc, row_t, col_t, chk, row_f, row_m, row_s, col_f, col_m, col_s, waited, lsem, rsem) = refs[:-2]

    def copies(side, slot):
        pieces = lefts if side == 0 else rights
        base = 0 if side == 0 else len(lefts)
        buf, sem = (lbuf, lsem) if side == 0 else (rbuf, rsem)
        made = []
        for i, (s, src, dst, count) in enumerate(pieces):
            if s == slot:
                made.append(
                    pltpu.make_async_copy(
                        blocks[base + i].at[pl.ds(src, count), :], buf.at[slot, pl.ds(dst, count), :], sem.at[slot]
                    )
                )
        return made

    def used(flags):
        return functools.reduce(jnp.logical_or, [f > 0 for f in flags])

    need_l = [used([live[q * nr + r] for r in range(nr)]) for q in range(nl)]
    need_r = [used([live[q * nr + r] for q in range(nl)]) for r in range(nr)]
    for r in range(nr):
        waited[r] = 0

        @pl.when(need_r[r])
        def _(r=r):
            for c in copies(1, r):
                c.start()

    for q in range(nl):

        @pl.when(need_l[q])
        def _(q=q):
            for c in copies(0, q):
                c.start()

    col_f[...] = jnp.zeros_like(col_f)
    col_s[...] = jnp.zeros_like(col_s)
    col_m[...] = jnp.full_like(col_m, FLOOR)

    def pair(q, r, width, diag):
        def dot(i):
            sc[i * CH : (i + 1) * CH, :width] = lax.dot_general(
                lbuf[q, i * CH : (i + 1) * CH, :],
                rbuf[r, :width, :],
                (((1,), (1,)), ((), ())),
                preferred_element_type=jnp.float32,
            )

        def sums(i):
            cols = jnp.zeros((8, width), jnp.float32)
            size = jnp.zeros((8, 128), jnp.float32)
            for g in range(CH // G):
                at = i * CH + g * G
                v = sc[at : at + G, :width]
                if diag:
                    r_at = lax.broadcasted_iota(jnp.int32, (G, width), 0) + at
                    c_at = lax.broadcasted_iota(jnp.int32, (G, width), 1)
                    eye = r_at == c_at
                    absv = jnp.where(eye, 0.0, jnp.abs(v))
                    v = jnp.where(eye, MASKED, v)
                    sc[at : at + G, :width] = v
                else:
                    absv = jnp.abs(v)
                e = jnp.exp2(v * GAIN)
                row_t[at : at + G, :] = lanes(e, jnp.add)
                if not diag:
                    cols = cols + rows8(e, jnp.add)
                size = jnp.maximum(size, rows8(lanes(absv, jnp.maximum), jnp.maximum))
            if not diag:
                col_t[:, :width] = cols if i == 0 else col_t[:, :width] + cols
            chk[...] = size if i == 0 else jnp.maximum(chk[...], size)

        n = B // CH
        dot(0)
        for i in range(n):
            if i + 1 < n:
                dot(i + 1)
            sums(i)
        plain = jnp.max(chk[...]) <= PLAIN

        @pl.when(plain)
        def _():
            row_f[...] += row_t[...]
            if not diag:
                col_f[r, :, :width] += col_t[:, :width]

        @pl.when(jnp.logical_not(plain))
        def _():
            def group(g, _):
                at = pl.multiple_of(g * G, G)
                w = sc[pl.ds(at, G), :width] * GAIN
                old = row_m[pl.ds(at, G), :]
                top = jnp.maximum(old, lanes(w, jnp.maximum))
                total = row_s[pl.ds(at, G), :] * jnp.exp2(old - top)
                for k in range(width // 128):
                    total = total + jnp.exp2(w[:, k * 128 : (k + 1) * 128] - top)
                row_m[pl.ds(at, G), :] = top
                row_s[pl.ds(at, G), :] = total
                if not diag:
                    old = col_m[r, :, :width]
                    top = jnp.maximum(old, rows8(w, jnp.maximum))
                    total = col_s[r, :, :width] * jnp.exp2(old - top)
                    for k in range(G // 8):
                        total = total + jnp.exp2(w[k * 8 : (k + 1) * 8, :] - top)
                    col_m[r, :, :width] = top
                    col_s[r, :, :width] = total
                return 0

            lax.fori_loop(0, B // G, group, 0)

    def arrive(r):
        @pl.when(waited[r] == 0)
        def _():
            for s in range(nr):

                @pl.when(r == s)
                def _(s=s):
                    for c in copies(1, s):
                        c.wait()

            waited[r] = 1

    def runs():
        start = 0
        for r in range(1, nr + 1):
            if r == nr or widths[r] != widths[start]:
                yield start, r, widths[start]
                start = r

    def left(q, _):
        needed = functools.reduce(jnp.logical_or, [live[q * nr + r] > 0 for r in range(nr)])
        row_out[pl.ds(q, 1), :] = jnp.full((1, B), FLOOR, jnp.float32)

        @pl.when(needed)
        def _():
            row_f[...] = jnp.zeros_like(row_f)
            row_s[...] = jnp.zeros_like(row_s)
            row_m[...] = jnp.full_like(row_m, FLOOR)
            for s in range(nl):

                @pl.when(q == s)
                def _(s=s):
                    for c in copies(0, s):
                        c.wait()

            if own_first:

                @pl.when(q == 0)
                def _():
                    arrive(0)
                    pair(0, 0, B, True)

            for start, stop, width in runs():

                def step(r, _, width=width):
                    go = live[q * nr + r] > 0
                    if own_first:
                        go = jnp.logical_and(go, q + r > 0)

                    @pl.when(go)
                    def _():
                        arrive(r)
                        pair(q, r, width, False)

                    return 0

                lax.fori_loop(start, stop, step, 0)
            row_out[pl.ds(q, 1), :] = fold(row_m[...].T, row_s[...].T, row_f[...].T, 0)

        return 0

    lax.fori_loop(0, nl, left, 0)
    for r in range(nr):
        col_out[r : r + 1, :] = jnp.full((1, B), FLOOR, jnp.float32)

        @pl.when(need_r[r])
        def _(r=r):
            col_out[r : r + 1, :] = fold(col_m[r], col_s[r], col_f[r], 0)

    for out, prevs in ((row_out, row_prev), (col_out, col_prev)):
        at = 0
        for prev in prevs:
            to = at + prev.shape[0]
            out[at:to, :] = log2_add(out[at:to, :], prev[...])
            at = to

    if last:
        ring_out, next_out, after_out = outs
        chip, core = live[nl * nr], live[nl * nr + 1]
        for q in range(nl):
            at = (chip + PLACES[q][0]) % 4 * 2 + (core + PLACES[q][1]) % 2
            row = row_out[q : q + 1, :]
            ring_out[at] = row if q else log2_add(row, col_out[0:1, :])
        next_out[...] = col_out[1:2, :]
        after_out[:, : B // 2] = col_out[3:4, : B // 2]
        after_out[:, B // 2 :] = col_out[2:3, : B // 2]


def stage(name, live, lefts, rights, row_prev=(), col_prev=(), own_first=False, last=False):
    nl, nr = len(lefts), len(rights)
    flat, tables = [], []
    for side in (lefts, rights):
        table = []
        for slot, pieces in enumerate(side):
            for array, src, dst, count in pieces:
                flat.append(array)
                table.append((slot, src, dst, count))
        tables.append(tuple(table))
    widths = tuple(sum(piece[3] for piece in pieces) for pieces in rights)
    nrow, ncol = tuple(p.shape[0] for p in row_prev), tuple(p.shape[0] for p in col_prev)
    plan = (nl, nr, tables[0], tables[1], widths, nrow, ncol, own_first, last)
    f32 = jnp.float32
    shapes = [(RING, 1, B), (1, B), (1, B)] if last else [(nl, B), (nr, B)]
    shapes = [jax.ShapeDtypeStruct(shape, f32) for shape in shapes]
    return pl.pallas_call(
        functools.partial(stage_kernel, plan),
        out_shape=shapes,
        in_specs=[pl.BlockSpec(memory_space=pltpu.SMEM)]
        + [pl.BlockSpec(memory_space=pltpu.VMEM)] * (len(nrow) + len(ncol))
        + [pl.BlockSpec(memory_space=pl.ANY)] * len(flat),
        out_specs=[pl.BlockSpec(memory_space=pltpu.VMEM)] * len(shapes),
        scratch_shapes=[
            pltpu.VMEM((nl, B, D), jnp.bfloat16),
            pltpu.VMEM((nr, B, D), jnp.bfloat16),
            pltpu.VMEM((B, B), f32),
            pltpu.VMEM((B, 128), f32),
            pltpu.VMEM((8, B), f32),
            pltpu.VMEM((8, 128), f32),
            pltpu.VMEM((B, 128), f32),
            pltpu.VMEM((B, 128), f32),
            pltpu.VMEM((B, 128), f32),
            pltpu.VMEM((nr, 8, B), f32),
            pltpu.VMEM((nr, 8, B), f32),
            pltpu.VMEM((nr, 8, B), f32),
            pltpu.SMEM((nr,), jnp.int32),
            pltpu.SemaphoreType.DMA((nl,)),
            pltpu.SemaphoreType.DMA((nr,)),
            pltpu.VMEM((nl, B), f32),
            pltpu.VMEM((nr, B), f32),
        ],
        compiler_params=pltpu.CompilerParams(vmem_limit_bytes=GRANT),
        cost_estimate=pl.CostEstimate(
            flops=2 * B * B * D * max(1, nl * nr // 4), bytes_accessed=2 * B * D * (nl + nr), transcendentals=0
        ),
        name=name,
    )(live, *row_prev, *col_prev, *flat)


def last_kernel(row_ref, ring_ref, *refs):
    parts, o_ref = refs[:-1], refs[-1]
    row = row_ref[0]
    got = [ring_ref[k] for k in range(RING)]
    for k, part in enumerate(parts):
        got.append(jnp.where(row > k, part[...], FLOOR))
    got = jnp.concatenate(got, 0)
    best = jnp.max(got, 0, keepdims=True)
    total = jnp.sum(jnp.exp2(got - best), 0, keepdims=True)
    o_ref[...] = (best + jnp.log2(total)) * (LN2 / SCALE)


def body(embeddings, partners, pair_count):
    unit, top, low = normalize(embeddings, partners, pair_count)
    me = lax.axis_index("dp")
    column = me % RING
    swap = along(0, 1)

    a = send(unit, around(1))
    b = send(unit, around(-1))
    c = send(unit, along(-RING))
    over, on = [], []
    for d in range(2 * RING, COUNT):
        z, y = d // 32, (d // RING) % 4
        relay = (z - (y < 2)) * 32 + (y + 1) % 4 * RING + d % RING
        over.append((d, relay))
        on.append((relay, d - 2 * RING))
    relayed = send(low, over)
    sib = send(unit, swap)

    targets = me + RING * jnp.array([0, 1, 2, 2], jnp.int32)

    def pairs_of(*arrays):
        lists = jnp.concatenate([x[-LIST : 1 - LIST, :16] for x in arrays], 0).astype(jnp.int32)
        return jnp.any(lists[:, None, :] == targets[None, :, None], -1).astype(jnp.int32)

    def whole(array):
        return [(array, 0, 0, B)]

    rights = [whole(unit)]
    row_0, _ = stage("own", jnp.ones((1,), jnp.int32), rights, rights, own_first=True)
    relayed, sib, row_0 = lax.optimization_barrier((relayed, sib, row_0))
    d_low = send(relayed, on)
    sib_pairs = pairs_of(sib)
    row_1, col_1 = stage("sibling", sib_pairs[0, :1], [whole(sib)], rights)
    a, b, c, d_low, row_1 = lax.optimization_barrier((a, b, c, d_low, row_1))

    a_top, b_low = halves(a, b)
    f_top = send(a_top, around(1))
    f_low = send(b_low, around(-1))
    top, a, b, a_top = lax.optimization_barrier((top, a, b, a_top))
    d_top = send(top, along(-2 * RING))
    a_sib = send(a, swap)
    b_sib = send(b, swap)

    rights = rights + [whole(c), [(d_low, 0, 0, H)]]
    early = jnp.concatenate([pairs_of(unit), sib_pairs, pairs_of(a, b)], 0)
    live = early.at[:2, :1].set(0)[:, :3]
    lefts = [whole(unit), whole(sib), whole(a), whole(b)]
    row_2, col_2 = stage("near", live.reshape(-1), lefts, rights, [row_0, row_1], [col_1])
    a_sib, b_sib, row_2 = lax.optimization_barrier((a_sib, b_sib, row_2))
    more = pairs_of(a_sib, b_sib)
    row_3, col_3 = stage("mid", more[:, :3].reshape(-1), [whole(a_sib), whole(b_sib)], rights, [], [col_2])
    f_top, f_low, d_top, row_3 = lax.optimization_barrier((f_top, f_low, d_top, row_3))
    f_top_sib = send(f_top, swap)
    f_low_sib = send(f_low, swap)

    rights = rights + [[(d_top, 0, 0, H)]]
    lefts = lefts + [whole(a_sib), whole(b_sib)]
    lefts = lefts + [[(f_top, 0, 0, H), (f_low, 0, H, H)], [(f_top_sib, 0, 0, H), (f_low_sib, 0, H, H)]]
    early = jnp.concatenate([early, more], 0).at[:, :3].set(0)
    live = jnp.concatenate([early, pairs_of(f_low, f_low_sib)], 0)
    place = jnp.stack([column // 2, column % 2]).astype(jnp.int32)
    live = jnp.concatenate([live.reshape(-1), place])
    ring_part, next_part, after_part = stage("far", live, lefts, rights, [row_2, row_3], [col_3], last=True)

    next_got = send(next_part, along(RING))
    after_got = send(after_part, along(2 * RING))
    groups = [[r * RING + k for k in range(RING)] for r in range(COUNT // RING)]
    ring_got = lax.all_to_all(ring_part, "dp", 0, 0, axis_index_groups=groups, tiled=True)
    out = pl.pallas_call(
        last_kernel,
        in_specs=[pl.BlockSpec(memory_space=pltpu.SMEM)] + [pl.BlockSpec(memory_space=pltpu.VMEM)] * 3,
        out_shape=jax.ShapeDtypeStruct((1, B), jnp.float32),
        name="last_sum",
    )((me // RING)[None].astype(jnp.int32), ring_got, next_got, after_got)
    return out.reshape(B)


def solution(mesh):
    placed = (P("dp", None), P("dp", None), P("dp"))
    return jax.shard_map(body, mesh=mesh, in_specs=placed, out_specs=P("dp"), check_vma=False)
```

```python
import functools

import jax
import jax.numpy as jnp
from jax import lax
from jax.experimental import pallas as pl
from jax.experimental.pallas import tpu as pltpu
from jax.sharding import PartitionSpec as P

SCALE = 256.0
LOG2E = 1.4426950408889634
LN2 = 0.6931471805599453
GAIN = SCALE * LOG2E
LEAST = 2.0**-60
MOST = 2.0**112
FLOOR = -1e30
MASKED = -1e27
SCRATCH = 18
PLACES = [(0, 0), (0, 1), (3, 0), (1, 0), (3, 1), (1, 1), (2, 0), (2, 1)]
B = 1024
D = 1024
H = B // 2
CH = 256
G = 32
COUNT = 128
RING = 8
HALVES = B // 2 // CH
LIST = 16
GRANT = 63 * 2**20 + 2**19


def around(dx):
    moves = []
    for d in range(COUNT):
        core, x, rest = d % 2, (d // 2) % 4, d // RING
        moves.append((d, rest * RING + ((x + dx) % 4) * 2 + core))
    return moves


def along(steps, flip=0):
    return [(d, (d + steps) ^ flip) for d in range(COUNT) if 0 <= d + steps < COUNT]


def send(value, moves):
    return lax.ppermute(value, "dp", moves)


def unit_kernel(list_ref, count_ref, x_ref, o_ref, top_ref, low_ref, x, o, in_sem, out_sem):
    def rows(i):
        return pl.ds(i * CH, CH)

    loads = [pltpu.make_async_copy(x_ref.at[rows(i), :], x.at[rows(i), :], in_sem.at[i]) for i in range(B // CH)]
    for load in loads:
        load.start()
    lane = lax.broadcasted_iota(jnp.int32, (LIST, D), 1)
    pairs = jnp.full((LIST, D), -1.0, jnp.float32)
    for k in range(list_ref.shape[1]):
        entry = jnp.where(k < count_ref[0], list_ref[0, k], -1).astype(jnp.float32)
        pairs = jnp.where(lane == k, entry, pairs)
    o[B : B + LIST, :] = pairs.astype(jnp.bfloat16)
    stores = [
        pltpu.make_async_copy(o.at[pl.ds(B, LIST), :], o_ref.at[pl.ds(B, LIST), :], out_sem.at[0]),
        pltpu.make_async_copy(o.at[pl.ds(B, LIST), :], low_ref.at[pl.ds(H, LIST), :], out_sem.at[2 * (B // CH) + 1]),
    ]
    stores[0].start()
    stores[1].start()
    for i in range(B // CH):
        loads[i].wait()
        for g in range(CH // G):
            at = slice(i * CH + g * G, i * CH + (g + 1) * G)
            v = x[at, :].astype(jnp.float32)
            size = jnp.sum(v * v, -1, keepdims=True)
            o[at, :] = (v * lax.rsqrt(size + 1e-06)).astype(jnp.bfloat16)
        stores.append(pltpu.make_async_copy(o.at[rows(i), :], o_ref.at[rows(i), :], out_sem.at[2 * i + 1]))
        half = top_ref.at[rows(i), :] if i < HALVES else low_ref.at[rows(i - HALVES), :]
        stores.append(pltpu.make_async_copy(o.at[rows(i), :], half, out_sem.at[2 * i + 2]))
        stores[-2].start()
        stores[-1].start()
    for store in stores:
        store.wait()


def normalize(embeddings, partners, pair_count):
    bf16 = jnp.bfloat16
    smem, anywhere = pl.BlockSpec(memory_space=pltpu.SMEM), pl.BlockSpec(memory_space=pl.ANY)
    return pl.pallas_call(
        unit_kernel,
        in_specs=[smem, smem, anywhere],
        out_specs=[anywhere] * 3,
        out_shape=[
            jax.ShapeDtypeStruct((B + LIST, D), bf16),
            jax.ShapeDtypeStruct((H, D), bf16),
            jax.ShapeDtypeStruct((H + LIST, D), bf16),
        ],
        scratch_shapes=[
            pltpu.VMEM((B, D), bf16),
            pltpu.VMEM((B + LIST, D), bf16),
            pltpu.SemaphoreType.DMA((B // CH,)),
            pltpu.SemaphoreType.DMA((2 * (B // CH) + 2,)),
        ],
        compiler_params=pltpu.CompilerParams(vmem_limit_bytes=GRANT),
        name="unit_rows",
    )(partners, pair_count, embeddings)


def lanes(value, op):
    return functools.reduce(op, [value[:, q * 128 : (q + 1) * 128] for q in range(value.shape[1] // 128)])


def rows8(value, op):
    return functools.reduce(op, [value[q * 8 : (q + 1) * 8, :] for q in range(value.shape[0] // 8)])


def fold(m, s, f, axis):
    top = jnp.max(m, axis, keepdims=True)
    plain = jnp.sum(f, axis, keepdims=True)
    top = jnp.maximum(top, jnp.where(plain > 0.0, 0.0, FLOOR))
    total = jnp.sum(s * jnp.exp2(m - top), axis, keepdims=True)
    total = total + plain * jnp.exp2(jnp.minimum(-top, 0.0))
    return jnp.maximum(top + jnp.log2(total), FLOOR)


def log2_add(a, b):
    top = jnp.maximum(a, b)
    return top + jnp.log2(jnp.exp2(a - top) + jnp.exp2(b - top))


def stage_kernel(plan, live, *refs):
    nl, nr, lefts, rights, widths, nrow, ncol, own_first, last = plan
    row_prev, col_prev, refs = refs[: len(nrow)], refs[len(nrow) : len(nrow) + len(ncol)], refs[len(nrow) + len(ncol) :]
    blocks, refs = refs[: len(lefts) + len(rights)], refs[len(lefts) + len(rights) :]
    outs, refs = refs[:-SCRATCH], refs[-SCRATCH:]
    row_out, col_out = refs[-2:] if last else outs
    (lbuf, rbuf, sc, row_t, col_t, chk, row_f, row_m, row_s, col_f, col_m, col_s, waited, shifted, lsem, rsem) = refs[:-2]

    def copies(side, slot):
        pieces = lefts if side == 0 else rights
        base = 0 if side == 0 else len(lefts)
        buf, sem = (lbuf, lsem) if side == 0 else (rbuf, rsem)
        made = []
        for i, (s, src, dst, count) in enumerate(pieces):
            if s == slot:
                made.append(
                    pltpu.make_async_copy(
                        blocks[base + i].at[pl.ds(src, count), :], buf.at[slot, pl.ds(dst, count), :], sem.at[slot]
                    )
                )
        return made

    def used(flags):
        return functools.reduce(jnp.logical_or, [f > 0 for f in flags])

    need_l = [used([live[q * nr + r] for r in range(nr)]) for q in range(nl)]
    need_r = [used([live[q * nr + r] for q in range(nl)]) for r in range(nr)]
    for r in range(nr):
        waited[r] = 0

        @pl.when(need_r[r])
        def _(r=r):
            for c in copies(1, r):
                c.start()

    for q in range(nl):

        @pl.when(need_l[q])
        def _(q=q):
            for c in copies(0, q):
                c.start()

    col_f[...] = jnp.zeros_like(col_f)
    col_s[...] = jnp.zeros_like(col_s)
    col_m[...] = jnp.full_like(col_m, FLOOR)

    def pair(q, r, width, diag):
        def dot(i):
            sc[i * CH : (i + 1) * CH, :width] = lax.dot_general(
                lbuf[q, i * CH : (i + 1) * CH, :],
                rbuf[r, :width, :],
                (((1,), (1,)), ((), ())),
                preferred_element_type=jnp.float32,
            )

        def sums(i):
            cols = jnp.zeros((8, width), jnp.float32)
            most = jnp.zeros((8, 128), jnp.float32)
            least = jnp.full((8, 128), MOST, jnp.float32)
            for g in range(CH // G):
                at = i * CH + g * G
                v = sc[at : at + G, :width]
                if diag:
                    r_at = lax.broadcasted_iota(jnp.int32, (G, width), 0) + at
                    c_at = lax.broadcasted_iota(jnp.int32, (G, width), 1)
                    eye = r_at == c_at
                    v = jnp.where(eye, MASKED, v)
                    sc[at : at + G, :width] = v
                e = jnp.exp2(v * GAIN)
                part = lanes(e, jnp.add)
                row_t[at : at + G, :] = part
                if not diag:
                    cols = cols + rows8(e, jnp.add)
                most = jnp.maximum(most, rows8(part, jnp.maximum))
                least = jnp.minimum(least, rows8(part, jnp.minimum))
            if not diag:
                if i:
                    cols = col_t[:, :width] + cols
                col_t[:, :width] = cols
                if i == B // CH - 1:
                    least = jnp.minimum(least, lanes(cols, jnp.minimum))
            if i:
                most, least = jnp.maximum(chk[0], most), jnp.minimum(chk[1], least)
            chk[0], chk[1] = most, least

        n = B // CH
        dot(0)
        for i in range(n):
            if i + 1 < n:
                dot(i + 1)
            sums(i)
        safe = jnp.logical_and(chk[0] <= MOST, chk[1] >= LEAST)
        plain = jnp.max(jnp.where(safe, 0.0, 1.0)) == 0.0

        @pl.when(plain)
        def _():
            row_f[...] += row_t[...]
            if not diag:
                col_f[r, :, :width] += col_t[:, :width]

        @pl.when(jnp.logical_not(plain))
        def _():
            @pl.when(shifted[0] == 0)
            def _():
                row_s[...] = jnp.zeros_like(row_s)
                row_m[...] = jnp.full_like(row_m, FLOOR)
                shifted[0] = 1

            def group(g, _):
                at = pl.multiple_of(g * G, G)
                w = sc[pl.ds(at, G), :width] * GAIN
                old = row_m[pl.ds(at, G), :]
                top = jnp.maximum(old, lanes(w, jnp.maximum))
                total = row_s[pl.ds(at, G), :] * jnp.exp2(old - top)
                for k in range(width // 128):
                    total = total + jnp.exp2(w[:, k * 128 : (k + 1) * 128] - top)
                row_m[pl.ds(at, G), :] = top
                row_s[pl.ds(at, G), :] = total
                if not diag:
                    old = col_m[r, :, :width]
                    top = jnp.maximum(old, rows8(w, jnp.maximum))
                    total = col_s[r, :, :width] * jnp.exp2(old - top)
                    for k in range(G // 8):
                        total = total + jnp.exp2(w[k * 8 : (k + 1) * 8, :] - top)
                    col_m[r, :, :width] = top
                    col_s[r, :, :width] = total
                return 0

            lax.fori_loop(0, B // G, group, 0)

    def arrive(r):
        @pl.when(waited[r] == 0)
        def _():
            for s in range(nr):

                @pl.when(r == s)
                def _(s=s):
                    for c in copies(1, s):
                        c.wait()

            waited[r] = 1

    def runs():
        start = 0
        for r in range(1, nr + 1):
            if r == nr or widths[r] != widths[start]:
                yield start, r, widths[start]
                start = r

    def left(q, _):
        needed = functools.reduce(jnp.logical_or, [live[q * nr + r] > 0 for r in range(nr)])
        row_out[pl.ds(q, 1), :] = jnp.full((1, B), FLOOR, jnp.float32)

        @pl.when(needed)
        def _():
            row_f[...] = jnp.zeros_like(row_f)
            shifted[0] = 0
            for s in range(nl):

                @pl.when(q == s)
                def _(s=s):
                    for c in copies(0, s):
                        c.wait()

            if own_first:

                @pl.when(q == 0)
                def _():
                    arrive(0)
                    pair(0, 0, B, True)

            for start, stop, width in runs():

                def step(r, _, width=width):
                    go = live[q * nr + r] > 0
                    if own_first:
                        go = jnp.logical_and(go, q + r > 0)

                    @pl.when(go)
                    def _():
                        arrive(r)
                        pair(q, r, width, False)

                    return 0

                lax.fori_loop(start, stop, step, 0)

            @pl.when(shifted[0] == 0)
            def _():
                row_out[pl.ds(q, 1), :] = jnp.log2(jnp.sum(row_f[...].T, 0, keepdims=True))

            @pl.when(shifted[0] > 0)
            def _():
                row_out[pl.ds(q, 1), :] = fold(row_m[...].T, row_s[...].T, row_f[...].T, 0)

        return 0

    lax.fori_loop(0, nl, left, 0)
    for r in range(nr):
        col_out[r : r + 1, :] = jnp.full((1, B), FLOOR, jnp.float32)

        @pl.when(need_r[r])
        def _(r=r):
            col_out[r : r + 1, :] = fold(col_m[r], col_s[r], col_f[r], 0)

    for out, prevs in ((row_out, row_prev), (col_out, col_prev)):
        at = 0
        for prev in prevs:
            to = at + prev.shape[0]
            out[at:to, :] = log2_add(out[at:to, :], prev[...])
            at = to

    if last:
        ring_out, next_out, after_out = outs
        chip, core = live[nl * nr], live[nl * nr + 1]
        for q in range(nl):
            at = (chip + PLACES[q][0]) % 4 * 2 + (core + PLACES[q][1]) % 2
            row = row_out[q : q + 1, :]
            ring_out[at] = row if q else log2_add(row, col_out[0:1, :])
        next_out[...] = col_out[1:2, :]
        after_out[:, : B // 2] = col_out[3:4, : B // 2]
        after_out[:, B // 2 :] = col_out[2:3, : B // 2]


def stage(name, live, lefts, rights, row_prev=(), col_prev=(), own_first=False, last=False):
    nl, nr = len(lefts), len(rights)
    flat, tables = [], []
    for side in (lefts, rights):
        table = []
        for slot, pieces in enumerate(side):
            for array, src, dst, count in pieces:
                flat.append(array)
                table.append((slot, src, dst, count))
        tables.append(tuple(table))
    widths = tuple(sum(piece[3] for piece in pieces) for pieces in rights)
    nrow, ncol = tuple(p.shape[0] for p in row_prev), tuple(p.shape[0] for p in col_prev)
    plan = (nl, nr, tables[0], tables[1], widths, nrow, ncol, own_first, last)
    cost = 2 * B * B * D * 4 if own_first else B
    f32 = jnp.float32
    shapes = [(RING, 1, B), (1, B), (1, B)] if last else [(nl, B), (nr, B)]
    shapes = [jax.ShapeDtypeStruct(shape, f32) for shape in shapes]
    return pl.pallas_call(
        functools.partial(stage_kernel, plan),
        out_shape=shapes,
        in_specs=[pl.BlockSpec(memory_space=pltpu.SMEM)]
        + [pl.BlockSpec(memory_space=pltpu.VMEM)] * (len(nrow) + len(ncol))
        + [pl.BlockSpec(memory_space=pl.ANY)] * len(flat),
        out_specs=[pl.BlockSpec(memory_space=pltpu.VMEM)] * len(shapes),
        scratch_shapes=[
            pltpu.VMEM((nl, B, D), jnp.bfloat16),
            pltpu.VMEM((nr, B, D), jnp.bfloat16),
            pltpu.VMEM((B, B), f32),
            pltpu.VMEM((B, 128), f32),
            pltpu.VMEM((8, B), f32),
            pltpu.VMEM((2, 8, 128), f32),
            pltpu.VMEM((B, 128), f32),
            pltpu.VMEM((B, 128), f32),
            pltpu.VMEM((B, 128), f32),
            pltpu.VMEM((nr, 8, B), f32),
            pltpu.VMEM((nr, 8, B), f32),
            pltpu.VMEM((nr, 8, B), f32),
            pltpu.SMEM((nr,), jnp.int32),
            pltpu.SMEM((1,), jnp.int32),
            pltpu.SemaphoreType.DMA((nl,)),
            pltpu.SemaphoreType.DMA((nr,)),
            pltpu.VMEM((nl, B), f32),
            pltpu.VMEM((nr, B), f32),
        ],
        compiler_params=pltpu.CompilerParams(vmem_limit_bytes=GRANT),
        cost_estimate=pl.CostEstimate(
            flops=cost, bytes_accessed=B, transcendentals=0
        ),
        name=name,
    )(live, *row_prev, *col_prev, *flat)


def last_kernel(row_ref, ring_ref, *refs):
    parts, o_ref = refs[:-1], refs[-1]
    row = row_ref[0]
    got = [ring_ref[k] for k in range(RING)]
    for k, part in enumerate(parts):
        got.append(jnp.where(row > k, part[...], FLOOR))
    got = jnp.concatenate(got, 0)
    best = jnp.max(got, 0, keepdims=True)
    total = jnp.sum(jnp.exp2(got - best), 0, keepdims=True)
    o_ref[...] = (best + jnp.log2(total)) * (LN2 / SCALE)


def body(embeddings, partners, pair_count):
    unit, top, low = normalize(embeddings, partners, pair_count)
    me = lax.axis_index("dp")
    column = me % RING
    swap = along(0, 1)
    together = lax.optimization_barrier

    over, on = [], []
    for d in range(2 * RING, COUNT):
        z, y = d // 32, (d // RING) % 4
        relay = (z - (y < 2)) * 32 + (y + 1) % 4 * RING + d % RING
        over.append((d, relay))
        on.append((relay, d - 2 * RING))

    targets = me + RING * jnp.array([0, 1, 2, 2], jnp.int32)

    def pairs_of(*arrays):
        lists = jnp.concatenate([x[-LIST : 1 - LIST, :16] for x in arrays], 0).astype(jnp.int32)
        return jnp.any(lists[:, None, :] == targets[None, :, None], -1).astype(jnp.int32)

    def whole(array):
        return [(array, 0, 0, B)]

    def joined(upper, lower):
        return [(upper, 0, 0, H), (lower, 0, H, H)]

    a_top = send(top, around(1))
    b_low = send(low, around(-1))
    c_top = send(top, along(-RING))
    relayed = send(low, over)
    sib = send(unit, swap)
    first_pairs = pairs_of(unit, sib)
    lefts = [whole(unit), whole(sib)]
    row_0, col_0 = stage("own", first_pairs[:, 0], lefts, [whole(unit)], own_first=True)

    a_top, b_low, c_top, relayed, row_0 = together((a_top, b_low, c_top, relayed, row_0))
    top, low, _ = together((top, low, c_top))
    a_low = send(low, around(1))
    b_top = send(top, around(-1))
    c_low = send(low, along(-RING))
    d_low = send(relayed, on)
    a_top_sib = send(a_top, swap)

    a_low, a_top_sib = together((a_low, a_top_sib))
    a_top, b_low, a_low = together((a_top, b_low, a_low))
    f_top = send(a_top, around(1))
    a_low_sib = send(a_low, swap)
    b_low_sib = send(b_low, swap)
    b_low, b_top, a_low = together((b_low, b_top, a_low))
    f_low = send(b_low, around(-1))
    b_top_sib = send(b_top, swap)
    c_low, d_low, a_low, b_top = together((c_low, d_low, a_low, b_top))
    top, _ = together((top, c_low))
    d_top = send(top, along(-2 * RING))

    rights = [whole(unit), joined(c_top, c_low), [(d_low, 0, 0, H)]]
    lefts += [joined(a_top, a_low), joined(b_top, b_low)]
    lefts += [joined(a_top_sib, a_low_sib), joined(b_top_sib, b_low_sib)]
    near_pairs = jnp.concatenate([first_pairs, pairs_of(a_low, b_low, a_low_sib, b_low_sib)], 0)
    live = near_pairs.at[:2, :1].set(0)[:, :3]
    row_2, col_2 = stage("near", live.reshape(-1), lefts, rights, [row_0], [col_0])
    f_top, f_low, d_top, row_2 = together((f_top, f_low, d_top, row_2))
    f_top_sib = send(f_top, swap)
    f_low_sib = send(f_low, swap)

    rights = rights + [[(d_top, 0, 0, H)]]
    lefts = lefts + [joined(f_top, f_low), joined(f_top_sib, f_low_sib)]
    live = jnp.concatenate([near_pairs.at[:, :3].set(0), pairs_of(f_low, f_low_sib)], 0)
    place = jnp.stack([column // 2, column % 2]).astype(jnp.int32)
    live = jnp.concatenate([live.reshape(-1), place])
    ring_part, next_part, after_part = stage("far", live, lefts, rights, [row_2], [col_2], last=True)

    next_got = send(next_part, along(RING))
    after_got = send(after_part, along(2 * RING))
    groups = [[r * RING + k for k in range(RING)] for r in range(COUNT // RING)]
    ring_got = lax.all_to_all(ring_part, "dp", 0, 0, axis_index_groups=groups, tiled=True)
    out = pl.pallas_call(
        last_kernel,
        in_specs=[pl.BlockSpec(memory_space=pltpu.SMEM)] + [pl.BlockSpec(memory_space=pltpu.VMEM)] * 3,
        out_shape=jax.ShapeDtypeStruct((1, B), jnp.float32),
        name="last_sum",
    )((me // RING)[None].astype(jnp.int32), ring_got, next_got, after_got)
    return out.reshape(B)


def solution(mesh):
    placed = (P("dp", None), P("dp", None), P("dp"))
    return jax.shard_map(body, mesh=mesh, in_specs=placed, out_specs=P("dp"), check_vma=False)
```

```python
import functools

import jax
import jax.numpy as jnp
from jax import lax
from jax.experimental import pallas as pl
from jax.experimental.pallas import tpu as pltpu
from jax.sharding import PartitionSpec as P

SCALE = 256.0
LOG2E = 1.4426950408889634
LN2 = 0.6931471805599453
GAIN = SCALE * LOG2E
LEAST = 2.0**-60
MOST = 2.0**112
FLOOR = -1e30
MASKED = -1e27
SCRATCH = 18
PLACES = [(0, 0), (0, 1), (3, 0), (1, 0), (3, 1), (1, 1), (2, 0), (2, 1)]
B = 1024
D = 1024
H = B // 2
CH = 256
G = 32
COUNT = 128
RING = 8
HALVES = B // 2 // CH
LIST = 16
GRANT = 63 * 2**20 + 2**19


def around(dx):
    moves = []
    for d in range(COUNT):
        core, x, rest = d % 2, (d // 2) % 4, d // RING
        moves.append((d, rest * RING + ((x + dx) % 4) * 2 + core))
    return moves


def along(steps, flip=0):
    return [(d, (d + steps) ^ flip) for d in range(COUNT) if 0 <= d + steps < COUNT]


def send(value, moves):
    return lax.ppermute(value, "dp", moves)


def unit_kernel(list_ref, count_ref, x_ref, o_ref, top_ref, low_ref, x, o, in_sem, out_sem):
    def rows(i):
        return pl.ds(i * CH, CH)

    loads = [pltpu.make_async_copy(x_ref.at[rows(i), :], x.at[rows(i), :], in_sem.at[i]) for i in range(B // CH)]
    for load in loads:
        load.start()
    lane = lax.broadcasted_iota(jnp.int32, (LIST, D), 1)
    pairs = jnp.full((LIST, D), -1.0, jnp.float32)
    for k in range(list_ref.shape[1]):
        entry = jnp.where(k < count_ref[0], list_ref[0, k], -1).astype(jnp.float32)
        pairs = jnp.where(lane == k, entry, pairs)
    o[B : B + LIST, :] = pairs.astype(jnp.bfloat16)
    stores = [pltpu.make_async_copy(o.at[pl.ds(B, LIST), :], o_ref.at[pl.ds(B, LIST), :], out_sem.at[0])]
    stores[0].start()
    for i in range(B // CH):
        loads[i].wait()
        for g in range(CH // G):
            at = slice(i * CH + g * G, i * CH + (g + 1) * G)
            v = x[at, :].astype(jnp.float32)
            size = jnp.sum(v * v, -1, keepdims=True)
            o[at, :] = (v * lax.rsqrt(size + 1e-06)).astype(jnp.bfloat16)
        stores.append(pltpu.make_async_copy(o.at[rows(i), :], o_ref.at[rows(i), :], out_sem.at[2 * i + 1]))
        half = top_ref.at[rows(i), :] if i < HALVES else low_ref.at[rows(i - HALVES), :]
        stores.append(pltpu.make_async_copy(o.at[rows(i), :], half, out_sem.at[2 * i + 2]))
        stores[-2].start()
        stores[-1].start()
    for store in stores:
        store.wait()


def normalize(embeddings, partners, pair_count):
    bf16 = jnp.bfloat16
    smem, anywhere = pl.BlockSpec(memory_space=pltpu.SMEM), pl.BlockSpec(memory_space=pl.ANY)
    return pl.pallas_call(
        unit_kernel,
        in_specs=[smem, smem, anywhere],
        out_specs=[anywhere] * 3,
        out_shape=[
            jax.ShapeDtypeStruct((B + LIST, D), bf16),
            jax.ShapeDtypeStruct((B // 2, D), bf16),
            jax.ShapeDtypeStruct((B // 2, D), bf16),
        ],
        scratch_shapes=[
            pltpu.VMEM((B, D), bf16),
            pltpu.VMEM((B + LIST, D), bf16),
            pltpu.SemaphoreType.DMA((B // CH,)),
            pltpu.SemaphoreType.DMA((2 * (B // CH) + 1,)),
        ],
        compiler_params=pltpu.CompilerParams(vmem_limit_bytes=GRANT),
        name="unit_rows",
    )(partners, pair_count, embeddings)


def halves_kernel(a_ref, b_ref, top_ref, low_ref, buf, sem):
    n = B // 2 // CH
    moves = []
    for i in range(2 * n):
        count = CH + LIST if i == 2 * n - 1 else CH
        src = a_ref.at[pl.ds(i * CH, count), :] if i < n else b_ref.at[pl.ds(i * CH, count), :]
        dst = top_ref.at[pl.ds(i * CH, count), :] if i < n else low_ref.at[pl.ds((i - n) * CH, count), :]
        held = buf.at[pl.ds(i * CH, count), :]
        moves.append((pltpu.make_async_copy(src, held, sem.at[2 * i]), pltpu.make_async_copy(held, dst, sem.at[2 * i + 1])))
    for load, _ in moves:
        load.start()
    for load, store in moves:
        load.wait()
        store.start()
    for _, store in moves:
        store.wait()


def halves(a, b):
    bf16, anywhere = jnp.bfloat16, pl.BlockSpec(memory_space=pl.ANY)
    return pl.pallas_call(
        halves_kernel,
        in_specs=[anywhere] * 2,
        out_specs=[anywhere] * 2,
        out_shape=[jax.ShapeDtypeStruct((B // 2, D), bf16), jax.ShapeDtypeStruct((B // 2 + LIST, D), bf16)],
        scratch_shapes=[pltpu.VMEM((B + LIST, D), bf16), pltpu.SemaphoreType.DMA((2 * B // CH,))],
        compiler_params=pltpu.CompilerParams(vmem_limit_bytes=GRANT),
        name="halves",
    )(a, b)


def lanes(value, op):
    return functools.reduce(op, [value[:, q * 128 : (q + 1) * 128] for q in range(value.shape[1] // 128)])


def rows8(value, op):
    return functools.reduce(op, [value[q * 8 : (q + 1) * 8, :] for q in range(value.shape[0] // 8)])


def fold(m, s, f, axis):
    top = jnp.max(m, axis, keepdims=True)
    plain = jnp.sum(f, axis, keepdims=True)
    top = jnp.maximum(top, jnp.where(plain > 0.0, 0.0, FLOOR))
    total = jnp.sum(s * jnp.exp2(m - top), axis, keepdims=True)
    total = total + plain * jnp.exp2(jnp.minimum(-top, 0.0))
    return jnp.maximum(top + jnp.log2(total), FLOOR)


def log2_add(a, b):
    top = jnp.maximum(a, b)
    return top + jnp.log2(jnp.exp2(a - top) + jnp.exp2(b - top))


def stage_kernel(plan, live, *refs):
    nl, nr, lefts, rights, widths, nrow, ncol, own_first, last = plan
    row_prev, col_prev, refs = refs[: len(nrow)], refs[len(nrow) : len(nrow) + len(ncol)], refs[len(nrow) + len(ncol) :]
    blocks, refs = refs[: len(lefts) + len(rights)], refs[len(lefts) + len(rights) :]
    outs, refs = refs[:-SCRATCH], refs[-SCRATCH:]
    row_out, col_out = refs[-2:] if last else outs
    (lbuf, rbuf, sc, row_t, col_t, chk, row_f, row_m, row_s, col_f, col_m, col_s, waited, shifted, lsem, rsem) = refs[:-2]

    def copies(side, slot):
        pieces = lefts if side == 0 else rights
        base = 0 if side == 0 else len(lefts)
        buf, sem = (lbuf, lsem) if side == 0 else (rbuf, rsem)
        made = []
        for i, (s, src, dst, count) in enumerate(pieces):
            if s == slot:
                made.append(
                    pltpu.make_async_copy(
                        blocks[base + i].at[pl.ds(src, count), :], buf.at[slot, pl.ds(dst, count), :], sem.at[slot]
                    )
                )
        return made

    def used(flags):
        return functools.reduce(jnp.logical_or, [f > 0 for f in flags])

    need_l = [used([live[q * nr + r] for r in range(nr)]) for q in range(nl)]
    need_r = [used([live[q * nr + r] for q in range(nl)]) for r in range(nr)]
    for r in range(nr):
        waited[r] = 0

        @pl.when(need_r[r])
        def _(r=r):
            for c in copies(1, r):
                c.start()

    for q in range(nl):

        @pl.when(need_l[q])
        def _(q=q):
            for c in copies(0, q):
                c.start()

    col_f[...] = jnp.zeros_like(col_f)
    col_s[...] = jnp.zeros_like(col_s)
    col_m[...] = jnp.full_like(col_m, FLOOR)

    def pair(q, r, width, diag):
        def dot(i):
            sc[i * CH : (i + 1) * CH, :width] = lax.dot_general(
                lbuf[q, i * CH : (i + 1) * CH, :],
                rbuf[r, :width, :],
                (((1,), (1,)), ((), ())),
                preferred_element_type=jnp.float32,
            )

        def sums(i):
            cols = jnp.zeros((8, width), jnp.float32)
            most = jnp.zeros((8, 128), jnp.float32)
            least = jnp.full((8, 128), MOST, jnp.float32)
            for g in range(CH // G):
                at = i * CH + g * G
                v = sc[at : at + G, :width]
                if diag:
                    r_at = lax.broadcasted_iota(jnp.int32, (G, width), 0) + at
                    c_at = lax.broadcasted_iota(jnp.int32, (G, width), 1)
                    eye = r_at == c_at
                    v = jnp.where(eye, MASKED, v)
                    sc[at : at + G, :width] = v
                e = jnp.exp2(v * GAIN)
                part = lanes(e, jnp.add)
                row_t[at : at + G, :] = part
                if not diag:
                    cols = cols + rows8(e, jnp.add)
                most = jnp.maximum(most, rows8(part, jnp.maximum))
                least = jnp.minimum(least, rows8(part, jnp.minimum))
            if not diag:
                if i:
                    cols = col_t[:, :width] + cols
                col_t[:, :width] = cols
                if i == B // CH - 1:
                    least = jnp.minimum(least, lanes(cols, jnp.minimum))
            if i:
                most, least = jnp.maximum(chk[0], most), jnp.minimum(chk[1], least)
            chk[0], chk[1] = most, least

        n = B // CH
        dot(0)
        for i in range(n):
            if i + 1 < n:
                dot(i + 1)
            sums(i)
        safe = jnp.logical_and(chk[0] <= MOST, chk[1] >= LEAST)
        plain = jnp.max(jnp.where(safe, 0.0, 1.0)) == 0.0

        @pl.when(plain)
        def _():
            row_f[...] += row_t[...]
            if not diag:
                col_f[r, :, :width] += col_t[:, :width]

        @pl.when(jnp.logical_not(plain))
        def _():
            @pl.when(shifted[0] == 0)
            def _():
                row_s[...] = jnp.zeros_like(row_s)
                row_m[...] = jnp.full_like(row_m, FLOOR)
                shifted[0] = 1

            def group(g, _):
                at = pl.multiple_of(g * G, G)
                w = sc[pl.ds(at, G), :width] * GAIN
                old = row_m[pl.ds(at, G), :]
                top = jnp.maximum(old, lanes(w, jnp.maximum))
                total = row_s[pl.ds(at, G), :] * jnp.exp2(old - top)
                for k in range(width // 128):
                    total = total + jnp.exp2(w[:, k * 128 : (k + 1) * 128] - top)
                row_m[pl.ds(at, G), :] = top
                row_s[pl.ds(at, G), :] = total
                if not diag:
                    old = col_m[r, :, :width]
                    top = jnp.maximum(old, rows8(w, jnp.maximum))
                    total = col_s[r, :, :width] * jnp.exp2(old - top)
                    for k in range(G // 8):
                        total = total + jnp.exp2(w[k * 8 : (k + 1) * 8, :] - top)
                    col_m[r, :, :width] = top
                    col_s[r, :, :width] = total
                return 0

            lax.fori_loop(0, B // G, group, 0)

    def arrive(r):
        @pl.when(waited[r] == 0)
        def _():
            for s in range(nr):

                @pl.when(r == s)
                def _(s=s):
                    for c in copies(1, s):
                        c.wait()

            waited[r] = 1

    def runs():
        start = 0
        for r in range(1, nr + 1):
            if r == nr or widths[r] != widths[start]:
                yield start, r, widths[start]
                start = r

    def left(q, _):
        needed = functools.reduce(jnp.logical_or, [live[q * nr + r] > 0 for r in range(nr)])
        row_out[pl.ds(q, 1), :] = jnp.full((1, B), FLOOR, jnp.float32)

        @pl.when(needed)
        def _():
            row_f[...] = jnp.zeros_like(row_f)
            shifted[0] = 0
            for s in range(nl):

                @pl.when(q == s)
                def _(s=s):
                    for c in copies(0, s):
                        c.wait()

            if own_first:

                @pl.when(q == 0)
                def _():
                    arrive(0)
                    pair(0, 0, B, True)

            for start, stop, width in runs():

                def step(r, _, width=width):
                    go = live[q * nr + r] > 0
                    if own_first:
                        go = jnp.logical_and(go, q + r > 0)

                    @pl.when(go)
                    def _():
                        arrive(r)
                        pair(q, r, width, False)

                    return 0

                lax.fori_loop(start, stop, step, 0)

            @pl.when(shifted[0] == 0)
            def _():
                row_out[pl.ds(q, 1), :] = jnp.log2(jnp.sum(row_f[...].T, 0, keepdims=True))

            @pl.when(shifted[0] > 0)
            def _():
                row_out[pl.ds(q, 1), :] = fold(row_m[...].T, row_s[...].T, row_f[...].T, 0)

        return 0

    lax.fori_loop(0, nl, left, 0)
    for r in range(nr):
        col_out[r : r + 1, :] = jnp.full((1, B), FLOOR, jnp.float32)

        @pl.when(need_r[r])
        def _(r=r):
            col_out[r : r + 1, :] = fold(col_m[r], col_s[r], col_f[r], 0)

    for out, prevs in ((row_out, () if last else row_prev), (col_out, col_prev)):
        at = 0
        for prev in prevs:
            to = at + prev.shape[0]
            out[at:to, :] = log2_add(out[at:to, :], prev[...])
            at = to

    if last:
        ring_out, next_out, after_out = outs
        chip, core = live[nl * nr], live[nl * nr + 1]
        for q in range(RING):
            at = (chip + PLACES[q][0]) % 4 * 2 + (core + PLACES[q][1]) % 2
            row = row_out[0:1, :] if q == RING - 1 else row_prev[0][q : q + 1, :]
            ring_out[at] = row if q else log2_add(row, col_out[0:1, :])
        next_out[...] = col_out[1:2, :]
        after_out[:, : B // 2] = col_out[3:4, : B // 2]
        after_out[:, B // 2 :] = col_out[2:3, : B // 2]


def stage(name, live, lefts, rights, row_prev=(), col_prev=(), own_first=False, last=False):
    nl, nr = len(lefts), len(rights)
    flat, tables = [], []
    for side in (lefts, rights):
        table = []
        for slot, pieces in enumerate(side):
            for array, src, dst, count in pieces:
                flat.append(array)
                table.append((slot, src, dst, count))
        tables.append(tuple(table))
    widths = tuple(sum(piece[3] for piece in pieces) for pieces in rights)
    nrow, ncol = tuple(p.shape[0] for p in row_prev), tuple(p.shape[0] for p in col_prev)
    plan = (nl, nr, tables[0], tables[1], widths, nrow, ncol, own_first, last)
    cost = 2 * B * B * D * 4 if own_first else B
    f32 = jnp.float32
    shapes = [(RING, 1, B), (1, B), (1, B)] if last else [(nl, B), (nr, B)]
    shapes = [jax.ShapeDtypeStruct(shape, f32) for shape in shapes]
    return pl.pallas_call(
        functools.partial(stage_kernel, plan),
        out_shape=shapes,
        in_specs=[pl.BlockSpec(memory_space=pltpu.SMEM)]
        + [pl.BlockSpec(memory_space=pltpu.VMEM)] * (len(nrow) + len(ncol))
        + [pl.BlockSpec(memory_space=pl.ANY)] * len(flat),
        out_specs=[pl.BlockSpec(memory_space=pltpu.VMEM)] * len(shapes),
        scratch_shapes=[
            pltpu.VMEM((nl, B, D), jnp.bfloat16),
            pltpu.VMEM((nr, B, D), jnp.bfloat16),
            pltpu.VMEM((B, B), f32),
            pltpu.VMEM((B, 128), f32),
            pltpu.VMEM((8, B), f32),
            pltpu.VMEM((2, 8, 128), f32),
            pltpu.VMEM((B, 128), f32),
            pltpu.VMEM((B, 128), f32),
            pltpu.VMEM((B, 128), f32),
            pltpu.VMEM((nr, 8, B), f32),
            pltpu.VMEM((nr, 8, B), f32),
            pltpu.VMEM((nr, 8, B), f32),
            pltpu.SMEM((nr,), jnp.int32),
            pltpu.SMEM((1,), jnp.int32),
            pltpu.SemaphoreType.DMA((nl,)),
            pltpu.SemaphoreType.DMA((nr,)),
            pltpu.VMEM((nl, B), f32),
            pltpu.VMEM((nr, B), f32),
        ],
        compiler_params=pltpu.CompilerParams(vmem_limit_bytes=GRANT),
        cost_estimate=pl.CostEstimate(
            flops=cost, bytes_accessed=B, transcendentals=0
        ),
        name=name,
    )(live, *row_prev, *col_prev, *flat)


def last_kernel(row_ref, ring_ref, *refs):
    parts, o_ref = refs[:-1], refs[-1]
    row = row_ref[0]
    got = [ring_ref[k] for k in range(RING)]
    for k, part in enumerate(parts):
        got.append(jnp.where(row > k, part[...], FLOOR))
    got = jnp.concatenate(got, 0)
    best = jnp.max(got, 0, keepdims=True)
    total = jnp.sum(jnp.exp2(got - best), 0, keepdims=True)
    o_ref[...] = (best + jnp.log2(total)) * (LN2 / SCALE)


def body(embeddings, partners, pair_count):
    unit, top, low = normalize(embeddings, partners, pair_count)
    me = lax.axis_index("dp")
    column = me % RING
    swap = along(0, 1)
    together = lax.optimization_barrier

    over, on = [], []
    for d in range(2 * RING, COUNT):
        z, y = d // 32, (d // RING) % 4
        relay = (z - (y < 2)) * 32 + (y + 1) % 4 * RING + d % RING
        over.append((d, relay))
        on.append((relay, d - 2 * RING))

    targets = me + RING * jnp.array([0, 1, 2, 2], jnp.int32)

    def pairs_of(*arrays):
        lists = jnp.concatenate([x[-LIST : 1 - LIST, :16] for x in arrays], 0).astype(jnp.int32)
        return jnp.any(lists[:, None, :] == targets[None, :, None], -1).astype(jnp.int32)

    def whole(array):
        return [(array, 0, 0, B)]

    a = send(unit, around(1))
    b = send(unit, around(-1))
    relayed = send(low, over)
    c = send(unit, along(-RING))
    row_0, _ = stage("own", jnp.ones((1,), jnp.int32), [whole(unit)], [whole(unit)], own_first=True)
    relayed, row_0, late = together((relayed, row_0, unit))
    d_low = send(relayed, on)
    sib = send(late, swap)
    a, b, c, d_low, sib = together((a, b, c, d_low, sib))

    a_top, b_low = halves(a, b)
    f_top = send(a_top, around(1))
    f_low = send(b_low, around(-1))
    a, b, top, a_top = together((a, b, top, a_top))
    d_top = send(top, along(-2 * RING))
    a_sib = send(a, swap)
    b_sib = send(b, swap)

    rights = [whole(unit), whole(c), [(d_low, 0, 0, H)]]
    early = pairs_of(unit, sib, a, b)
    live = early.at[:1, :1].set(0)[:, :3]
    lefts = [whole(unit), whole(sib), whole(a), whole(b)]
    row_1, col_1 = stage("near", live.reshape(-1), lefts, rights, [row_0], [])
    a_sib, b_sib, row_1 = together((a_sib, b_sib, row_1))
    more = pairs_of(a_sib, b_sib)
    row_2, col_2 = stage("mid", more[:, :3].reshape(-1), [whole(a_sib), whole(b_sib)], rights, [], [col_1])
    f_top, f_low, d_top, row_2 = together((f_top, f_low, d_top, row_2))
    f_top_sib = send(f_top, swap)
    f_low_sib = send(f_low, swap)

    rights = rights + [[(d_top, 0, 0, H)]]
    lefts = lefts + [whole(a_sib), whole(b_sib), [(f_top, 0, 0, H), (f_low, 0, H, H)]]
    early = jnp.concatenate([early, more], 0).at[:, :3].set(0)
    live = jnp.concatenate([early, pairs_of(f_low)], 0)
    row_3, col_3 = stage("far", live.reshape(-1), lefts, rights, [row_1, row_2], [col_2])
    f_low_sib, f_top_sib, row_3 = together((f_low_sib, f_top_sib, row_3))
    place = jnp.stack([column // 2, column % 2]).astype(jnp.int32)
    live = jnp.concatenate([pairs_of(f_low_sib).reshape(-1), place])
    lefts = [[(f_top_sib, 0, 0, H), (f_low_sib, 0, H, H)]]
    ring_part, next_part, after_part = stage("last", live, lefts, rights, [row_3], [col_3], last=True)

    next_got = send(next_part, along(RING))
    after_got = send(after_part, along(2 * RING))
    groups = [[r * RING + k for k in range(RING)] for r in range(COUNT // RING)]
    ring_got = lax.all_to_all(ring_part, "dp", 0, 0, axis_index_groups=groups, tiled=True)
    out = pl.pallas_call(
        last_kernel,
        in_specs=[pl.BlockSpec(memory_space=pltpu.SMEM)] + [pl.BlockSpec(memory_space=pltpu.VMEM)] * 3,
        out_shape=jax.ShapeDtypeStruct((1, B), jnp.float32),
        name="last_sum",
    )((me // RING)[None].astype(jnp.int32), ring_got, next_got, after_got)
    return out.reshape(B)


def solution(mesh):
    placed = (P("dp", None), P("dp", None), P("dp"))
    return jax.shard_map(body, mesh=mesh, in_specs=placed, out_specs=P("dp"), check_vma=False)
```

```python
import functools

import jax
import jax.numpy as jnp
from jax import lax
from jax.experimental import pallas as pl
from jax.experimental.pallas import tpu as pltpu
from jax.sharding import PartitionSpec as P

SCALE = 256.0
LOG2E = 1.4426950408889634
LN2 = 0.6931471805599453
GAIN = SCALE * LOG2E
LEAST = 2.0**-60
MOST = 2.0**112
FLOOR = -1e30
MASKED = -1e27
SCRATCH = 22
PLACES = [(0, 0), (0, 1), (3, 0), (1, 0), (3, 1), (1, 1), (2, 0), (2, 1)]
B = 1024
D = 1024
H = B // 2
CH = 256
G = 32
COUNT = 128
RING = 8
HALVES = B // 2 // CH
LIST = 16
GRANT = 63 * 2**20 + 2**19


def around(dx):
    moves = []
    for d in range(COUNT):
        core, x, rest = d % 2, (d // 2) % 4, d // RING
        moves.append((d, rest * RING + ((x + dx) % 4) * 2 + core))
    return moves


def along(steps, flip=0):
    return [(d, (d + steps) ^ flip) for d in range(COUNT) if 0 <= d + steps < COUNT]


def send(value, moves):
    return lax.ppermute(value, "dp", moves)


def unit_kernel(list_ref, count_ref, x_ref, o_ref, top_ref, low_ref, x, o, in_sem, out_sem):
    def rows(i):
        return pl.ds(i * CH, CH)

    loads = [pltpu.make_async_copy(x_ref.at[rows(i), :], x.at[rows(i), :], in_sem.at[i]) for i in range(B // CH)]
    for load in loads:
        load.start()
    lane = lax.broadcasted_iota(jnp.int32, (LIST, D), 1)
    pairs = jnp.full((LIST, D), -1.0, jnp.float32)
    for k in range(list_ref.shape[1]):
        entry = jnp.where(k < count_ref[0], list_ref[0, k], -1).astype(jnp.float32)
        pairs = jnp.where(lane == k, entry, pairs)
    o[B : B + LIST, :] = pairs.astype(jnp.bfloat16)
    stores = [pltpu.make_async_copy(o.at[pl.ds(B, LIST), :], o_ref.at[pl.ds(B, LIST), :], out_sem.at[0])]
    stores[0].start()
    for i in range(B // CH):
        loads[i].wait()
        for g in range(CH // G):
            at = slice(i * CH + g * G, i * CH + (g + 1) * G)
            v = x[at, :].astype(jnp.float32)
            size = jnp.sum(v * v, -1, keepdims=True)
            o[at, :] = (v * lax.rsqrt(size + 1e-06)).astype(jnp.bfloat16)
        stores.append(pltpu.make_async_copy(o.at[rows(i), :], o_ref.at[rows(i), :], out_sem.at[2 * i + 1]))
        half = top_ref.at[rows(i), :] if i < HALVES else low_ref.at[rows(i - HALVES), :]
        stores.append(pltpu.make_async_copy(o.at[rows(i), :], half, out_sem.at[2 * i + 2]))
        stores[-2].start()
        stores[-1].start()
    for store in stores:
        store.wait()


def normalize(embeddings, partners, pair_count):
    bf16 = jnp.bfloat16
    smem, anywhere = pl.BlockSpec(memory_space=pltpu.SMEM), pl.BlockSpec(memory_space=pl.ANY)
    return pl.pallas_call(
        unit_kernel,
        in_specs=[smem, smem, anywhere],
        out_specs=[anywhere] * 3,
        out_shape=[
            jax.ShapeDtypeStruct((B + LIST, D), bf16),
            jax.ShapeDtypeStruct((B // 2, D), bf16),
            jax.ShapeDtypeStruct((B // 2, D), bf16),
        ],
        scratch_shapes=[
            pltpu.VMEM((B, D), bf16),
            pltpu.VMEM((B + LIST, D), bf16),
            pltpu.SemaphoreType.DMA((B // CH,)),
            pltpu.SemaphoreType.DMA((2 * (B // CH) + 1,)),
        ],
        compiler_params=pltpu.CompilerParams(vmem_limit_bytes=GRANT),
        name="unit_rows",
    )(partners, pair_count, embeddings)


def halves_kernel(a_ref, b_ref, top_ref, low_ref, buf, sem):
    n = B // 2 // CH
    moves = []
    for i in range(2 * n):
        count = CH + LIST if i == 2 * n - 1 else CH
        src = a_ref.at[pl.ds(i * CH, count), :] if i < n else b_ref.at[pl.ds(i * CH, count), :]
        dst = top_ref.at[pl.ds(i * CH, count), :] if i < n else low_ref.at[pl.ds((i - n) * CH, count), :]
        held = buf.at[pl.ds(i * CH, count), :]
        moves.append((pltpu.make_async_copy(src, held, sem.at[2 * i]), pltpu.make_async_copy(held, dst, sem.at[2 * i + 1])))
    for load, _ in moves:
        load.start()
    for load, store in moves:
        load.wait()
        store.start()
    for _, store in moves:
        store.wait()


def halves(a, b):
    bf16, anywhere = jnp.bfloat16, pl.BlockSpec(memory_space=pl.ANY)
    return pl.pallas_call(
        halves_kernel,
        in_specs=[anywhere] * 2,
        out_specs=[anywhere] * 2,
        out_shape=[jax.ShapeDtypeStruct((B // 2, D), bf16), jax.ShapeDtypeStruct((B // 2 + LIST, D), bf16)],
        scratch_shapes=[pltpu.VMEM((B + LIST, D), bf16), pltpu.SemaphoreType.DMA((2 * B // CH,))],
        compiler_params=pltpu.CompilerParams(vmem_limit_bytes=GRANT),
        name="halves",
    )(a, b)


def lanes(value, op):
    return functools.reduce(op, [value[:, q * 128 : (q + 1) * 128] for q in range(value.shape[1] // 128)])


def rows8(value, op):
    return functools.reduce(op, [value[q * 8 : (q + 1) * 8, :] for q in range(value.shape[0] // 8)])


def fold(m, s, f, axis):
    top = jnp.max(m, axis, keepdims=True)
    plain = jnp.sum(f, axis, keepdims=True)
    top = jnp.maximum(top, jnp.where(plain > 0.0, 0.0, FLOOR))
    total = jnp.sum(s * jnp.exp2(m - top), axis, keepdims=True)
    total = total + plain * jnp.exp2(jnp.minimum(-top, 0.0))
    return jnp.maximum(top + jnp.log2(total), FLOOR)


def log2_add(a, b):
    top = jnp.maximum(a, b)
    return top + jnp.log2(jnp.exp2(a - top) + jnp.exp2(b - top))


def stage_kernel(plan, *refs):
    nl, nr, lefts, rights, widths, lists, wanted, nrow, ncol, own_first, last = plan
    row_prev, col_prev, refs = refs[: len(nrow)], refs[len(nrow) : len(nrow) + len(ncol)], refs[len(nrow) + len(ncol) :]
    blocks, refs = refs[: len(lefts) + len(rights)], refs[len(lefts) + len(rights) :]
    outs, refs = refs[:-SCRATCH], refs[-SCRATCH:]
    row_out, col_out = refs[-2:] if last else outs
    listed, flags, live, list_sem = refs[-6:-2]
    (lbuf, rbuf, sc, row_t, col_t, chk, row_f, row_m, row_s, col_f, col_m, col_s, waited, shifted, lsem, rsem) = refs[:-6]

    def copies(side, slot):
        pieces = lefts if side == 0 else rights
        base = 0 if side == 0 else len(lefts)
        buf, sem = (lbuf, lsem) if side == 0 else (rbuf, rsem)
        made = []
        for i, (s, src, dst, count) in enumerate(pieces):
            if s == slot:
                made.append(
                    pltpu.make_async_copy(
                        blocks[base + i].at[pl.ds(src, count), :], buf.at[slot, pl.ds(dst, count), :], sem.at[slot]
                    )
                )
        return made

    def used(flags):
        return functools.reduce(jnp.logical_or, [f > 0 for f in flags])

    me = lax.axis_index("dp")
    if own_first:
        live[0, 0] = 1
    else:
        fetched = [
            pltpu.make_async_copy(blocks[i].at[pl.ds(row, LIST), pl.ds(0, 128)], listed.at[q], list_sem.at[q])
            for q, (i, row) in enumerate(lists)
        ]
        for copy in fetched:
            copy.start()
        row_at = lax.broadcasted_iota(jnp.int32, (8, 128), 0)
        lane_at = lax.broadcasted_iota(jnp.int32, (8, 128), 1)
        found = jnp.zeros((8, 128), jnp.float32)
        for q in range(nl):
            fetched[q].wait()
            names = listed[q].astype(jnp.float32)[:8, :]
            for r in range(nr):
                if wanted[q][r]:
                    target = (me + RING * min(r, 2)).astype(jnp.float32)
                    hit = jnp.max(jnp.where(names == target, 1.0, 0.0), 1, keepdims=True)
                    found = jnp.where(jnp.logical_and(row_at == q, lane_at == r), hit, found)
        flags[...] = found.astype(jnp.int32)
        noted = pltpu.make_async_copy(flags, live, list_sem.at[nl])
        noted.start()
        noted.wait()

    need_l = [used([live[q, r] for r in range(nr)]) for q in range(nl)]
    need_r = [used([live[q, r] for q in range(nl)]) for r in range(nr)]

    def fetch(q):
        @pl.when(need_l[q])
        def _():
            for c in copies(0, q):
                c.start()

    fetch(0)
    for r in range(nr):
        waited[r] = 0

        @pl.when(need_r[r])
        def _(r=r):
            for c in copies(1, r):
                c.start()

    col_f[...] = jnp.zeros_like(col_f)
    col_s[...] = jnp.zeros_like(col_s)
    col_m[...] = jnp.full_like(col_m, FLOOR)

    def pair(q, r, width, diag):
        def dot(i):
            sc[i * CH : (i + 1) * CH, :width] = lax.dot_general(
                lbuf[q, i * CH : (i + 1) * CH, :],
                rbuf[r, :width, :],
                (((1,), (1,)), ((), ())),
                preferred_element_type=jnp.float32,
            )

        def sums(i):
            cols = jnp.zeros((8, width), jnp.float32)
            most = jnp.zeros((8, 128), jnp.float32)
            least = jnp.full((8, 128), MOST, jnp.float32)
            for g in range(CH // G):
                at = i * CH + g * G
                v = sc[at : at + G, :width]
                if diag:
                    r_at = lax.broadcasted_iota(jnp.int32, (G, width), 0) + at
                    c_at = lax.broadcasted_iota(jnp.int32, (G, width), 1)
                    eye = r_at == c_at
                    v = jnp.where(eye, MASKED, v)
                    sc[at : at + G, :width] = v
                e = jnp.exp2(v * GAIN)
                part = lanes(e, jnp.add)
                row_t[at : at + G, :] = part
                if not diag:
                    cols = cols + rows8(e, jnp.add)
                most = jnp.maximum(most, rows8(part, jnp.maximum))
                least = jnp.minimum(least, rows8(part, jnp.minimum))
            if not diag:
                if i:
                    cols = col_t[:, :width] + cols
                col_t[:, :width] = cols
                if i == B // CH - 1:
                    least = jnp.minimum(least, lanes(cols, jnp.minimum))
            if i:
                most, least = jnp.maximum(chk[0], most), jnp.minimum(chk[1], least)
            chk[0], chk[1] = most, least

        n = B // CH
        dot(0)
        for i in range(n):
            if i + 1 < n:
                dot(i + 1)
            sums(i)
        safe = jnp.logical_and(chk[0] <= MOST, chk[1] >= LEAST)
        plain = jnp.max(jnp.where(safe, 0.0, 1.0)) == 0.0

        @pl.when(plain)
        def _():
            row_f[...] += row_t[...]
            if not diag:
                col_f[r, :, :width] += col_t[:, :width]

        @pl.when(jnp.logical_not(plain))
        def _():
            @pl.when(shifted[0] == 0)
            def _():
                row_s[...] = jnp.zeros_like(row_s)
                row_m[...] = jnp.full_like(row_m, FLOOR)
                shifted[0] = 1

            def group(g, _):
                at = pl.multiple_of(g * G, G)
                w = sc[pl.ds(at, G), :width] * GAIN
                old = row_m[pl.ds(at, G), :]
                top = jnp.maximum(old, lanes(w, jnp.maximum))
                total = row_s[pl.ds(at, G), :] * jnp.exp2(old - top)
                for k in range(width // 128):
                    total = total + jnp.exp2(w[:, k * 128 : (k + 1) * 128] - top)
                row_m[pl.ds(at, G), :] = top
                row_s[pl.ds(at, G), :] = total
                if not diag:
                    old = col_m[r, :, :width]
                    top = jnp.maximum(old, rows8(w, jnp.maximum))
                    total = col_s[r, :, :width] * jnp.exp2(old - top)
                    for k in range(G // 8):
                        total = total + jnp.exp2(w[k * 8 : (k + 1) * 8, :] - top)
                    col_m[r, :, :width] = top
                    col_s[r, :, :width] = total
                return 0

            lax.fori_loop(0, B // G, group, 0)

    def arrive(r):
        @pl.when(waited[r] == 0)
        def _():
            for s in range(nr):

                @pl.when(r == s)
                def _(s=s):
                    for c in copies(1, s):
                        c.wait()

            waited[r] = 1

    def runs():
        start = 0
        for r in range(1, nr + 1):
            if r == nr or widths[r] != widths[start]:
                yield start, r, widths[start]
                start = r

    def left(q, _):
        needed = functools.reduce(jnp.logical_or, [live[q, r] > 0 for r in range(nr)])
        for s in range(1, nl):

            @pl.when(q + 1 == s)
            def _(s=s):
                fetch(s)

        row_out[pl.ds(q, 1), :] = jnp.full((1, B), FLOOR, jnp.float32)

        @pl.when(needed)
        def _():
            row_f[...] = jnp.zeros_like(row_f)
            shifted[0] = 0
            for s in range(nl):

                @pl.when(q == s)
                def _(s=s):
                    for c in copies(0, s):
                        c.wait()

            if own_first:

                @pl.when(q == 0)
                def _():
                    arrive(0)
                    pair(0, 0, B, True)

            for start, stop, width in runs():

                def step(r, _, width=width):
                    go = live[q, r] > 0
                    if own_first:
                        go = jnp.logical_and(go, q + r > 0)

                    @pl.when(go)
                    def _():
                        arrive(r)
                        pair(q, r, width, False)

                    return 0

                lax.fori_loop(start, stop, step, 0)

            @pl.when(shifted[0] == 0)
            def _():
                row_out[pl.ds(q, 1), :] = jnp.log2(jnp.sum(row_f[...].T, 0, keepdims=True))

            @pl.when(shifted[0] > 0)
            def _():
                row_out[pl.ds(q, 1), :] = fold(row_m[...].T, row_s[...].T, row_f[...].T, 0)

        return 0

    lax.fori_loop(0, nl, left, 0)
    for r in range(nr):
        col_out[r : r + 1, :] = jnp.full((1, B), FLOOR, jnp.float32)

        @pl.when(need_r[r])
        def _(r=r):
            col_out[r : r + 1, :] = fold(col_m[r], col_s[r], col_f[r], 0)

    for out, prevs in ((row_out, () if last else row_prev), (col_out, col_prev)):
        at = 0
        for prev in prevs:
            to = at + prev.shape[0]
            out[at:to, :] = log2_add(out[at:to, :], prev[...])
            at = to

    if last:
        ring_out, next_out, after_out = outs
        chip, core = me % RING // 2, me % 2
        for q in range(RING):
            at = (chip + PLACES[q][0]) % 4 * 2 + (core + PLACES[q][1]) % 2
            row = row_out[0:1, :] if q == RING - 1 else row_prev[0][q : q + 1, :]
            ring_out[at] = row if q else log2_add(row, col_out[0:1, :])
        next_out[...] = col_out[1:2, :]
        after_out[:, : B // 2] = col_out[3:4, : B // 2]
        after_out[:, B // 2 :] = col_out[2:3, : B // 2]


def stage(name, wanted, lefts, rights, row_prev=(), col_prev=(), own_first=False, last=False):
    nl, nr = len(lefts), len(rights)
    flat, tables = [], []
    for side in (lefts, rights):
        table = []
        for slot, pieces in enumerate(side):
            for array, src, dst, count in pieces:
                flat.append(array)
                table.append((slot, src, dst, count))
        tables.append(tuple(table))
    widths = tuple(sum(piece[3] for piece in pieces) for pieces in rights)
    nrow, ncol = tuple(p.shape[0] for p in row_prev), tuple(p.shape[0] for p in col_prev)
    lists, at = [], 0
    for pieces in lefts:
        at += len(pieces)
        lists.append((at - 1, pieces[-1][3]))
    plan = (nl, nr, tables[0], tables[1], widths, lists, wanted, nrow, ncol, own_first, last)
    cost = 2 * B * B * D * 4 if own_first else B
    f32 = jnp.float32
    shapes = [(RING, 1, B), (1, B), (1, B)] if last else [(nl, B), (nr, B)]
    shapes = [jax.ShapeDtypeStruct(shape, f32) for shape in shapes]
    return pl.pallas_call(
        functools.partial(stage_kernel, plan),
        out_shape=shapes,
        in_specs=[pl.BlockSpec(memory_space=pltpu.VMEM)] * (len(nrow) + len(ncol))
        + [pl.BlockSpec(memory_space=pl.ANY)] * len(flat),
        out_specs=[pl.BlockSpec(memory_space=pltpu.VMEM)] * len(shapes),
        scratch_shapes=[
            pltpu.VMEM((nl, B, D), jnp.bfloat16),
            pltpu.VMEM((nr, B, D), jnp.bfloat16),
            pltpu.VMEM((B, B), f32),
            pltpu.VMEM((B, 128), f32),
            pltpu.VMEM((8, B), f32),
            pltpu.VMEM((2, 8, 128), f32),
            pltpu.VMEM((B, 128), f32),
            pltpu.VMEM((B, 128), f32),
            pltpu.VMEM((B, 128), f32),
            pltpu.VMEM((nr, 8, B), f32),
            pltpu.VMEM((nr, 8, B), f32),
            pltpu.VMEM((nr, 8, B), f32),
            pltpu.SMEM((nr,), jnp.int32),
            pltpu.SMEM((1,), jnp.int32),
            pltpu.SemaphoreType.DMA((nl,)),
            pltpu.SemaphoreType.DMA((nr,)),
            pltpu.VMEM((nl, LIST, 128), jnp.bfloat16),
            pltpu.VMEM((8, 128), jnp.int32),
            pltpu.SMEM((8, 128), jnp.int32),
            pltpu.SemaphoreType.DMA((nl + 1,)),
            pltpu.VMEM((nl, B), f32),
            pltpu.VMEM((nr, B), f32),
        ],
        compiler_params=pltpu.CompilerParams(vmem_limit_bytes=GRANT),
        cost_estimate=pl.CostEstimate(
            flops=cost, bytes_accessed=B, transcendentals=0
        ),
        name=name,
    )(*row_prev, *col_prev, *flat)


def last_kernel(row_ref, ring_ref, *refs):
    parts, o_ref = refs[:-1], refs[-1]
    row = row_ref[0]
    got = [ring_ref[k] for k in range(RING)]
    for k, part in enumerate(parts):
        got.append(jnp.where(row > k, part[...], FLOOR))
    got = jnp.concatenate(got, 0)
    best = jnp.max(got, 0, keepdims=True)
    total = jnp.sum(jnp.exp2(got - best), 0, keepdims=True)
    o_ref[...] = (best + jnp.log2(total)) * (LN2 / SCALE)


def body(embeddings, partners, pair_count):
    unit, top, low = normalize(embeddings, partners, pair_count)
    me = lax.axis_index("dp")
    swap = along(0, 1)
    together = lax.optimization_barrier

    over, on = [], []
    for d in range(2 * RING, COUNT):
        z, y = d // 32, (d // RING) % 4
        relay = (z - (y < 2)) * 32 + (y + 1) % 4 * RING + d % RING
        over.append((d, relay))
        on.append((relay, d - 2 * RING))

    def whole(array):
        return [(array, 0, 0, B)]

    a = send(unit, around(1))
    b = send(unit, around(-1))
    relayed = send(low, over)
    c = send(unit, along(-RING))
    row_0, _ = stage("own", ((1,),), [whole(unit)], [whole(unit)], own_first=True)
    relayed, row_0, late = together((relayed, row_0, unit))
    d_low = send(relayed, on)
    sib = send(late, swap)
    a, b, c, d_low, sib = together((a, b, c, d_low, sib))

    a_top, b_low = halves(a, b)
    f_top = send(a_top, around(1))
    f_low = send(b_low, around(-1))
    a, b, top, a_top = together((a, b, top, a_top))
    d_top = send(top, along(-2 * RING))
    a_sib = send(a, swap)
    b_sib = send(b, swap)

    rights = [whole(unit), whole(c), [(d_low, 0, 0, H)]]
    lefts = [whole(unit), whole(sib), whole(a), whole(b)]
    row_1, col_1 = stage("near", ((0, 1, 1),) + ((1, 1, 1),) * 3, lefts, rights, [row_0], [])
    a_sib, b_sib, row_1 = together((a_sib, b_sib, row_1))
    row_2, col_2 = stage("mid", ((1, 1, 1),) * 2, [whole(a_sib), whole(b_sib)], rights, [], [col_1])
    f_top, f_low, d_top, row_2 = together((f_top, f_low, d_top, row_2))
    f_top_sib = send(f_top, swap)
    f_low_sib = send(f_low, swap)

    rights = rights + [[(d_top, 0, 0, H)]]
    lefts = lefts + [whole(a_sib), whole(b_sib), [(f_top, 0, 0, H), (f_low, 0, H, H)]]
    wanted = ((0, 0, 0, 1),) * 6 + ((1, 1, 1, 1),)
    row_3, col_3 = stage("far", wanted, lefts, rights, [row_1, row_2], [col_2])
    f_low_sib, f_top_sib, row_3 = together((f_low_sib, f_top_sib, row_3))
    lefts = [[(f_top_sib, 0, 0, H), (f_low_sib, 0, H, H)]]
    ring_part, next_part, after_part = stage("last", ((1, 1, 1, 1),), lefts, rights, [row_3], [col_3], last=True)

    next_got = send(next_part, along(RING))
    after_got = send(after_part, along(2 * RING))
    groups = [[r * RING + k for k in range(RING)] for r in range(COUNT // RING)]
    ring_got = lax.all_to_all(ring_part, "dp", 0, 0, axis_index_groups=groups, tiled=True)
    out = pl.pallas_call(
        last_kernel,
        in_specs=[pl.BlockSpec(memory_space=pltpu.SMEM)] + [pl.BlockSpec(memory_space=pltpu.VMEM)] * 3,
        out_shape=jax.ShapeDtypeStruct((1, B), jnp.float32),
        name="last_sum",
    )((me // RING)[None].astype(jnp.int32), ring_got, next_got, after_got)
    return out.reshape(B)


def solution(mesh):
    placed = (P("dp", None), P("dp", None), P("dp"))
    return jax.shard_map(body, mesh=mesh, in_specs=placed, out_specs=P("dp"), check_vma=False)
```

```python
import functools

import jax
import jax.numpy as jnp
from jax import lax
from jax.experimental import pallas as pl
from jax.experimental.pallas import tpu as pltpu
from jax.sharding import PartitionSpec as P

SCALE = 256.0
LOG2E = 1.4426950408889634
LN2 = 0.6931471805599453
GAIN = SCALE * LOG2E
LEAST = 2.0**-60
MOST = 2.0**112
FLOOR = -1e30
MASKED = -1e27
SCRATCH = 22
PLACES = [(0, 0), (0, 1), (3, 0), (1, 0), (3, 1), (1, 1), (2, 0), (2, 1)]
B = 1024
D = 1024
H = B // 2
CH = 256
G = 32
COUNT = 128
RING = 8
HALVES = B // 2 // CH
LIST = 16
GRANT = 63 * 2**20 + 2**19


def around(dx):
    moves = []
    for d in range(COUNT):
        core, x, rest = d % 2, (d // 2) % 4, d // RING
        moves.append((d, rest * RING + ((x + dx) % 4) * 2 + core))
    return moves


def along(steps, flip=0):
    return [(d, (d + steps) ^ flip) for d in range(COUNT) if 0 <= d + steps < COUNT]


def send(value, moves):
    return lax.ppermute(value, "dp", moves)


def unit_kernel(list_ref, count_ref, x_ref, o_ref, top_ref, low_ref, x, o, in_sem, out_sem):
    def rows(i):
        return pl.ds(i * CH, CH)

    loads = [pltpu.make_async_copy(x_ref.at[rows(i), :], x.at[rows(i), :], in_sem.at[i]) for i in range(B // CH)]
    for load in loads:
        load.start()
    lane = lax.broadcasted_iota(jnp.int32, (LIST, D), 1)
    pairs = jnp.full((LIST, D), -1.0, jnp.float32)
    for k in range(list_ref.shape[1]):
        entry = jnp.where(k < count_ref[0], list_ref[0, k], -1).astype(jnp.float32)
        pairs = jnp.where(lane == k, entry, pairs)
    o[B : B + LIST, :] = pairs.astype(jnp.bfloat16)
    stores = [pltpu.make_async_copy(o.at[pl.ds(B, LIST), :], o_ref.at[pl.ds(B, LIST), :], out_sem.at[0])]
    stores[0].start()
    for i in range(B // CH):
        loads[i].wait()
        for g in range(CH // G):
            at = slice(i * CH + g * G, i * CH + (g + 1) * G)
            v = x[at, :].astype(jnp.float32)
            size = jnp.sum(v * v, -1, keepdims=True)
            o[at, :] = (v * lax.rsqrt(size + 1e-06)).astype(jnp.bfloat16)
        stores.append(pltpu.make_async_copy(o.at[rows(i), :], o_ref.at[rows(i), :], out_sem.at[2 * i + 1]))
        half = top_ref.at[rows(i), :] if i < HALVES else low_ref.at[rows(i - HALVES), :]
        stores.append(pltpu.make_async_copy(o.at[rows(i), :], half, out_sem.at[2 * i + 2]))
        stores[-2].start()
        stores[-1].start()
    for store in stores:
        store.wait()


def normalize(embeddings, partners, pair_count):
    bf16 = jnp.bfloat16
    smem, anywhere = pl.BlockSpec(memory_space=pltpu.SMEM), pl.BlockSpec(memory_space=pl.ANY)
    return pl.pallas_call(
        unit_kernel,
        in_specs=[smem, smem, anywhere],
        out_specs=[anywhere] * 3,
        out_shape=[
            jax.ShapeDtypeStruct((B + LIST, D), bf16),
            jax.ShapeDtypeStruct((B // 2, D), bf16),
            jax.ShapeDtypeStruct((B // 2, D), bf16),
        ],
        scratch_shapes=[
            pltpu.VMEM((B, D), bf16),
            pltpu.VMEM((B + LIST, D), bf16),
            pltpu.SemaphoreType.DMA((B // CH,)),
            pltpu.SemaphoreType.DMA((2 * (B // CH) + 1,)),
        ],
        compiler_params=pltpu.CompilerParams(vmem_limit_bytes=GRANT),
        name="unit_rows",
    )(partners, pair_count, embeddings)


def halves_kernel(a_ref, b_ref, top_ref, low_ref, buf, sem):
    n = B // 2 // CH
    moves = []
    for i in range(2 * n):
        count = CH + LIST if i == 2 * n - 1 else CH
        src = a_ref.at[pl.ds(i * CH, count), :] if i < n else b_ref.at[pl.ds(i * CH, count), :]
        dst = top_ref.at[pl.ds(i * CH, count), :] if i < n else low_ref.at[pl.ds((i - n) * CH, count), :]
        held = buf.at[pl.ds(i * CH, count), :]
        moves.append((pltpu.make_async_copy(src, held, sem.at[2 * i]), pltpu.make_async_copy(held, dst, sem.at[2 * i + 1])))
    for load, _ in moves:
        load.start()
    for load, store in moves:
        load.wait()
        store.start()
    for _, store in moves:
        store.wait()


def halves(a, b):
    bf16, anywhere = jnp.bfloat16, pl.BlockSpec(memory_space=pl.ANY)
    return pl.pallas_call(
        halves_kernel,
        in_specs=[anywhere] * 2,
        out_specs=[anywhere] * 2,
        out_shape=[jax.ShapeDtypeStruct((B // 2, D), bf16), jax.ShapeDtypeStruct((B // 2 + LIST, D), bf16)],
        scratch_shapes=[pltpu.VMEM((B + LIST, D), bf16), pltpu.SemaphoreType.DMA((2 * B // CH,))],
        compiler_params=pltpu.CompilerParams(vmem_limit_bytes=GRANT),
        name="halves",
    )(a, b)


def lanes(value, op):
    return functools.reduce(op, [value[:, q * 128 : (q + 1) * 128] for q in range(value.shape[1] // 128)])


def rows8(value, op):
    return functools.reduce(op, [value[q * 8 : (q + 1) * 8, :] for q in range(value.shape[0] // 8)])


def fold(m, s, f, axis):
    top = jnp.max(m, axis, keepdims=True)
    plain = jnp.sum(f, axis, keepdims=True)
    top = jnp.maximum(top, jnp.where(plain > 0.0, 0.0, FLOOR))
    total = jnp.sum(s * jnp.exp2(m - top), axis, keepdims=True)
    total = total + plain * jnp.exp2(jnp.minimum(-top, 0.0))
    return jnp.maximum(top + jnp.log2(total), FLOOR)


def log2_add(a, b):
    top = jnp.maximum(a, b)
    return top + jnp.log2(jnp.exp2(a - top) + jnp.exp2(b - top))


def stage_kernel(plan, *refs):
    nl, nr, lefts, rights, widths, lists, wanted, nrow, ncol, own_first, last = plan
    row_prev, col_prev, refs = refs[: len(nrow)], refs[len(nrow) : len(nrow) + len(ncol)], refs[len(nrow) + len(ncol) :]
    blocks, refs = refs[: len(lefts) + len(rights)], refs[len(lefts) + len(rights) :]
    outs, refs = refs[:-SCRATCH], refs[-SCRATCH:]
    row_out, col_out = refs[-2:] if last else outs
    listed, flags, live, list_sem = refs[-6:-2]
    (lbuf, rbuf, sc, row_t, col_t, chk, row_f, row_m, row_s, col_f, col_m, col_s, waited, shifted, lsem, rsem) = refs[:-6]

    def copies(side, slot):
        pieces = lefts if side == 0 else rights
        base = 0 if side == 0 else len(lefts)
        buf, sem = (lbuf, lsem) if side == 0 else (rbuf, rsem)
        made = []
        for i, (s, src, dst, count) in enumerate(pieces):
            if s == slot:
                made.append(
                    pltpu.make_async_copy(
                        blocks[base + i].at[pl.ds(src, count), :], buf.at[slot, pl.ds(dst, count), :], sem.at[slot]
                    )
                )
        return made

    def used(flags):
        return functools.reduce(jnp.logical_or, [f > 0 for f in flags])

    me = lax.axis_index("dp")
    if own_first:
        live[0, 0] = 1
    else:
        fetched = [
            pltpu.make_async_copy(blocks[i].at[pl.ds(row, LIST), pl.ds(0, 128)], listed.at[q], list_sem.at[q])
            for q, (i, row) in enumerate(lists)
        ]
        for copy in fetched:
            copy.start()
        row_at = lax.broadcasted_iota(jnp.int32, (8, 128), 0)
        lane_at = lax.broadcasted_iota(jnp.int32, (8, 128), 1)
        found = jnp.zeros((8, 128), jnp.float32)
        for q in range(nl):
            fetched[q].wait()
            names = listed[q].astype(jnp.float32)[:8, :]
            for r in range(nr):
                if wanted[q][r]:
                    target = (me + RING * min(r, 2)).astype(jnp.float32)
                    hit = jnp.max(jnp.where(names == target, 1.0, 0.0), 1, keepdims=True)
                    found = jnp.where(jnp.logical_and(row_at == q, lane_at == r), hit, found)
        flags[...] = found.astype(jnp.int32)
        noted = pltpu.make_async_copy(flags, live, list_sem.at[nl])
        noted.start()
        noted.wait()

    need_l = [used([live[q, r] for r in range(nr)]) for q in range(nl)]
    need_r = [used([live[q, r] for q in range(nl)]) for r in range(nr)]

    def fetch(q):
        @pl.when(need_l[q])
        def _():
            for c in copies(0, q):
                c.start()

    fetch(0)
    for r in range(nr):
        waited[r] = 0

        @pl.when(need_r[r])
        def _(r=r):
            for c in copies(1, r):
                c.start()

    col_f[...] = jnp.zeros_like(col_f)
    col_s[...] = jnp.zeros_like(col_s)
    col_m[...] = jnp.full_like(col_m, FLOOR)

    def pair(q, r, width, diag):
        def dot(i):
            sc[i * CH : (i + 1) * CH, :width] = lax.dot_general(
                lbuf[q, i * CH : (i + 1) * CH, :],
                rbuf[r, :width, :],
                (((1,), (1,)), ((), ())),
                preferred_element_type=jnp.float32,
            )

        def sums(i):
            cols = jnp.zeros((8, width), jnp.float32)
            most = jnp.zeros((8, 128), jnp.float32)
            least = jnp.full((8, 128), MOST, jnp.float32)
            for g in range(CH // G):
                at = i * CH + g * G
                v = sc[at : at + G, :width]
                if diag:
                    r_at = lax.broadcasted_iota(jnp.int32, (G, width), 0) + at
                    c_at = lax.broadcasted_iota(jnp.int32, (G, width), 1)
                    eye = r_at == c_at
                    v = jnp.where(eye, MASKED, v)
                    sc[at : at + G, :width] = v
                e = jnp.exp2(v * GAIN)
                part = lanes(e, jnp.add)
                row_t[at : at + G, :] = part
                if not diag:
                    cols = cols + rows8(e, jnp.add)
                most = jnp.maximum(most, rows8(part, jnp.maximum))
                least = jnp.minimum(least, rows8(part, jnp.minimum))
            if not diag:
                if i:
                    cols = col_t[:, :width] + cols
                col_t[:, :width] = cols
                if i == B // CH - 1:
                    least = jnp.minimum(least, lanes(cols, jnp.minimum))
            if i:
                most, least = jnp.maximum(chk[0], most), jnp.minimum(chk[1], least)
            chk[0], chk[1] = most, least

        n = B // CH
        dot(0)
        for i in range(n):
            if i + 1 < n:
                dot(i + 1)
            sums(i)
        safe = jnp.logical_and(chk[0] <= MOST, chk[1] >= LEAST)
        plain = jnp.max(jnp.where(safe, 0.0, 1.0)) == 0.0

        @pl.when(plain)
        def _():
            row_f[...] += row_t[...]
            if not diag:
                col_f[r, :, :width] += col_t[:, :width]

        @pl.when(jnp.logical_not(plain))
        def _():
            @pl.when(shifted[0] == 0)
            def _():
                row_s[...] = jnp.zeros_like(row_s)
                row_m[...] = jnp.full_like(row_m, FLOOR)
                shifted[0] = 1

            def group(g, _):
                at = pl.multiple_of(g * G, G)
                w = sc[pl.ds(at, G), :width] * GAIN
                old = row_m[pl.ds(at, G), :]
                top = jnp.maximum(old, lanes(w, jnp.maximum))
                total = row_s[pl.ds(at, G), :] * jnp.exp2(old - top)
                for k in range(width // 128):
                    total = total + jnp.exp2(w[:, k * 128 : (k + 1) * 128] - top)
                row_m[pl.ds(at, G), :] = top
                row_s[pl.ds(at, G), :] = total
                if not diag:
                    old = col_m[r, :, :width]
                    top = jnp.maximum(old, rows8(w, jnp.maximum))
                    total = col_s[r, :, :width] * jnp.exp2(old - top)
                    for k in range(G // 8):
                        total = total + jnp.exp2(w[k * 8 : (k + 1) * 8, :] - top)
                    col_m[r, :, :width] = top
                    col_s[r, :, :width] = total
                return 0

            lax.fori_loop(0, B // G, group, 0)

    def arrive(r):
        @pl.when(waited[r] == 0)
        def _():
            for s in range(nr):

                @pl.when(r == s)
                def _(s=s):
                    for c in copies(1, s):
                        c.wait()

            waited[r] = 1

    def runs():
        start = 0
        for r in range(1, nr + 1):
            if r == nr or widths[r] != widths[start]:
                yield start, r, widths[start]
                start = r

    def left(q, _):
        needed = functools.reduce(jnp.logical_or, [live[q, r] > 0 for r in range(nr)])
        for s in range(1, nl):

            @pl.when(q + 1 == s)
            def _(s=s):
                fetch(s)

        row_out[pl.ds(q, 1), :] = jnp.full((1, B), FLOOR, jnp.float32)

        @pl.when(needed)
        def _():
            row_f[...] = jnp.zeros_like(row_f)
            shifted[0] = 0
            for s in range(nl):

                @pl.when(q == s)
                def _(s=s):
                    for c in copies(0, s):
                        c.wait()

            if own_first:

                @pl.when(q == 0)
                def _():
                    arrive(0)
                    pair(0, 0, B, True)

            for start, stop, width in runs():

                def step(r, _, width=width):
                    go = live[q, r] > 0
                    if own_first:
                        go = jnp.logical_and(go, q + r > 0)

                    @pl.when(go)
                    def _():
                        arrive(r)
                        pair(q, r, width, False)

                    return 0

                lax.fori_loop(start, stop, step, 0)

            @pl.when(shifted[0] == 0)
            def _():
                row_out[pl.ds(q, 1), :] = jnp.log2(jnp.sum(row_f[...].T, 0, keepdims=True))

            @pl.when(shifted[0] > 0)
            def _():
                row_out[pl.ds(q, 1), :] = fold(row_m[...].T, row_s[...].T, row_f[...].T, 0)

        return 0

    lax.fori_loop(0, nl, left, 0)
    for r in range(nr):
        col_out[r : r + 1, :] = jnp.full((1, B), FLOOR, jnp.float32)

        @pl.when(need_r[r])
        def _(r=r):
            col_out[r : r + 1, :] = fold(col_m[r], col_s[r], col_f[r], 0)

    for out, prevs in ((row_out, () if last else row_prev), (col_out, col_prev)):
        at = 0
        for prev in prevs:
            to = at + prev.shape[0]
            out[at:to, :] = log2_add(out[at:to, :], prev[...])
            at = to

    if last:
        ring_out, next_out, after_out = outs
        chip, core = me % RING // 2, me % 2
        for q in range(RING):
            at = (chip + PLACES[q][0]) % 4 * 2 + (core + PLACES[q][1]) % 2
            row = row_out[0:1, :] if q == RING - 1 else row_prev[0][q : q + 1, :]
            ring_out[at] = row if q else log2_add(row, col_out[0:1, :])
        next_out[...] = col_out[1:2, :]
        after_out[:, : B // 2] = col_out[3:4, : B // 2]
        after_out[:, B // 2 :] = col_out[2:3, : B // 2]


def stage(name, wanted, lefts, rights, row_prev=(), col_prev=(), own_first=False, last=False):
    nl, nr = len(lefts), len(rights)
    flat, tables = [], []
    for side in (lefts, rights):
        table = []
        for slot, pieces in enumerate(side):
            for array, src, dst, count in pieces:
                flat.append(array)
                table.append((slot, src, dst, count))
        tables.append(tuple(table))
    widths = tuple(sum(piece[3] for piece in pieces) for pieces in rights)
    nrow, ncol = tuple(p.shape[0] for p in row_prev), tuple(p.shape[0] for p in col_prev)
    lists, at = [], 0
    for pieces in lefts:
        at += len(pieces)
        lists.append((at - 1, pieces[-1][3]))
    plan = (nl, nr, tables[0], tables[1], widths, lists, wanted, nrow, ncol, own_first, last)
    cost = 2 * B * B * D * 4 if own_first else B
    f32 = jnp.float32
    shapes = [(RING, 1, B), (1, B), (1, B)] if last else [(nl, B), (nr, B)]
    shapes = [jax.ShapeDtypeStruct(shape, f32) for shape in shapes]
    return pl.pallas_call(
        functools.partial(stage_kernel, plan),
        out_shape=shapes,
        in_specs=[pl.BlockSpec(memory_space=pltpu.VMEM)] * (len(nrow) + len(ncol))
        + [pl.BlockSpec(memory_space=pl.ANY)] * len(flat),
        out_specs=[pl.BlockSpec(memory_space=pltpu.VMEM)] * len(shapes),
        scratch_shapes=[
            pltpu.VMEM((nl, B, D), jnp.bfloat16),
            pltpu.VMEM((nr, B, D), jnp.bfloat16),
            pltpu.VMEM((B, B), f32),
            pltpu.VMEM((B, 128), f32),
            pltpu.VMEM((8, B), f32),
            pltpu.VMEM((2, 8, 128), f32),
            pltpu.VMEM((B, 128), f32),
            pltpu.VMEM((B, 128), f32),
            pltpu.VMEM((B, 128), f32),
            pltpu.VMEM((nr, 8, B), f32),
            pltpu.VMEM((nr, 8, B), f32),
            pltpu.VMEM((nr, 8, B), f32),
            pltpu.SMEM((nr,), jnp.int32),
            pltpu.SMEM((1,), jnp.int32),
            pltpu.SemaphoreType.DMA((nl,)),
            pltpu.SemaphoreType.DMA((nr,)),
            pltpu.VMEM((nl, LIST, 128), jnp.bfloat16),
            pltpu.VMEM((8, 128), jnp.int32),
            pltpu.SMEM((8, 128), jnp.int32),
            pltpu.SemaphoreType.DMA((nl + 1,)),
            pltpu.VMEM((nl, B), f32),
            pltpu.VMEM((nr, B), f32),
        ],
        compiler_params=pltpu.CompilerParams(vmem_limit_bytes=GRANT),
        cost_estimate=pl.CostEstimate(
            flops=cost, bytes_accessed=B, transcendentals=0
        ),
        name=name,
    )(*row_prev, *col_prev, *flat)


def last_kernel(ring_ref, *refs):
    parts, o_ref = refs[:-1], refs[-1]
    row = lax.axis_index("dp") // RING
    got = [ring_ref[k] for k in range(RING)]
    for k, part in enumerate(parts):
        got.append(jnp.where(row > k, part[...], FLOOR))
    got = jnp.concatenate(got, 0)
    best = jnp.max(got, 0, keepdims=True)
    total = jnp.sum(jnp.exp2(got - best), 0, keepdims=True)
    o_ref[...] = (best + jnp.log2(total)) * (LN2 / SCALE)


def body(embeddings, partners, pair_count):
    unit, top, low = normalize(embeddings, partners, pair_count)
    swap = along(0, 1)
    together = lax.optimization_barrier

    over, on = [], []
    for d in range(2 * RING, COUNT):
        z, y = d // 32, (d // RING) % 4
        relay = (z - (y < 2)) * 32 + (y + 1) % 4 * RING + d % RING
        over.append((d, relay))
        on.append((relay, d - 2 * RING))

    def whole(array):
        return [(array, 0, 0, B)]

    a = send(unit, around(1))
    b = send(unit, around(-1))
    relayed = send(low, over)
    c = send(unit, along(-RING))
    row_0, _ = stage("own", ((1,),), [whole(unit)], [whole(unit)], own_first=True)
    relayed, row_0, late = together((relayed, row_0, unit))
    d_low = send(relayed, on)
    sib = send(late, swap)
    a, b = together((a, b))

    a_top, b_low = halves(a, b)
    f_top = send(a_top, around(1))
    f_low = send(b_low, around(-1))
    c, d_low, sib = together((c, d_low, sib))
    a, b, top, a_top, c = together((a, b, top, a_top, c))
    d_top = send(top, along(-2 * RING))
    a_sib = send(a, swap)
    b_sib = send(b, swap)

    rights = [whole(unit), whole(c), [(d_low, 0, 0, H)]]
    lefts = [whole(unit), whole(sib), whole(a), whole(b)]
    row_1, col_1 = stage("near", ((0, 1, 1),) + ((1, 1, 1),) * 3, lefts, rights, [row_0], [])
    a_sib, b_sib, row_1 = together((a_sib, b_sib, row_1))
    row_2, col_2 = stage("mid", ((1, 1, 1),) * 2, [whole(a_sib), whole(b_sib)], rights, [], [col_1])
    f_top, f_low, d_top, row_2 = together((f_top, f_low, d_top, row_2))
    f_top_sib = send(f_top, swap)
    f_low_sib = send(f_low, swap)

    rights = rights + [[(d_top, 0, 0, H)]]
    lefts = lefts + [whole(a_sib), whole(b_sib), [(f_top, 0, 0, H), (f_low, 0, H, H)]]
    wanted = ((0, 0, 0, 1),) * 6 + ((1, 1, 1, 1),)
    row_3, col_3 = stage("far", wanted, lefts, rights, [row_1, row_2], [col_2])
    f_low_sib, f_top_sib, row_3 = together((f_low_sib, f_top_sib, row_3))
    lefts = [[(f_top_sib, 0, 0, H), (f_low_sib, 0, H, H)]]
    ring_part, next_part, after_part = stage("last", ((1, 1, 1, 1),), lefts, rights, [row_3], [col_3], last=True)

    next_got = send(next_part, along(RING))
    after_got = send(after_part, along(2 * RING))
    groups = [[r * RING + k for k in range(RING)] for r in range(COUNT // RING)]
    ring_got = lax.all_to_all(ring_part, "dp", 0, 0, axis_index_groups=groups, tiled=True)
    out = pl.pallas_call(
        last_kernel,
        out_shape=jax.ShapeDtypeStruct((1, B), jnp.float32),
        name="last_sum",
    )(ring_got, next_got, after_got)
    return out.reshape(B)


def solution(mesh):
    placed = (P("dp", None), P("dp", None), P("dp"))
    return jax.shard_map(body, mesh=mesh, in_specs=placed, out_specs=P("dp"), check_vma=False)
```

```python
import functools

import jax
import jax.numpy as jnp
from jax import lax
from jax.experimental import pallas as pl
from jax.experimental.pallas import tpu as pltpu
from jax.sharding import PartitionSpec as P

SCALE = 256.0
LOG2E = 1.4426950408889634
LN2 = 0.6931471805599453
GAIN = SCALE * LOG2E
LEAST = 2.0**-60
MOST = 2.0**112
FLOOR = -1e30
MASKED = -1e27
SCRATCH = 22
PLACES = [(0, 0), (0, 1), (3, 0), (1, 0), (3, 1), (1, 1), (2, 0), (2, 1)]
B = 1024
D = 1024
H = B // 2
CH = 256
G = 32
COUNT = 128
RING = 8
HALVES = B // 2 // CH
LIST = 16
GRANT = 63 * 2**20 + 2**19


def around(dx):
    moves = []
    for d in range(COUNT):
        core, x, rest = d % 2, (d // 2) % 4, d // RING
        moves.append((d, rest * RING + ((x + dx) % 4) * 2 + core))
    return moves


def along(steps, flip=0):
    return [(d, (d + steps) ^ flip) for d in range(COUNT) if 0 <= d + steps < COUNT]


def send(value, moves):
    return lax.ppermute(value, "dp", moves)


def unit_kernel(list_ref, count_ref, x_ref, o_ref, top_ref, low_ref, x, o, in_sem, out_sem):
    def rows(i):
        return pl.ds(i * CH, CH)

    loads = [pltpu.make_async_copy(x_ref.at[rows(i), :], x.at[rows(i), :], in_sem.at[i]) for i in range(B // CH)]
    for load in loads:
        load.start()
    lane = lax.broadcasted_iota(jnp.int32, (LIST, D), 1)
    pairs = jnp.full((LIST, D), -1.0, jnp.float32)
    for k in range(list_ref.shape[1]):
        entry = jnp.where(k < count_ref[0], list_ref[0, k], -1).astype(jnp.float32)
        pairs = jnp.where(lane == k, entry, pairs)
    o[B : B + LIST, :] = pairs.astype(jnp.bfloat16)
    stores = [pltpu.make_async_copy(o.at[pl.ds(B, LIST), :], o_ref.at[pl.ds(B, LIST), :], out_sem.at[0])]
    stores[0].start()
    for i in range(B // CH):
        loads[i].wait()
        for g in range(CH // G):
            at = slice(i * CH + g * G, i * CH + (g + 1) * G)
            v = x[at, :].astype(jnp.float32)
            size = jnp.sum(v * v, -1, keepdims=True)
            o[at, :] = (v * lax.rsqrt(size + 1e-06)).astype(jnp.bfloat16)
        stores.append(pltpu.make_async_copy(o.at[rows(i), :], o_ref.at[rows(i), :], out_sem.at[2 * i + 1]))
        half = top_ref.at[rows(i), :] if i < HALVES else low_ref.at[rows(i - HALVES), :]
        stores.append(pltpu.make_async_copy(o.at[rows(i), :], half, out_sem.at[2 * i + 2]))
        stores[-2].start()
        stores[-1].start()
    for store in stores:
        store.wait()


def normalize(embeddings, partners, pair_count):
    bf16 = jnp.bfloat16
    smem, anywhere = pl.BlockSpec(memory_space=pltpu.SMEM), pl.BlockSpec(memory_space=pl.ANY)
    return pl.pallas_call(
        unit_kernel,
        in_specs=[smem, smem, anywhere],
        out_specs=[anywhere] * 3,
        out_shape=[
            jax.ShapeDtypeStruct((B + LIST, D), bf16),
            jax.ShapeDtypeStruct((B // 2, D), bf16),
            jax.ShapeDtypeStruct((B // 2, D), bf16),
        ],
        scratch_shapes=[
            pltpu.VMEM((B, D), bf16),
            pltpu.VMEM((B + LIST, D), bf16),
            pltpu.SemaphoreType.DMA((B // CH,)),
            pltpu.SemaphoreType.DMA((2 * (B // CH) + 1,)),
        ],
        compiler_params=pltpu.CompilerParams(vmem_limit_bytes=GRANT),
        name="unit_rows",
    )(partners, pair_count, embeddings)


def halves_kernel(a_ref, b_ref, top_ref, low_ref, buf, sem):
    n = B // 2 // CH
    moves = []
    for i in range(2 * n):
        count = CH + LIST if i == 2 * n - 1 else CH
        src = a_ref.at[pl.ds(i * CH, count), :] if i < n else b_ref.at[pl.ds(i * CH, count), :]
        dst = top_ref.at[pl.ds(i * CH, count), :] if i < n else low_ref.at[pl.ds((i - n) * CH, count), :]
        held = buf.at[pl.ds(i * CH, count), :]
        moves.append((pltpu.make_async_copy(src, held, sem.at[2 * i]), pltpu.make_async_copy(held, dst, sem.at[2 * i + 1])))
    for load, _ in moves:
        load.start()
    for load, store in moves:
        load.wait()
        store.start()
    for _, store in moves:
        store.wait()


def halves(a, b):
    bf16, anywhere = jnp.bfloat16, pl.BlockSpec(memory_space=pl.ANY)
    return pl.pallas_call(
        halves_kernel,
        in_specs=[anywhere] * 2,
        out_specs=[anywhere] * 2,
        out_shape=[jax.ShapeDtypeStruct((B // 2, D), bf16), jax.ShapeDtypeStruct((B // 2 + LIST, D), bf16)],
        scratch_shapes=[pltpu.VMEM((B + LIST, D), bf16), pltpu.SemaphoreType.DMA((2 * B // CH,))],
        compiler_params=pltpu.CompilerParams(vmem_limit_bytes=GRANT),
        name="halves",
    )(a, b)


def lanes(value, op):
    return functools.reduce(op, [value[:, q * 128 : (q + 1) * 128] for q in range(value.shape[1] // 128)])


def rows8(value, op):
    return functools.reduce(op, [value[q * 8 : (q + 1) * 8, :] for q in range(value.shape[0] // 8)])


def fold(m, s, f, axis):
    top = jnp.max(m, axis, keepdims=True)
    plain = jnp.sum(f, axis, keepdims=True)
    top = jnp.maximum(top, jnp.where(plain > 0.0, 0.0, FLOOR))
    total = jnp.sum(s * jnp.exp2(m - top), axis, keepdims=True)
    total = total + plain * jnp.exp2(jnp.minimum(-top, 0.0))
    return jnp.maximum(top + jnp.log2(total), FLOOR)


def log2_add(a, b):
    top = jnp.maximum(a, b)
    return top + jnp.log2(jnp.exp2(a - top) + jnp.exp2(b - top))


def stage_kernel(plan, *refs):
    nl, nr, lefts, rights, widths, lists, wanted, nrow, ncol, own_first, last = plan
    row_prev, col_prev, refs = refs[: len(nrow)], refs[len(nrow) : len(nrow) + len(ncol)], refs[len(nrow) + len(ncol) :]
    blocks, refs = refs[: len(lefts) + len(rights)], refs[len(lefts) + len(rights) :]
    outs, refs = refs[:-SCRATCH], refs[-SCRATCH:]
    row_out, col_out = refs[-2:] if last else outs
    listed, flags, live, list_sem = refs[-6:-2]
    (lbuf, rbuf, sc, row_t, col_t, chk, row_f, row_m, row_s, col_f, col_m, col_s, waited, shifted, lsem, rsem) = refs[:-6]

    def copies(side, slot):
        pieces = lefts if side == 0 else rights
        base = 0 if side == 0 else len(lefts)
        buf, sem = (lbuf, lsem) if side == 0 else (rbuf, rsem)
        made = []
        for i, (s, src, dst, count) in enumerate(pieces):
            if s == slot:
                made.append(
                    pltpu.make_async_copy(
                        blocks[base + i].at[pl.ds(src, count), :], buf.at[slot, pl.ds(dst, count), :], sem.at[slot]
                    )
                )
        return made

    def used(flags):
        return functools.reduce(jnp.logical_or, [f > 0 for f in flags])

    me = lax.axis_index("dp")
    if own_first:
        live[0, 0] = 1
    else:
        fetched = [
            pltpu.make_async_copy(blocks[i].at[pl.ds(row, LIST), pl.ds(0, 128)], listed.at[q], list_sem.at[q])
            for q, (i, row) in enumerate(lists)
        ]
        for copy in fetched:
            copy.start()
        row_at = lax.broadcasted_iota(jnp.int32, (8, 128), 0)
        lane_at = lax.broadcasted_iota(jnp.int32, (8, 128), 1)
        found = jnp.zeros((8, 128), jnp.float32)
        for q in range(nl):
            fetched[q].wait()
            names = listed[q].astype(jnp.float32)[:8, :]
            for r in range(nr):
                if wanted[q][r]:
                    target = (me + RING * min(r, 2)).astype(jnp.float32)
                    hit = jnp.max(jnp.where(names == target, 1.0, 0.0), 1, keepdims=True)
                    found = jnp.where(jnp.logical_and(row_at == q, lane_at == r), hit, found)
        flags[...] = found.astype(jnp.int32)
        noted = pltpu.make_async_copy(flags, live, list_sem.at[nl])
        noted.start()
        noted.wait()

    need_l = [used([live[q, r] for r in range(nr)]) for q in range(nl)]
    need_r = [used([live[q, r] for q in range(nl)]) for r in range(nr)]

    def fetch(q):
        @pl.when(need_l[q])
        def _():
            for c in copies(0, q):
                c.start()

    fetch(0)
    for r in range(nr):
        waited[r] = 0

        @pl.when(need_r[r])
        def _(r=r):
            for c in copies(1, r):
                c.start()

    col_f[...] = jnp.zeros_like(col_f)
    col_s[...] = jnp.zeros_like(col_s)
    col_m[...] = jnp.full_like(col_m, FLOOR)

    def pair(q, r, width, diag):
        def dot(i):
            sc[i * CH : (i + 1) * CH, :width] = lax.dot_general(
                lbuf[q, i * CH : (i + 1) * CH, :],
                rbuf[r, :width, :],
                (((1,), (1,)), ((), ())),
                preferred_element_type=jnp.float32,
            )

        def sums(i):
            cols = jnp.zeros((8, width), jnp.float32)
            most = jnp.zeros((8, 128), jnp.float32)
            least = jnp.full((8, 128), MOST, jnp.float32)
            for g in range(CH // G):
                at = i * CH + g * G
                v = sc[at : at + G, :width]
                if diag:
                    r_at = lax.broadcasted_iota(jnp.int32, (G, width), 0) + at
                    c_at = lax.broadcasted_iota(jnp.int32, (G, width), 1)
                    eye = r_at == c_at
                    v = jnp.where(eye, MASKED, v)
                    sc[at : at + G, :width] = v
                e = jnp.exp2(v * GAIN)
                part = lanes(e, jnp.add)
                row_t[at : at + G, :] = part
                if not diag:
                    cols = cols + rows8(e, jnp.add)
                most = jnp.maximum(most, rows8(part, jnp.maximum))
                least = jnp.minimum(least, rows8(part, jnp.minimum))
            if not diag:
                if i:
                    cols = col_t[:, :width] + cols
                col_t[:, :width] = cols
                if i == B // CH - 1:
                    least = jnp.minimum(least, lanes(cols, jnp.minimum))
            if i:
                most, least = jnp.maximum(chk[0], most), jnp.minimum(chk[1], least)
            chk[0], chk[1] = most, least

        n = B // CH
        dot(0)
        for i in range(n):
            if i + 1 < n:
                dot(i + 1)
            sums(i)
        safe = jnp.logical_and(chk[0] <= MOST, chk[1] >= LEAST)
        plain = jnp.max(jnp.where(safe, 0.0, 1.0)) == 0.0

        @pl.when(plain)
        def _():
            row_f[...] += row_t[...]
            if not diag:
                col_f[r, :, :width] += col_t[:, :width]

        @pl.when(jnp.logical_not(plain))
        def _():
            @pl.when(shifted[0] == 0)
            def _():
                row_s[...] = jnp.zeros_like(row_s)
                row_m[...] = jnp.full_like(row_m, FLOOR)
                shifted[0] = 1

            def group(g, _):
                at = pl.multiple_of(g * G, G)
                w = sc[pl.ds(at, G), :width] * GAIN
                old = row_m[pl.ds(at, G), :]
                top = jnp.maximum(old, lanes(w, jnp.maximum))
                total = row_s[pl.ds(at, G), :] * jnp.exp2(old - top)
                for k in range(width // 128):
                    total = total + jnp.exp2(w[:, k * 128 : (k + 1) * 128] - top)
                row_m[pl.ds(at, G), :] = top
                row_s[pl.ds(at, G), :] = total
                if not diag:
                    old = col_m[r, :, :width]
                    top = jnp.maximum(old, rows8(w, jnp.maximum))
                    total = col_s[r, :, :width] * jnp.exp2(old - top)
                    for k in range(G // 8):
                        total = total + jnp.exp2(w[k * 8 : (k + 1) * 8, :] - top)
                    col_m[r, :, :width] = top
                    col_s[r, :, :width] = total
                return 0

            lax.fori_loop(0, B // G, group, 0, unroll=4)

    def arrive(r):
        @pl.when(waited[r] == 0)
        def _():
            for s in range(nr):

                @pl.when(r == s)
                def _(s=s):
                    for c in copies(1, s):
                        c.wait()

            waited[r] = 1

    def runs():
        start = 0
        for r in range(1, nr + 1):
            if r == nr or widths[r] != widths[start]:
                yield start, r, widths[start]
                start = r

    def left(q, _):
        needed = functools.reduce(jnp.logical_or, [live[q, r] > 0 for r in range(nr)])
        for s in range(1, nl):

            @pl.when(q + 1 == s)
            def _(s=s):
                fetch(s)

        row_out[pl.ds(q, 1), :] = jnp.full((1, B), FLOOR, jnp.float32)

        @pl.when(needed)
        def _():
            row_f[...] = jnp.zeros_like(row_f)
            shifted[0] = 0
            for s in range(nl):

                @pl.when(q == s)
                def _(s=s):
                    for c in copies(0, s):
                        c.wait()

            if own_first:

                @pl.when(q == 0)
                def _():
                    arrive(0)
                    pair(0, 0, B, True)

            for start, stop, width in runs():

                def step(r, _, width=width):
                    go = live[q, r] > 0
                    if own_first:
                        go = jnp.logical_and(go, q + r > 0)

                    @pl.when(go)
                    def _():
                        arrive(r)
                        pair(q, r, width, False)

                    return 0

                lax.fori_loop(start, stop, step, 0)

            @pl.when(shifted[0] == 0)
            def _():
                row_out[pl.ds(q, 1), :] = jnp.log2(jnp.sum(row_f[...].T, 0, keepdims=True))

            @pl.when(shifted[0] > 0)
            def _():
                row_out[pl.ds(q, 1), :] = fold(row_m[...].T, row_s[...].T, row_f[...].T, 0)

        return 0

    lax.fori_loop(0, nl, left, 0)
    for r in range(nr):
        col_out[r : r + 1, :] = jnp.full((1, B), FLOOR, jnp.float32)

        @pl.when(need_r[r])
        def _(r=r):
            col_out[r : r + 1, :] = fold(col_m[r], col_s[r], col_f[r], 0)

    for out, prevs in ((row_out, () if last else row_prev), (col_out, col_prev)):
        at = 0
        for prev in prevs:
            to = at + prev.shape[0]
            out[at:to, :] = log2_add(out[at:to, :], prev[...])
            at = to

    if last:
        ring_out, next_out, after_out = outs
        chip, core = me % RING // 2, me % 2
        for q in range(RING):
            at = (chip + PLACES[q][0]) % 4 * 2 + (core + PLACES[q][1]) % 2
            row = row_out[0:1, :] if q == RING - 1 else row_prev[0][q : q + 1, :]
            ring_out[at] = row if q else log2_add(row, col_out[0:1, :])
        next_out[...] = col_out[1:2, :]
        after_out[:, : B // 2] = col_out[3:4, : B // 2]
        after_out[:, B // 2 :] = col_out[2:3, : B // 2]


def stage(name, wanted, lefts, rights, row_prev=(), col_prev=(), own_first=False, last=False):
    nl, nr = len(lefts), len(rights)
    flat, tables = [], []
    for side in (lefts, rights):
        table = []
        for slot, pieces in enumerate(side):
            for array, src, dst, count in pieces:
                flat.append(array)
                table.append((slot, src, dst, count))
        tables.append(tuple(table))
    widths = tuple(sum(piece[3] for piece in pieces) for pieces in rights)
    nrow, ncol = tuple(p.shape[0] for p in row_prev), tuple(p.shape[0] for p in col_prev)
    lists, at = [], 0
    for pieces in lefts:
        at += len(pieces)
        lists.append((at - 1, pieces[-1][3]))
    plan = (nl, nr, tables[0], tables[1], widths, lists, wanted, nrow, ncol, own_first, last)
    cost = 2 * B * B * D * 4 if own_first else B
    f32 = jnp.float32
    shapes = [(RING, 1, B), (1, B), (1, B)] if last else [(nl, B), (nr, B)]
    shapes = [jax.ShapeDtypeStruct(shape, f32) for shape in shapes]
    return pl.pallas_call(
        functools.partial(stage_kernel, plan),
        out_shape=shapes,
        in_specs=[pl.BlockSpec(memory_space=pltpu.VMEM)] * (len(nrow) + len(ncol))
        + [pl.BlockSpec(memory_space=pl.ANY)] * len(flat),
        out_specs=[pl.BlockSpec(memory_space=pltpu.VMEM)] * len(shapes),
        scratch_shapes=[
            pltpu.VMEM((nl, B, D), jnp.bfloat16),
            pltpu.VMEM((nr, B, D), jnp.bfloat16),
            pltpu.VMEM((B, B), f32),
            pltpu.VMEM((B, 128), f32),
            pltpu.VMEM((8, B), f32),
            pltpu.VMEM((2, 8, 128), f32),
            pltpu.VMEM((B, 128), f32),
            pltpu.VMEM((B, 128), f32),
            pltpu.VMEM((B, 128), f32),
            pltpu.VMEM((nr, 8, B), f32),
            pltpu.VMEM((nr, 8, B), f32),
            pltpu.VMEM((nr, 8, B), f32),
            pltpu.SMEM((nr,), jnp.int32),
            pltpu.SMEM((1,), jnp.int32),
            pltpu.SemaphoreType.DMA((nl,)),
            pltpu.SemaphoreType.DMA((nr,)),
            pltpu.VMEM((nl, LIST, 128), jnp.bfloat16),
            pltpu.VMEM((8, 128), jnp.int32),
            pltpu.SMEM((8, 128), jnp.int32),
            pltpu.SemaphoreType.DMA((nl + 1,)),
            pltpu.VMEM((nl, B), f32),
            pltpu.VMEM((nr, B), f32),
        ],
        compiler_params=pltpu.CompilerParams(vmem_limit_bytes=GRANT),
        cost_estimate=pl.CostEstimate(
            flops=cost, bytes_accessed=B, transcendentals=0
        ),
        name=name,
    )(*row_prev, *col_prev, *flat)


def last_kernel(ring_ref, *refs):
    parts, o_ref = refs[:-1], refs[-1]
    row = lax.axis_index("dp") // RING
    got = [ring_ref[k] for k in range(RING)]
    for k, part in enumerate(parts):
        got.append(jnp.where(row > k, part[...], FLOOR))
    got = jnp.concatenate(got, 0)
    best = jnp.max(got, 0, keepdims=True)
    total = jnp.sum(jnp.exp2(got - best), 0, keepdims=True)
    o_ref[...] = (best + jnp.log2(total)) * (LN2 / SCALE)


def body(embeddings, partners, pair_count):
    unit, top, low = normalize(embeddings, partners, pair_count)
    swap = along(0, 1)
    together = lax.optimization_barrier

    over, on = [], []
    for d in range(2 * RING, COUNT):
        z, y = d // 32, (d // RING) % 4
        relay = (z - (y < 2)) * 32 + (y + 1) % 4 * RING + d % RING
        over.append((d, relay))
        on.append((relay, d - 2 * RING))

    def whole(array):
        return [(array, 0, 0, B)]

    a = send(unit, around(1))
    b = send(unit, around(-1))
    relayed = send(low, over)
    c = send(unit, along(-RING))
    row_0, _ = stage("own", ((1,),), [whole(unit)], [whole(unit)], own_first=True)
    relayed, row_0, late = together((relayed, row_0, unit))
    d_low = send(relayed, on)
    sib = send(late, swap)
    a, b = together((a, b))

    a_top, b_low = halves(a, b)
    f_top = send(a_top, around(1))
    f_low = send(b_low, around(-1))
    c, d_low, sib = together((c, d_low, sib))
    a, b, top, a_top, c = together((a, b, top, a_top, c))
    d_top = send(top, along(-2 * RING))
    a_sib = send(a, swap)
    b_sib = send(b, swap)

    rights = [whole(unit), whole(c), [(d_low, 0, 0, H)]]
    lefts = [whole(unit), whole(sib), whole(a), whole(b)]
    row_1, col_1 = stage("near", ((0, 1, 1),) + ((1, 1, 1),) * 3, lefts, rights, [row_0], [])
    a_sib, b_sib, row_1 = together((a_sib, b_sib, row_1))
    row_2, col_2 = stage("mid", ((1, 1, 1),) * 2, [whole(a_sib), whole(b_sib)], rights, [], [col_1])
    f_top, f_low, d_top, row_2 = together((f_top, f_low, d_top, row_2))
    f_top_sib = send(f_top, swap)
    f_low_sib = send(f_low, swap)

    rights = rights + [[(d_top, 0, 0, H)]]
    lefts = lefts + [whole(a_sib), whole(b_sib), [(f_top, 0, 0, H), (f_low, 0, H, H)]]
    wanted = ((0, 0, 0, 1),) * 6 + ((1, 1, 1, 1),)
    row_3, col_3 = stage("far", wanted, lefts, rights, [row_1, row_2], [col_2])
    f_low_sib, f_top_sib, row_3 = together((f_low_sib, f_top_sib, row_3))
    lefts = [[(f_top_sib, 0, 0, H), (f_low_sib, 0, H, H)]]
    ring_part, next_part, after_part = stage("last", ((1, 1, 1, 1),), lefts, rights, [row_3], [col_3], last=True)

    next_got = send(next_part, along(RING))
    after_got = send(after_part, along(2 * RING))
    groups = [[r * RING + k for k in range(RING)] for r in range(COUNT // RING)]
    ring_got = lax.all_to_all(ring_part, "dp", 0, 0, axis_index_groups=groups, tiled=True)
    out = pl.pallas_call(
        last_kernel,
        out_shape=jax.ShapeDtypeStruct((1, B), jnp.float32),
        name="last_sum",
    )(ring_got, next_got, after_got)
    return out.reshape(B)


def solution(mesh):
    placed = (P("dp", None), P("dp", None), P("dp"))
    return jax.shard_map(body, mesh=mesh, in_specs=placed, out_specs=P("dp"), check_vma=False)
```

```python
import functools

import jax
import jax.numpy as jnp
from jax import lax
from jax.experimental import pallas as pl
from jax.experimental.pallas import tpu as pltpu
from jax.sharding import PartitionSpec as P

SCALE = 256.0
LOG2E = 1.4426950408889634
LN2 = 0.6931471805599453
GAIN = SCALE * LOG2E
LEAST = 2.0**-60
MOST = 2.0**112
FLOOR = -1e30
MASKED = -1e27
SCRATCH = 22
PLACES = [(0, 0), (0, 1), (3, 0), (1, 0), (3, 1), (1, 1), (2, 0), (2, 1)]
B = 1024
D = 1024
H = B // 2
CH = 256
G = 32
COUNT = 128
RING = 8
HALVES = B // 2 // CH
LIST = 16
GRANT = 63 * 2**20 + 2**19


def around(dx):
    moves = []
    for d in range(COUNT):
        core, x, rest = d % 2, (d // 2) % 4, d // RING
        moves.append((d, rest * RING + ((x + dx) % 4) * 2 + core))
    return moves


def along(steps, flip=0):
    return [(d, (d + steps) ^ flip) for d in range(COUNT) if 0 <= d + steps < COUNT]


def send(value, moves):
    return lax.ppermute(value, "dp", moves)


def unit_kernel(list_ref, count_ref, x_ref, o_ref, top_ref, low_ref, x, o, in_sem, out_sem):
    def rows(i):
        return pl.ds(i * CH, CH)

    loads = [pltpu.make_async_copy(x_ref.at[rows(i), :], x.at[rows(i), :], in_sem.at[i]) for i in range(B // CH)]
    for load in loads:
        load.start()
    lane = lax.broadcasted_iota(jnp.int32, (LIST, D), 1)
    pairs = jnp.full((LIST, D), -1.0, jnp.float32)
    for k in range(list_ref.shape[1]):
        entry = jnp.where(k < count_ref[0], list_ref[0, k], -1).astype(jnp.float32)
        pairs = jnp.where(lane == k, entry, pairs)
    o[B : B + LIST, :] = pairs.astype(jnp.bfloat16)
    stores = [pltpu.make_async_copy(o.at[pl.ds(B, LIST), :], o_ref.at[pl.ds(B, LIST), :], out_sem.at[0])]
    stores[0].start()
    for i in range(B // CH):
        loads[i].wait()
        for g in range(CH // G):
            at = slice(i * CH + g * G, i * CH + (g + 1) * G)
            v = x[at, :].astype(jnp.float32)
            size = jnp.sum(v * v, -1, keepdims=True)
            o[at, :] = (v * lax.rsqrt(size + 1e-06)).astype(jnp.bfloat16)
        stores.append(pltpu.make_async_copy(o.at[rows(i), :], o_ref.at[rows(i), :], out_sem.at[2 * i + 1]))
        half = top_ref.at[rows(i), :] if i < HALVES else low_ref.at[rows(i - HALVES), :]
        stores.append(pltpu.make_async_copy(o.at[rows(i), :], half, out_sem.at[2 * i + 2]))
        stores[-2].start()
        stores[-1].start()
    for store in stores:
        store.wait()


def normalize(embeddings, partners, pair_count):
    bf16 = jnp.bfloat16
    smem, anywhere = pl.BlockSpec(memory_space=pltpu.SMEM), pl.BlockSpec(memory_space=pl.ANY)
    return pl.pallas_call(
        unit_kernel,
        in_specs=[smem, smem, anywhere],
        out_specs=[anywhere] * 3,
        out_shape=[
            jax.ShapeDtypeStruct((B + LIST, D), bf16),
            jax.ShapeDtypeStruct((B // 2, D), bf16),
            jax.ShapeDtypeStruct((B // 2, D), bf16),
        ],
        scratch_shapes=[
            pltpu.VMEM((B, D), bf16),
            pltpu.VMEM((B + LIST, D), bf16),
            pltpu.SemaphoreType.DMA((B // CH,)),
            pltpu.SemaphoreType.DMA((2 * (B // CH) + 1,)),
        ],
        compiler_params=pltpu.CompilerParams(vmem_limit_bytes=GRANT),
        name="unit_rows",
    )(partners, pair_count, embeddings)


def halves_kernel(a_ref, b_ref, top_ref, low_ref, buf, sem):
    n = B // 2 // CH
    moves = []
    for i in range(2 * n):
        count = CH + LIST if i == 2 * n - 1 else CH
        src = a_ref.at[pl.ds(i * CH, count), :] if i < n else b_ref.at[pl.ds(i * CH, count), :]
        dst = top_ref.at[pl.ds(i * CH, count), :] if i < n else low_ref.at[pl.ds((i - n) * CH, count), :]
        held = buf.at[pl.ds(i * CH, count), :]
        moves.append((pltpu.make_async_copy(src, held, sem.at[2 * i]), pltpu.make_async_copy(held, dst, sem.at[2 * i + 1])))
    for load, _ in moves:
        load.start()
    for load, store in moves:
        load.wait()
        store.start()
    for _, store in moves:
        store.wait()


def halves(a, b):
    bf16, anywhere = jnp.bfloat16, pl.BlockSpec(memory_space=pl.ANY)
    return pl.pallas_call(
        halves_kernel,
        in_specs=[anywhere] * 2,
        out_specs=[anywhere] * 2,
        out_shape=[jax.ShapeDtypeStruct((B // 2, D), bf16), jax.ShapeDtypeStruct((B // 2 + LIST, D), bf16)],
        scratch_shapes=[pltpu.VMEM((B + LIST, D), bf16), pltpu.SemaphoreType.DMA((2 * B // CH,))],
        compiler_params=pltpu.CompilerParams(vmem_limit_bytes=GRANT),
        name="halves",
    )(a, b)


def lanes(value, op):
    return functools.reduce(op, [value[:, q * 128 : (q + 1) * 128] for q in range(value.shape[1] // 128)])


def rows8(value, op):
    return functools.reduce(op, [value[q * 8 : (q + 1) * 8, :] for q in range(value.shape[0] // 8)])


def fold(m, s, f, axis):
    top = jnp.max(m, axis, keepdims=True)
    plain = jnp.sum(f, axis, keepdims=True)
    top = jnp.maximum(top, jnp.where(plain > 0.0, 0.0, FLOOR))
    total = jnp.sum(s * jnp.exp2(m - top), axis, keepdims=True)
    total = total + plain * jnp.exp2(jnp.minimum(-top, 0.0))
    return jnp.maximum(top + jnp.log2(total), FLOOR)


def log2_add(a, b):
    top = jnp.maximum(a, b)
    return top + jnp.log2(jnp.exp2(a - top) + jnp.exp2(b - top))


def stage_kernel(plan, *refs):
    nl, nr, lefts, rights, widths, lists, wanted, nrow, ncol, own_first, last = plan
    row_prev, col_prev, refs = refs[: len(nrow)], refs[len(nrow) : len(nrow) + len(ncol)], refs[len(nrow) + len(ncol) :]
    blocks, refs = refs[: len(lefts) + len(rights)], refs[len(lefts) + len(rights) :]
    outs, refs = refs[:-SCRATCH], refs[-SCRATCH:]
    row_out, col_out = refs[-2:] if last else outs
    listed, flags, live, list_sem = refs[-6:-2]
    (lbuf, rbuf, sc, row_t, col_t, chk, row_f, row_m, row_s, col_f, col_m, col_s, waited, shifted, lsem, rsem) = refs[:-6]

    def copies(side, slot):
        pieces = lefts if side == 0 else rights
        base = 0 if side == 0 else len(lefts)
        buf, sem = (lbuf, lsem) if side == 0 else (rbuf, rsem)
        made = []
        for i, (s, src, dst, count) in enumerate(pieces):
            if s == slot:
                made.append(
                    pltpu.make_async_copy(
                        blocks[base + i].at[pl.ds(src, count), :], buf.at[slot, pl.ds(dst, count), :], sem.at[slot]
                    )
                )
        return made

    def used(flags):
        return functools.reduce(jnp.logical_or, [f > 0 for f in flags])

    def early():
        for c in copies(0, 0):
            c.start()
        for r in range(nr):
            waited[r] = 0
            for c in copies(1, r):
                c.start()

    me = lax.axis_index("dp")
    if own_first:
        live[0, 0] = 1
        early()
    else:
        fetched = [
            pltpu.make_async_copy(blocks[i].at[pl.ds(row, LIST), pl.ds(0, 128)], listed.at[q], list_sem.at[q])
            for q, (i, row) in enumerate(lists)
        ]
        for copy in fetched:
            copy.start()
        early()
        row_at = lax.broadcasted_iota(jnp.int32, (8, 128), 0)
        lane_at = lax.broadcasted_iota(jnp.int32, (8, 128), 1)
        found = jnp.zeros((8, 128), jnp.float32)
        for q in range(nl):
            fetched[q].wait()
            names = listed[q].astype(jnp.float32)[:8, :]
            for r in range(nr):
                if wanted[q][r]:
                    target = (me + RING * min(r, 2)).astype(jnp.float32)
                    hit = jnp.max(jnp.where(names == target, 1.0, 0.0), 1, keepdims=True)
                    found = jnp.where(jnp.logical_and(row_at == q, lane_at == r), hit, found)
        flags[...] = found.astype(jnp.int32)
        noted = pltpu.make_async_copy(flags, live, list_sem.at[nl])
        noted.start()
        noted.wait()

    need_l = [used([live[q, r] for r in range(nr)]) for q in range(nl)]
    need_r = [used([live[q, r] for q in range(nl)]) for r in range(nr)]

    def fetch(q):
        @pl.when(need_l[q])
        def _():
            for c in copies(0, q):
                c.start()

    col_f[...] = jnp.zeros_like(col_f)
    col_s[...] = jnp.zeros_like(col_s)
    col_m[...] = jnp.full_like(col_m, FLOOR)

    def pair(q, r, width, diag):
        def dot(i):
            sc[i * CH : (i + 1) * CH, :width] = lax.dot_general(
                lbuf[q, i * CH : (i + 1) * CH, :],
                rbuf[r, :width, :],
                (((1,), (1,)), ((), ())),
                preferred_element_type=jnp.float32,
            )

        def sums(i):
            cols = jnp.zeros((8, width), jnp.float32)
            most = jnp.zeros((8, 128), jnp.float32)
            least = jnp.full((8, 128), MOST, jnp.float32)
            for g in range(CH // G):
                at = i * CH + g * G
                v = sc[at : at + G, :width]
                if diag:
                    r_at = lax.broadcasted_iota(jnp.int32, (G, width), 0) + at
                    c_at = lax.broadcasted_iota(jnp.int32, (G, width), 1)
                    eye = r_at == c_at
                    v = jnp.where(eye, MASKED, v)
                    sc[at : at + G, :width] = v
                e = jnp.exp2(v * GAIN)
                part = lanes(e, jnp.add)
                row_t[at : at + G, :] = part
                if not diag:
                    cols = cols + rows8(e, jnp.add)
                most = jnp.maximum(most, rows8(part, jnp.maximum))
                least = jnp.minimum(least, rows8(part, jnp.minimum))
            if not diag:
                if i:
                    cols = col_t[:, :width] + cols
                col_t[:, :width] = cols
                if i == B // CH - 1:
                    least = jnp.minimum(least, lanes(cols, jnp.minimum))
            if i:
                most, least = jnp.maximum(chk[0], most), jnp.minimum(chk[1], least)
            chk[0], chk[1] = most, least

        n = B // CH
        dot(0)
        for i in range(n):
            if i + 1 < n:
                dot(i + 1)
            sums(i)
        safe = jnp.logical_and(chk[0] <= MOST, chk[1] >= LEAST)
        plain = jnp.max(jnp.where(safe, 0.0, 1.0)) == 0.0

        @pl.when(plain)
        def _():
            row_f[...] += row_t[...]
            if not diag:
                col_f[r, :, :width] += col_t[:, :width]

        @pl.when(jnp.logical_not(plain))
        def _():
            @pl.when(shifted[0] == 0)
            def _():
                row_s[...] = jnp.zeros_like(row_s)
                row_m[...] = jnp.full_like(row_m, FLOOR)
                shifted[0] = 1

            def group(g, _):
                at = pl.multiple_of(g * G, G)
                w = sc[pl.ds(at, G), :width] * GAIN
                old = row_m[pl.ds(at, G), :]
                top = jnp.maximum(old, lanes(w, jnp.maximum))
                total = row_s[pl.ds(at, G), :] * jnp.exp2(old - top)
                for k in range(width // 128):
                    total = total + jnp.exp2(w[:, k * 128 : (k + 1) * 128] - top)
                row_m[pl.ds(at, G), :] = top
                row_s[pl.ds(at, G), :] = total
                if not diag:
                    old = col_m[r, :, :width]
                    top = jnp.maximum(old, rows8(w, jnp.maximum))
                    total = col_s[r, :, :width] * jnp.exp2(old - top)
                    for k in range(G // 8):
                        total = total + jnp.exp2(w[k * 8 : (k + 1) * 8, :] - top)
                    col_m[r, :, :width] = top
                    col_s[r, :, :width] = total
                return 0

            lax.fori_loop(0, B // G, group, 0, unroll=4)

    def arrive(r):
        @pl.when(waited[r] == 0)
        def _():
            for s in range(nr):

                @pl.when(r == s)
                def _(s=s):
                    for c in copies(1, s):
                        c.wait()

            waited[r] = 1

    def runs():
        start = 0
        for r in range(1, nr + 1):
            if r == nr or widths[r] != widths[start]:
                yield start, r, widths[start]
                start = r

    def left(q, _):
        needed = functools.reduce(jnp.logical_or, [live[q, r] > 0 for r in range(nr)])
        for s in range(1, nl):

            @pl.when(q + 1 == s)
            def _(s=s):
                fetch(s)

        row_out[pl.ds(q, 1), :] = jnp.full((1, B), FLOOR, jnp.float32)

        @pl.when(needed)
        def _():
            row_f[...] = jnp.zeros_like(row_f)
            shifted[0] = 0
            for s in range(nl):

                @pl.when(q == s)
                def _(s=s):
                    for c in copies(0, s):
                        c.wait()

            if own_first:

                @pl.when(q == 0)
                def _():
                    arrive(0)
                    pair(0, 0, B, True)

            for start, stop, width in runs():

                def step(r, _, width=width):
                    go = live[q, r] > 0
                    if own_first:
                        go = jnp.logical_and(go, q + r > 0)

                    @pl.when(go)
                    def _():
                        arrive(r)
                        pair(q, r, width, False)

                    return 0

                lax.fori_loop(start, stop, step, 0)

            @pl.when(shifted[0] == 0)
            def _():
                row_out[pl.ds(q, 1), :] = jnp.log2(jnp.sum(row_f[...].T, 0, keepdims=True))

            @pl.when(shifted[0] > 0)
            def _():
                row_out[pl.ds(q, 1), :] = fold(row_m[...].T, row_s[...].T, row_f[...].T, 0)

        return 0

    lax.fori_loop(0, nl, left, 0)

    @pl.when(jnp.logical_not(need_l[0]))
    def _():
        for c in copies(0, 0):
            c.wait()

    for r in range(nr):

        @pl.when(waited[r] == 0)
        def _(r=r):
            for c in copies(1, r):
                c.wait()

    for r in range(nr):
        col_out[r : r + 1, :] = jnp.full((1, B), FLOOR, jnp.float32)

        @pl.when(need_r[r])
        def _(r=r):
            col_out[r : r + 1, :] = fold(col_m[r], col_s[r], col_f[r], 0)

    for out, prevs in ((row_out, () if last else row_prev), (col_out, col_prev)):
        at = 0
        for prev in prevs:
            to = at + prev.shape[0]
            out[at:to, :] = log2_add(out[at:to, :], prev[...])
            at = to

    if last:
        ring_out, next_out, after_out = outs
        chip, core = me % RING // 2, me % 2
        for q in range(RING):
            at = (chip + PLACES[q][0]) % 4 * 2 + (core + PLACES[q][1]) % 2
            row = row_out[0:1, :] if q == RING - 1 else row_prev[0][q : q + 1, :]
            ring_out[at] = row if q else log2_add(row, col_out[0:1, :])
        next_out[...] = col_out[1:2, :]
        after_out[:, : B // 2] = col_out[3:4, : B // 2]
        after_out[:, B // 2 :] = col_out[2:3, : B // 2]


def stage(name, wanted, lefts, rights, row_prev=(), col_prev=(), own_first=False, last=False):
    nl, nr = len(lefts), len(rights)
    flat, tables = [], []
    for side in (lefts, rights):
        table = []
        for slot, pieces in enumerate(side):
            for array, src, dst, count in pieces:
                flat.append(array)
                table.append((slot, src, dst, count))
        tables.append(tuple(table))
    widths = tuple(sum(piece[3] for piece in pieces) for pieces in rights)
    nrow, ncol = tuple(p.shape[0] for p in row_prev), tuple(p.shape[0] for p in col_prev)
    lists, at = [], 0
    for pieces in lefts:
        at += len(pieces)
        lists.append((at - 1, pieces[-1][3]))
    plan = (nl, nr, tables[0], tables[1], widths, lists, wanted, nrow, ncol, own_first, last)
    cost = 2 * B * B * D * 4 if own_first else B
    f32 = jnp.float32
    shapes = [(RING, 1, B), (1, B), (1, B)] if last else [(nl, B), (nr, B)]
    shapes = [jax.ShapeDtypeStruct(shape, f32) for shape in shapes]
    return pl.pallas_call(
        functools.partial(stage_kernel, plan),
        out_shape=shapes,
        in_specs=[pl.BlockSpec(memory_space=pltpu.VMEM)] * (len(nrow) + len(ncol))
        + [pl.BlockSpec(memory_space=pl.ANY)] * len(flat),
        out_specs=[pl.BlockSpec(memory_space=pltpu.VMEM)] * len(shapes),
        scratch_shapes=[
            pltpu.VMEM((nl, B, D), jnp.bfloat16),
            pltpu.VMEM((nr, B, D), jnp.bfloat16),
            pltpu.VMEM((B, B), f32),
            pltpu.VMEM((B, 128), f32),
            pltpu.VMEM((8, B), f32),
            pltpu.VMEM((2, 8, 128), f32),
            pltpu.VMEM((B, 128), f32),
            pltpu.VMEM((B, 128), f32),
            pltpu.VMEM((B, 128), f32),
            pltpu.VMEM((nr, 8, B), f32),
            pltpu.VMEM((nr, 8, B), f32),
            pltpu.VMEM((nr, 8, B), f32),
            pltpu.SMEM((nr,), jnp.int32),
            pltpu.SMEM((1,), jnp.int32),
            pltpu.SemaphoreType.DMA((nl,)),
            pltpu.SemaphoreType.DMA((nr,)),
            pltpu.VMEM((nl, LIST, 128), jnp.bfloat16),
            pltpu.VMEM((8, 128), jnp.int32),
            pltpu.SMEM((8, 128), jnp.int32),
            pltpu.SemaphoreType.DMA((nl + 1,)),
            pltpu.VMEM((nl, B), f32),
            pltpu.VMEM((nr, B), f32),
        ],
        compiler_params=pltpu.CompilerParams(vmem_limit_bytes=GRANT),
        cost_estimate=pl.CostEstimate(
            flops=cost, bytes_accessed=B, transcendentals=0
        ),
        name=name,
    )(*row_prev, *col_prev, *flat)


def last_kernel(ring_ref, *refs):
    parts, o_ref = refs[:-1], refs[-1]
    row = lax.axis_index("dp") // RING
    got = [ring_ref[k] for k in range(RING)]
    for k, part in enumerate(parts):
        got.append(jnp.where(row > k, part[...], FLOOR))
    got = jnp.concatenate(got, 0)
    best = jnp.max(got, 0, keepdims=True)
    total = jnp.sum(jnp.exp2(got - best), 0, keepdims=True)
    o_ref[...] = (best + jnp.log2(total)) * (LN2 / SCALE)


def body(embeddings, partners, pair_count):
    unit, top, low = normalize(embeddings, partners, pair_count)
    swap = along(0, 1)
    together = lax.optimization_barrier

    over, on = [], []
    for d in range(2 * RING, COUNT):
        z, y = d // 32, (d // RING) % 4
        relay = (z - (y < 2)) * 32 + (y + 1) % 4 * RING + d % RING
        over.append((d, relay))
        on.append((relay, d - 2 * RING))

    def whole(array):
        return [(array, 0, 0, B)]

    a = send(unit, around(1))
    b = send(unit, around(-1))
    relayed = send(low, over)
    c = send(unit, along(-RING))
    row_0, _ = stage("own", ((1,),), [whole(unit)], [whole(unit)], own_first=True)
    relayed, row_0, late = together((relayed, row_0, unit))
    d_low = send(relayed, on)
    sib = send(late, swap)
    a, b = together((a, b))

    a_top, b_low = halves(a, b)
    f_top = send(a_top, around(1))
    f_low = send(b_low, around(-1))
    c, d_low, sib = together((c, d_low, sib))
    a, b, top, a_top, c = together((a, b, top, a_top, c))
    d_top = send(top, along(-2 * RING))
    a_sib = send(a, swap)
    b_sib = send(b, swap)

    rights = [whole(unit), whole(c), [(d_low, 0, 0, H)]]
    lefts = [whole(unit), whole(sib), whole(a), whole(b)]
    row_1, col_1 = stage("near", ((0, 1, 1),) + ((1, 1, 1),) * 3, lefts, rights, [row_0], [])
    a_sib, b_sib, row_1 = together((a_sib, b_sib, row_1))
    row_2, col_2 = stage("mid", ((1, 1, 1),) * 2, [whole(a_sib), whole(b_sib)], rights, [], [col_1])
    f_top, f_low, d_top, row_2 = together((f_top, f_low, d_top, row_2))
    f_top_sib = send(f_top, swap)
    f_low_sib = send(f_low, swap)

    rights = rights + [[(d_top, 0, 0, H)]]
    lefts = lefts + [whole(a_sib), whole(b_sib), [(f_top, 0, 0, H), (f_low, 0, H, H)]]
    wanted = ((0, 0, 0, 1),) * 6 + ((1, 1, 1, 1),)
    row_3, col_3 = stage("far", wanted, lefts, rights, [row_1, row_2], [col_2])
    f_low_sib, f_top_sib, row_3 = together((f_low_sib, f_top_sib, row_3))
    lefts = [[(f_top_sib, 0, 0, H), (f_low_sib, 0, H, H)]]
    ring_part, next_part, after_part = stage("last", ((1, 1, 1, 1),), lefts, rights, [row_3], [col_3], last=True)

    next_got = send(next_part, along(RING))
    after_got = send(after_part, along(2 * RING))
    groups = [[r * RING + k for k in range(RING)] for r in range(COUNT // RING)]
    ring_got = lax.all_to_all(ring_part, "dp", 0, 0, axis_index_groups=groups, tiled=True)
    out = pl.pallas_call(
        last_kernel,
        out_shape=jax.ShapeDtypeStruct((1, B), jnp.float32),
        name="last_sum",
    )(ring_got, next_got, after_got)
    return out.reshape(B)


def solution(mesh):
    placed = (P("dp", None), P("dp", None), P("dp"))
    return jax.shard_map(body, mesh=mesh, in_specs=placed, out_specs=P("dp"), check_vma=False)
```
